32 devices in a mesh: seq: 8 (over z, x), tp: 4 (over y, core).
Axes of the slice: x: 2, y: 2, z: 4, core: 2. Of those that a mesh axis runs over, the one named last changes fastest.
Arguments:
- tokens: bfloat16 [4096, 2304], P(('seq', 'tp')), may hold values from -6 to 6
- cotangent: bfloat16 [4096, 2304], P(('seq', 'tp')), may hold values from -6 to 6
- query_weight: bfloat16 [2304, 2048], P('seq', 'tp'), may hold values from -128 to 127, as said below
- key_weight: bfloat16 [2304, 1024], P('seq', 'tp'), may hold values from -128 to 127, as said below
- value_weight: bfloat16 [2304, 1024], P('seq', 'tp'), may hold values from -128 to 127, as said below
- output_weight: bfloat16 [2048, 2304], P('tp', 'seq'), may hold values from -128 to 127, as said below
- gate_weight: bfloat16 [2304, 9216], P('seq', 'tp'), may hold values from -128 to 127, as said below
- up_weight: bfloat16 [2304, 9216], P('seq', 'tp'), may hold values from -128 to 127, as said below
- down_weight: bfloat16 [9216, 2304], P('tp', 'seq'), may hold values from -128 to 127, as said below
- query_scale: float32 [2048], replicated, may hold values from 0 to 1, as said below
- key_scale: float32 [1024], replicated, may hold values from 0 to 1, as said below
- value_scale: float32 [1024], replicated, may hold values from 0 to 1, as said below
- output_scale: float32 [2304], replicated, may hold values from 0 to 1, as said below
- gate_scale: float32 [9216], replicated, may hold values from 0 to 1, as said below
- up_scale: float32 [9216], replicated, may hold values from 0 to 1, as said below
- down_scale: float32 [2304], replicated, may hold values from 0 to 1, as said below
- pre_attention: float32 [2304], replicated, may hold values from 0.25 to 1.75
- post_attention: float32 [2304], replicated, may hold values from 0.25 to 1.75
- pre_feedforward: float32 [2304], replicated, may hold values from 0.25 to 1.75
- post_feedforward: float32 [2304], replicated, may hold values from 0.25 to 1.75
- positions: int32 [4096], P('seq'), may hold values from 0 to 3584, as said below
Outputs:
- block_out: float32 [4096, 2304], P(('seq', 'tp'))
- token_grad: float32 [4096, 2304], P(('seq', 'tp'))
- query_grad: float32 [2304, 2048], P('seq', 'tp')
- key_grad: float32 [2304, 1024], P('seq', 'tp')
- value_grad: float32 [2304, 1024], P('seq', 'tp')
- output_grad: float32 [2048, 2304], P('tp', 'seq')
- gate_grad: float32 [2304, 9216], P('seq', 'tp')
- up_grad: float32 [2304, 9216], P('seq', 'tp')
- down_grad: float32 [9216, 2304], P('tp', 'seq')
- query_scale_grad: float32 [2048], replicated
- key_scale_grad: float32 [1024], replicated
- value_scale_grad: float32 [1024], replicated
- output_scale_grad: float32 [2304], replicated
- gate_scale_grad: float32 [9216], replicated
- up_scale_grad: float32 [9216], replicated
- down_scale_grad: float32 [2304], replicated
- pre_attention_grad: float32 [2304], replicated
- post_attention_grad: float32 [2304], replicated
- pre_feedforward_grad: float32 [2304], replicated
- post_feedforward_grad: float32 [2304], replicated
The draws below stay inside these ranges and needn't reach their ends.
Inputs may be any that keep to these rules, and one draw needn't show every extreme that they name: `positions`: 0 at each document's first token and one more at each next token of it; one document runs from the first block of 512 tokens to the last and has exactly 3585 tokens. `query_weight`: whole numbers. `key_weight`: whole numbers. `value_weight`: whole numbers. `output_weight`: whole numbers. `gate_weight`: whole numbers. `up_weight`: whole numbers. `down_weight`: whole numbers. `query_scale`: positive. `key_scale`: positive. `value_scale`: positive. `output_scale`: positive. `gate_scale`: positive. `up_scale`: positive. `down_scale`: positive.
All inputs are finite; a program needn't handle non-finite values.
Results may differ from the reference program's by a relative error of at most 0.017.
Values may be sent and summed in bfloat16 or wider, within the bound.
No kernel may reach another device: no remote copies, remote signals or barrier semaphores. Data moves between devices by JAX's collectives and lax.ppermute only.
A program may use at most 256 MiB of HBM per device.

```python
import math
from functools import partial
import jax
import jax.numpy as jnp
from jax import lax

D = 2304
HEADS = 8
KV_HEADS = 4
HEAD_DIM = 256
FF = 9216
WINDOW = 4096
CAP = 50
TOK = 512
TOKENS = 4096


def uniform_codes(key, row_count, column_count):
    integer_codes = jax.random.randint(key, (row_count, column_count), -128, 128)
    return integer_codes.astype(jnp.float32).astype(jnp.bfloat16)


def channel_scales(key, count, fan_in):
    exponent = jax.random.uniform(key, (count,), jnp.float32, math.log(0.7), math.log(1.4))
    return jnp.exp(exponent) / (70.0 * math.sqrt(fan_in))


def draw_tokens(key, part):
    key = jax.random.fold_in(key, 2)
    noise = jnp.clip(jax.random.normal(key, (TOKENS, D), jnp.float32), -6.0, 6.0)
    return noise.astype(jnp.bfloat16)


def draw_query_weight(key, part):
    key = jax.random.fold_in(key, 41)
    return uniform_codes(key, D, HEADS * HEAD_DIM)


def draw_key_weight(key, part):
    key = jax.random.fold_in(key, 42)
    return uniform_codes(key, D, KV_HEADS * HEAD_DIM)


def draw_value_weight(key, part):
    key = jax.random.fold_in(key, 43)
    return uniform_codes(key, D, KV_HEADS * HEAD_DIM)


def draw_output_weight(key, part):
    key = jax.random.fold_in(key, 44)
    return uniform_codes(key, HEADS * HEAD_DIM, D)


def draw_gate_weight(key, part):
    key = jax.random.fold_in(key, 45)
    return uniform_codes(key, D, FF)


def draw_up_weight(key, part):
    key = jax.random.fold_in(key, 46)
    return uniform_codes(key, D, FF)


def draw_down_weight(key, part):
    key = jax.random.fold_in(key, 47)
    return uniform_codes(key, FF, D)


def draw_query_scale(key, part):
    key = jax.random.fold_in(key, 31)
    return channel_scales(key, HEADS * HEAD_DIM, D)


def draw_key_scale(key, part):
    key = jax.random.fold_in(key, 32)
    return channel_scales(key, KV_HEADS * HEAD_DIM, D)


def draw_value_scale(key, part):
    key = jax.random.fold_in(key, 33)
    return channel_scales(key, KV_HEADS * HEAD_DIM, D)


def draw_output_scale(key, part):
    key = jax.random.fold_in(key, 34)
    return channel_scales(key, D, HEADS * HEAD_DIM)


def draw_gate_scale(key, part):
    key = jax.random.fold_in(key, 35)
    return channel_scales(key, FF, D)


def draw_up_scale(key, part):
    key = jax.random.fold_in(key, 36)
    return channel_scales(key, FF, D)


def draw_down_scale(key, part):
    key = jax.random.fold_in(key, 37)
    return channel_scales(key, D, FF)


def draw_positions(key, part):
    key = jax.random.fold_in(key, 11)
    start_key, early_key, late_key = jax.random.split(key, 3)
    middle = jax.random.randint(start_key, (), 2, TOK - 1).astype(jnp.int32)
    early = jax.random.randint(early_key, (), 1, middle).astype(jnp.int32)
    after = (middle + TOKENS - TOK + 1).astype(jnp.int32)
    late = jax.random.randint(late_key, (), after, TOKENS).astype(jnp.int32)
    starts = jnp.stack([jnp.zeros((), jnp.int32), early, middle, after, late])
    index = jnp.arange(TOKENS, dtype=jnp.int32)
    begin = jnp.max(jnp.where(starts[:, None] <= index[None, :], starts[:, None], 0), axis=0)
    return index - begin


def level_of(rng, extent, shards, low, top_value):
    factor_of, own = 1.0, jax.random.fold_in(rng, 6)
    for axis_at, parts in shards:
        draws = jnp.exp(jax.random.uniform(jax.random.fold_in(own, axis_at), (parts,), jnp.float32, low / len(shards), top_value / len(shards)))
        factor_of = factor_of * jnp.repeat(draws, extent[axis_at] // parts).reshape([-1 if axis == axis_at else 1 for axis in range(len(extent))])
    return factor_of


def centred(stream_key, dims, spread, bound, pieces=(), kind=jnp.bfloat16):
    entries = jax.random.normal(stream_key, dims, jnp.float32) * spread
    if len(pieces) > 0:
        entries = level_of(stream_key, dims, pieces, -0.22, 0.18) * entries
    return jnp.clip(entries, min=-bound, max=bound).astype(kind)


def setup_inputs(seed: int = 0) -> dict:
    seeds = jax.random.split(jax.random.key(seed), 22)
    tokens = draw_tokens(jax.random.fold_in(seeds[21], 71), 0)
    cotangent = centred(seeds[1], (TOKENS, D), 1.0, 6.0, ((0, 32),))
    query_weight = draw_query_weight(jax.random.fold_in(seeds[21], 71), 0)
    key_weight = draw_key_weight(jax.random.fold_in(seeds[21], 71), 0)
    value_weight = draw_value_weight(jax.random.fold_in(seeds[21], 71), 0)
    output_weight = draw_output_weight(jax.random.fold_in(seeds[21], 71), 0)
    gate_weight = draw_gate_weight(jax.random.fold_in(seeds[21], 71), 0)
    up_weight = draw_up_weight(jax.random.fold_in(seeds[21], 71), 0)
    down_weight = draw_down_weight(jax.random.fold_in(seeds[21], 71), 0)
    query_scale = draw_query_scale(jax.random.fold_in(seeds[21], 71), 0)
    key_scale = draw_key_scale(jax.random.fold_in(seeds[21], 71), 0)
    value_scale = draw_value_scale(jax.random.fold_in(seeds[21], 71), 0)
    output_scale = draw_output_scale(jax.random.fold_in(seeds[21], 71), 0)
    gate_scale = draw_gate_scale(jax.random.fold_in(seeds[21], 71), 0)
    up_scale = draw_up_scale(jax.random.fold_in(seeds[21], 71), 0)
    down_scale = draw_down_scale(jax.random.fold_in(seeds[21], 71), 0)
    pre_attention = jnp.clip(1.0 + 0.15 * jax.random.normal(seeds[16], (D,), jnp.float32), 0.25, 1.75)
    post_attention = jnp.clip(1.0 + 0.15 * jax.random.normal(seeds[17], (D,), jnp.float32), 0.25, 1.75)
    pre_feedforward = jnp.clip(1.0 + 0.15 * jax.random.normal(seeds[18], (D,), jnp.float32), 0.25, 1.75)
    post_feedforward = jnp.clip(1.0 + 0.15 * jax.random.normal(seeds[19], (D,), jnp.float32), 0.25, 1.75)
    positions = draw_positions(jax.random.fold_in(seeds[21], 71), 0)
    return dict(tokens=tokens, cotangent=cotangent, query_weight=query_weight, key_weight=key_weight, value_weight=value_weight, output_weight=output_weight, gate_weight=gate_weight, up_weight=up_weight, down_weight=down_weight, query_scale=query_scale, key_scale=key_scale, value_scale=value_scale, output_scale=output_scale, gate_scale=gate_scale, up_scale=up_scale, down_scale=down_scale, pre_attention=pre_attention, post_attention=post_attention, pre_feedforward=pre_feedforward, post_feedforward=post_feedforward, positions=positions)


@jax.custom_vjp
def low(v):
    return lax.optimization_barrier(v.astype(jnp.bfloat16)).astype(jnp.float32)

@jax.custom_vjp
def low_back(v):
    return v

def low_keep(v):
    return (low(v), None)

def low_pass(kept, grad):
    return (grad,)

def back_keep(v):
    return (v, None)

def back_low(kept, grad):
    return (low(grad),)
low.defvjp(low_keep, low_pass)
low_back.defvjp(back_keep, back_low)
HIGH = lax.Precision.HIGHEST
EPSILON = 1e-06

def matmul(left, right):
    return jnp.dot(left, right, precision=HIGH, preferred_element_type=jnp.float32)

def nested_slice(codes):
    values = codes.astype(jnp.float32)
    return jnp.clip(jnp.floor((values + 8.0) / 16.0), -8.0, 7.0) * 16.0

def normed(values):
    return values * lax.rsqrt(lax.optimization_barrier(jnp.mean(values * values, axis=-1, keepdims=True)) + EPSILON)

def phases(positions):
    freqs = 10000.0 ** (-2.0 * jnp.arange(HEAD_DIM // 2, dtype=jnp.float32) / HEAD_DIM)
    angle = positions.astype(jnp.float32)[:, None] * freqs[None, :]
    return (jnp.cos(angle), jnp.sin(angle))

def rotate(values, cosine, sine):
    half = values.shape[-1] // 2
    first = values[..., :half]
    second = values[..., half:]
    cosine = cosine[:, None, :]
    sine = sine[:, None, :]
    return jnp.concatenate([first * cosine - second * sine, second * cosine + first * sine], -1)

def attention(queries, keys, values, positions):
    qblock = min(TOK, 512)
    count = TOKENS // qblock
    reach = (WINDOW - 1 + qblock - 1) // qblock * qblock
    group = HEADS // KV_HEADS
    scale = 1.0 / math.sqrt(HEAD_DIM)
    padded_keys = jnp.concatenate([jnp.zeros((reach, KV_HEADS, HEAD_DIM), jnp.float32), keys], 0)
    padded_values = jnp.concatenate([jnp.zeros((reach, KV_HEADS, HEAD_DIM), jnp.float32), values], 0)

    def one_block(index):
        begin = (index * qblock).astype(jnp.int32)
        block_q = lax.dynamic_slice_in_dim(queries, begin, qblock, 0)
        block_k = jnp.repeat(lax.dynamic_slice_in_dim(padded_keys, begin, reach + qblock, 0), group, axis=1)
        block_v = jnp.repeat(lax.dynamic_slice_in_dim(padded_values, begin, reach + qblock, 0), group, axis=1)
        places = lax.dynamic_slice_in_dim(positions, begin, qblock, 0)
        query_at = begin + jnp.arange(qblock, dtype=jnp.int32)
        key_at = begin - reach + jnp.arange(reach + qblock, dtype=jnp.int32)
        raw = low_back(jnp.einsum('qhd,khd->hqk', block_q, block_k, precision=HIGH) * scale)
        capped = CAP * jnp.tanh(raw / CAP)
        distance = query_at[:, None] - key_at[None, :]
        allowed = (distance >= 0) & (distance < WINDOW) & (key_at[None, :] >= (query_at - places)[:, None])
        masked = jnp.where(allowed[None], capped, -1e+30)
        top = lax.optimization_barrier(jnp.max(masked, axis=-1, keepdims=True))
        expo = jnp.exp(masked - top)
        probs = expo / lax.optimization_barrier(jnp.sum(expo, axis=-1, keepdims=True))
        return jnp.einsum('hqk,khd->qhd', low(probs), block_v, precision=HIGH)
    blocks = lax.map(jax.checkpoint(one_block), jnp.arange(count, dtype=jnp.int32))
    return blocks.reshape(TOKENS, HEADS * HEAD_DIM)

def forward(positions, inputs, wq, wk, wv, wo, wg, wu, wd, sq, sk, sv, so, sg, su, sd, gain_one, gain_two, gain_three, gain_four):
    h_one = low(normed(inputs) * gain_one)
    cosine, sine = phases(positions)
    zq = low_back(matmul(h_one, wq))
    zk = low_back(matmul(h_one, wk))
    zv = low_back(matmul(h_one, wv))
    queries = low(rotate((zq * sq).reshape(TOKENS, HEADS, HEAD_DIM), cosine, sine))
    keys = low(rotate((zk * sk).reshape(TOKENS, KV_HEADS, HEAD_DIM), cosine, sine))
    values = low((zv * sv).reshape(TOKENS, KV_HEADS, HEAD_DIM))
    attended = low(low_back(attention(queries, keys, values, positions)))
    zo = low_back(matmul(attended, wo))
    middle = inputs + normed(zo * so) * gain_two
    h_two = low(normed(middle) * gain_three)

    def feed(rows_in):
        zg = low_back(matmul(rows_in, wg))
        zu = low_back(matmul(rows_in, wu))
        hidden = low(jax.nn.gelu(zg * sg, approximate=True) * (zu * su))
        zd = low_back(matmul(hidden, wd))
        return zd * sd
    rows = min(TOKENS, 4096)
    fed = lax.map(jax.checkpoint(feed), h_two.reshape(TOKENS // rows, rows, D)).reshape(TOKENS, D)
    return middle + normed(fed) * gain_four

def reference(tokens, cotangent, query_weight, key_weight, value_weight, output_weight, gate_weight, up_weight, down_weight, query_scale, key_scale, value_scale, output_scale, gate_scale, up_scale, down_scale, pre_attention, post_attention, pre_feedforward, post_feedforward, positions):
    sliced = [nested_slice(item) for item in (query_weight, key_weight, value_weight, output_weight, gate_weight, up_weight, down_weight)]
    others = [item.astype(jnp.float32) for item in (query_scale, key_scale, value_scale, output_scale, gate_scale, up_scale, down_scale, pre_attention, post_attention, pre_feedforward, post_feedforward)]
    floats = [tokens.astype(jnp.float32)] + sliced + others
    result, pull = jax.vjp(partial(forward, positions), *floats)
    grads = pull(cotangent.astype(jnp.float32))
    return (result, grads[0], grads[1], grads[2], grads[3], grads[4], grads[5], grads[6], grads[7], grads[8], grads[9], grads[10], grads[11], grads[12], grads[13], grads[14], grads[15], grads[16], grads[17], grads[18])
```

```python
import math

import jax
import jax.numpy as jnp
from jax import lax
from jax.sharding import Mesh
from jax.sharding import PartitionSpec as P

HEAD_DIM = 256
WINDOW = 4096
CAP = 50
EPSILON = 1e-06

EVERY = ("line", "pair", "row", "core")
SWAP = [(0, 1), (1, 0)]


def swapped(block, axis):
    return lax.ppermute(block, axis, SWAP)


def hop(block, distance):
    count = lax.axis_size("line")
    route = [(i, i + distance) for i in range(count) if 0 <= i + distance < count]
    return lax.ppermute(block, "line", route)


def nested_slice(codes):
    values = codes.astype(jnp.float32)
    return (jnp.clip(jnp.floor((values + 8.0) / 16.0), -8.0, 7.0) * 16.0).astype(jnp.bfloat16)


def inverse_rms(values):
    return lax.rsqrt(jnp.mean(values * values, axis=-1, keepdims=True) + EPSILON)


def norm_back(source, inverse, gain, upstream):
    scaled = upstream * gain
    inner = jnp.mean(scaled * source, axis=-1, keepdims=True)
    back = inverse * scaled - source * (inverse * inverse * inverse) * inner
    return (back, jnp.sum(upstream * source * inverse, axis=0))


def phases(positions):
    freqs = 10000.0 ** (-2.0 * jnp.arange(HEAD_DIM // 2, dtype=jnp.float32) / HEAD_DIM)
    angle = positions.astype(jnp.float32)[:, None] * freqs[None, :]
    return (jnp.cos(angle), jnp.sin(angle))


def rotate(values, cosine, sine):
    half = values.shape[-1] // 2
    first = values[..., :half]
    second = values[..., half:]
    return jnp.concatenate([first * cosine - second * sine, second * cosine + first * sine], -1)


def spread(piece, total, offset):
    return lax.dynamic_update_slice_in_dim(jnp.zeros((total,), jnp.float32), piece, offset, 0)


def in_order(mine, other, place):
    return lax.dynamic_slice_in_dim(
        jnp.concatenate([other, mine, other], 0), (1 - place) * mine.shape[0], 2 * mine.shape[0], 0
    )


def half_of(block, place):
    size = block.shape[1] // 2
    return lax.dynamic_slice_in_dim(block, place * size, size, 1)


def gather8(block):
    cut = block.shape[1] // 2
    left, right = block[:, :cut], block[:, cut:]
    left_p, right_r = swapped(left, "pair"), swapped(right, "row")
    left_r, right_p = swapped(left, "row"), swapped(right, "pair")
    left_pr, right_pr = swapped(left_p, "row"), swapped(right_r, "pair")
    lefts = jnp.concatenate([left, left_r, left_p, left_pr], 0)
    rights = jnp.concatenate([right, right_r, right_p, right_pr], 0)
    four = jnp.concatenate([lefts, rights], 1)
    other = swapped(four, "core")
    size = block.shape[0]
    rows = []
    for j in range(4):
        rows += [four[j * size : (j + 1) * size], other[j * size : (j + 1) * size]]
    return jnp.concatenate(rows, 0)


def scatter8(terms):
    size = terms.shape[0] // 8
    parts = terms.reshape(4, 2, size, terms.shape[1])
    four = parts[:, 0] + swapped(parts[:, 1].astype(jnp.bfloat16), "core").astype(jnp.float32)
    four = four.reshape(2, 2, size, terms.shape[1])
    cut = terms.shape[1] // 2
    left, right = four[..., :cut], four[..., cut:]
    left = left[0] + swapped(left[1].astype(jnp.bfloat16), "pair").astype(jnp.float32)
    right = right[:, 0] + swapped(right[:, 1].astype(jnp.bfloat16), "row").astype(jnp.float32)
    left = left[0] + swapped(left[1].astype(jnp.bfloat16), "row").astype(jnp.float32)
    right = right[0] + swapped(right[1].astype(jnp.bfloat16), "pair").astype(jnp.float32)
    return jnp.concatenate([left, right], 1)


def reordered(rows, me):
    size = rows.shape[0] // 8
    return jnp.concatenate(
        [lax.dynamic_slice_in_dim(rows, (j ^ me) * size, size, 0) for j in range(8)], 0
    )


def total(vector):
    for axis in ("core", "row", "pair"):
        vector = vector + swapped(vector, axis)
    count = lax.axis_size("line")
    step = 1
    while step < count:
        vector = vector + lax.ppermute(vector, "line", [(i, i ^ step) for i in range(count)])
        step *= 2
    return vector


def body(
    tokens,
    cotangent,
    query_weight,
    key_weight,
    value_weight,
    output_weight,
    gate_weight,
    up_weight,
    down_weight,
    query_scale,
    key_scale,
    value_scale,
    output_scale,
    gate_scale,
    up_scale,
    down_scale,
    pre_attention,
    post_attention,
    pre_feedforward,
    post_feedforward,
    positions,
):
    line = lax.axis_index("line")
    pair = lax.axis_index("pair")
    tp_index = lax.axis_index("row") * 2 + lax.axis_index("core")
    me = pair * 4 + tp_index
    lines = lax.axis_size("line")
    scale = 1.0 / math.sqrt(HEAD_DIM)
    even = pair == 0
    qcols = query_weight.shape[1] // 2
    kcols = key_weight.shape[1]
    ocols = output_weight.shape[0] // 2
    fcols = gate_weight.shape[1] // 2
    rows = 8 * tokens.shape[0]

    wq, wk, wv, wo, wg, wu, wd = (
        nested_slice(query_weight),
        nested_slice(key_weight),
        nested_slice(value_weight),
        nested_slice(output_weight.T),
        nested_slice(gate_weight),
        nested_slice(up_weight),
        nested_slice(down_weight.T),
    )

    def whole(keep, give):
        block = in_order(keep, swapped(give, "pair"), pair)
        return lax.all_gather(block, "line", axis=0, tiled=True)

    w_qkv = whole(
        jnp.concatenate([half_of(wq, pair), jnp.where(even, wk, wv)], 1),
        jnp.concatenate([half_of(wq, 1 - pair), jnp.where(even, wv, wk)], 1),
    )
    w_o = whole(half_of(wo, pair), half_of(wo, 1 - pair))
    w_gu = whole(
        jnp.concatenate([half_of(wg, pair), half_of(wu, pair)], 1),
        jnp.concatenate([half_of(wg, 1 - pair), half_of(wu, 1 - pair)], 1),
    )
    w_d = whole(half_of(wd, pair), half_of(wd, 1 - pair))

    q_at = tp_index * 2 * qcols + pair * qcols
    k_at = tp_index * kcols
    f_at = tp_index * 2 * fcols + pair * fcols
    q_scale = lax.dynamic_slice_in_dim(query_scale, q_at, qcols, 0)
    k_scale = lax.dynamic_slice_in_dim(key_scale, k_at, kcols, 0)
    v_scale = lax.dynamic_slice_in_dim(value_scale, k_at, kcols, 0)
    kv_scale = jnp.where(even, k_scale, v_scale)
    g_scale = lax.dynamic_slice_in_dim(gate_scale, f_at, fcols, 0)
    u_scale = lax.dynamic_slice_in_dim(up_scale, f_at, fcols, 0)

    inputs = tokens.astype(jnp.float32)
    inverse_one = inverse_rms(inputs)
    h_one = gather8((inputs * inverse_one * pre_attention).astype(jnp.bfloat16))
    places = in_order(positions, swapped(positions, "pair"), pair)
    cosine, sine = phases(places)

    z_qkv = reordered(jnp.dot(h_one, w_qkv, preferred_element_type=jnp.float32), me)
    zq, zkv = z_qkv[:, :qcols], z_qkv[:, qcols:]
    queries = rotate(zq * q_scale, cosine, sine).astype(jnp.bfloat16)
    kv_rows = zkv * kv_scale
    kv_rows = jnp.where(even, rotate(kv_rows, cosine, sine), kv_rows).astype(jnp.bfloat16)

    depth = min((WINDOW - 1 + rows - 1) // rows, lines - 1)
    kept = [kv_rows]
    for step in range(depth):
        kept.append(hop(kept[-1], 1))
    other = [swapped(block, "pair") for block in kept]
    kept, other = jnp.concatenate(kept[::-1], 0), jnp.concatenate(other[::-1], 0)
    keys = jnp.where(even, kept, other)
    values = jnp.where(even, other, kept)
    span = (depth + 1) * rows
    query_at = line * rows + jnp.arange(rows, dtype=jnp.int32)
    key_at = (line - depth) * rows + jnp.arange(span, dtype=jnp.int32)
    distance = query_at[:, None] - key_at[None, :]
    allowed = (
        (distance >= 0)
        & (distance < WINDOW)
        & (key_at[None, :] >= (query_at - places)[:, None])
    )

    def scored():
        raw = jnp.einsum("qd,kd->qk", queries, keys, preferred_element_type=jnp.float32) * scale
        return CAP * jnp.tanh(raw / CAP)

    masked = jnp.where(allowed, scored(), -1e30)
    top = jnp.max(masked, axis=-1, keepdims=True)
    expo = jnp.exp(masked - top)
    expo_sum = jnp.sum(expo, axis=-1, keepdims=True)
    probs = (expo / expo_sum).astype(jnp.bfloat16)
    lse = top + jnp.log(expo_sum)
    attended = jnp.dot(probs, values, preferred_element_type=jnp.float32).astype(jnp.bfloat16)
    attended = reordered(attended, me)

    zo = scatter8(jnp.einsum("tc,dc->td", attended, w_o, preferred_element_type=jnp.float32))
    after_attention = zo * output_scale
    inverse_two = inverse_rms(after_attention)
    middle = inputs + after_attention * inverse_two * post_attention
    inverse_three = inverse_rms(middle)
    h_two = gather8((middle * inverse_three * pre_feedforward).astype(jnp.bfloat16))
    z_gu = jnp.dot(h_two, w_gu, preferred_element_type=jnp.float32)
    zg, zu = z_gu[:, :fcols], z_gu[:, fcols:]
    gate_in = zg * g_scale
    up_in = zu * u_scale
    hidden = (jax.nn.gelu(gate_in, approximate=True) * up_in).astype(jnp.bfloat16)
    zd = scatter8(jnp.einsum("tf,df->td", hidden, w_d, preferred_element_type=jnp.float32))
    fed = zd * down_scale
    inverse_four = inverse_rms(fed)
    block_out = middle + fed * inverse_four * post_feedforward

    upstream = cotangent.astype(jnp.float32)
    dfed, gain_four_grad = norm_back(fed, inverse_four, post_feedforward, upstream)
    down_scale_sum = jnp.sum(dfed * zd, axis=0)
    dzd = gather8((dfed * down_scale).astype(jnp.bfloat16))

    def shared(term):
        part = lax.psum_scatter(term.astype(jnp.bfloat16), "line", scatter_dimension=0, tiled=True)
        size = part.shape[0] // 2
        keep = lax.dynamic_slice_in_dim(part, pair * size, size, 0)
        give = lax.dynamic_slice_in_dim(part, (1 - pair) * size, size, 0)
        return (keep.astype(jnp.float32), swapped(give, "pair").astype(jnp.float32))

    def side_by_side(keep, got):
        return jnp.where(
            even, jnp.concatenate([keep, got], 1), jnp.concatenate([got, keep], 1)
        )

    d_keep, d_got = shared(
        jnp.einsum("td,tf->df", dzd, hidden, preferred_element_type=jnp.float32)
    )
    down_grad = side_by_side(d_keep, d_got).T
    dhidden = jnp.dot(dzd, w_d, preferred_element_type=jnp.float32)
    unused, pull = jax.vjp(
        lambda left, right: jax.nn.gelu(left, approximate=True) * right, gate_in, up_in
    )
    dgate, dup = pull(dhidden)
    gate_scale_sum = jnp.sum(dgate * zg, axis=0)
    up_scale_sum = jnp.sum(dup * zu, axis=0)
    dz_gu = jnp.concatenate([dgate * g_scale, dup * u_scale], 1).astype(jnp.bfloat16)
    gu_keep, gu_got = shared(
        jnp.einsum("td,tf->df", h_two, dz_gu, preferred_element_type=jnp.float32)
    )
    gate_grad = side_by_side(gu_keep[:, :fcols], gu_got[:, :fcols])
    up_grad = side_by_side(gu_keep[:, fcols:], gu_got[:, fcols:])
    dh_mid = scatter8(jnp.einsum("tf,df->td", dz_gu, w_gu, preferred_element_type=jnp.float32))
    dmid_norm, gain_three_grad = norm_back(middle, inverse_three, pre_feedforward, dh_mid)
    dmiddle = upstream + dmid_norm
    dafter, gain_two_grad = norm_back(after_attention, inverse_two, post_attention, dmiddle)
    output_scale_sum = jnp.sum(dafter * zo, axis=0)
    dzo = gather8((dafter * output_scale).astype(jnp.bfloat16))
    o_keep, o_got = shared(
        jnp.einsum("td,tc->dc", dzo, attended, preferred_element_type=jnp.float32)
    )
    output_grad = side_by_side(o_keep, o_got).T
    dattended = reordered(
        jnp.dot(dzo, w_o, preferred_element_type=jnp.float32).astype(jnp.bfloat16), me
    )

    capped = scored()
    probs = jnp.where(allowed, jnp.exp(capped - lse), 0.0)
    dvalues = jnp.einsum(
        "qk,qd->kd", probs.astype(jnp.bfloat16), dattended, preferred_element_type=jnp.float32
    )
    dprobs = jnp.einsum("qd,kd->qk", dattended, values, preferred_element_type=jnp.float32)
    dcapped = probs * (dprobs - jnp.sum(probs * dprobs, axis=-1, keepdims=True))
    ratio = capped / CAP
    draw = (dcapped * (1.0 - ratio * ratio)).astype(jnp.bfloat16)
    dqueries = jnp.dot(draw, keys, preferred_element_type=jnp.float32) * scale
    dkeys = jnp.einsum("qk,qd->kd", draw, queries, preferred_element_type=jnp.float32) * scale

    keep = jnp.where(even, dkeys, dvalues)
    give = jnp.where(even, dvalues, dkeys).astype(jnp.bfloat16)
    both = [
        keep[i * rows : (i + 1) * rows]
        + swapped(give[i * rows : (i + 1) * rows], "pair").astype(jnp.float32)
        for i in range(depth + 1)
    ]
    dkv = both[0]
    for block in both[1:]:
        dkv = block + hop(dkv.astype(jnp.bfloat16), -1).astype(jnp.float32)
    equery = rotate(dqueries, cosine, -sine)
    ekv = jnp.where(even, rotate(dkv, cosine, -sine), dkv)
    query_scale_sum = jnp.sum(equery * zq, axis=0)
    kv_scale_sum = jnp.sum(ekv * zkv, axis=0)
    dz_qkv = reordered(
        jnp.concatenate([equery * q_scale, ekv * kv_scale], 1).astype(jnp.bfloat16), me
    )
    qkv_keep, qkv_got = shared(
        jnp.einsum("td,tc->dc", h_one, dz_qkv, preferred_element_type=jnp.float32)
    )
    query_grad = side_by_side(qkv_keep[:, :qcols], qkv_got[:, :qcols])
    key_grad = jnp.where(even, qkv_keep[:, qcols:], qkv_got[:, qcols:])
    value_grad = jnp.where(even, qkv_got[:, qcols:], qkv_keep[:, qcols:])
    dh_local = scatter8(jnp.einsum("tc,dc->td", dz_qkv, w_qkv, preferred_element_type=jnp.float32))
    dinput_norm, gain_one_grad = norm_back(inputs, inverse_one, pre_attention, dh_local)
    token_grad = dmiddle + dinput_norm

    early = (
        output_scale_sum,
        spread(gate_scale_sum, gate_scale.shape[0], f_at),
        spread(up_scale_sum, up_scale.shape[0], f_at),
        down_scale_sum,
        gain_two_grad,
        gain_three_grad,
        gain_four_grad,
    )
    late = (
        spread(query_scale_sum, query_scale.shape[0], q_at),
        spread(jnp.where(even, kv_scale_sum, 0.0), key_scale.shape[0], k_at),
        spread(jnp.where(even, 0.0, kv_scale_sum), value_scale.shape[0], k_at),
        gain_one_grad,
    )

    def summed(vectors):
        flat = total(jnp.concatenate(vectors))
        cuts, at = [], 0
        for vector in vectors:
            cuts.append(flat[at : at + vector.shape[0]])
            at += vector.shape[0]
        return cuts

    o_sum, g_sum, u_sum, d_sum, two_sum, three_sum, four_sum = summed(early)
    q_sum, k_sum, v_sum, one_sum = summed(late)
    return (
        block_out,
        token_grad,
        query_grad,
        key_grad,
        value_grad,
        output_grad,
        gate_grad,
        up_grad,
        down_grad,
        q_sum,
        k_sum,
        v_sum,
        o_sum,
        g_sum,
        u_sum,
        d_sum,
        one_sum,
        two_sum,
        three_sum,
        four_sum,
    )


def solution(mesh):
    seq_count, tp_count = mesh.shape["seq"], mesh.shape["tp"]
    wide = Mesh(mesh.devices.reshape(seq_count // 2, 2, tp_count // 2, 2), EVERY)
    seq, tp = ("line", "pair"), ("row", "core")
    return jax.shard_map(
        body,
        mesh=wide,
        in_specs=(P(EVERY, None),) * 2
        + (P(seq, tp),) * 3
        + (P(tp, seq),)
        + (P(seq, tp),) * 2
        + (P(tp, seq),)
        + (P(),) * 11
        + (P(seq),),
        out_specs=(P(EVERY, None),) * 2
        + (P(seq, tp),) * 3
        + (P(tp, seq),)
        + (P(seq, tp),) * 2
        + (P(tp, seq),)
        + (P(),) * 11,
        check_vma=False,
    )
```

```python
import math

import jax
import jax.numpy as jnp
from jax import lax
from jax.experimental import pallas as pl
from jax.experimental.pallas import tpu as pltpu
from jax.sharding import Mesh
from jax.sharding import PartitionSpec as P

HEAD_DIM = 256
WINDOW = 4096
CAP = 50
EPSILON = 1e-06

LINE = ("far", "near")
EVERY = ("far", "near", "pair", "row", "core")
SWAP = [(0, 1), (1, 0)]
FAR_PIECES = ("_own_far", "_met_far", "_own_far_pair", "_met_far_pair")


def swapped(block, axis):
    return lax.ppermute(block, axis, SWAP)


def hop(block, distance):
    count = lax.axis_size(LINE)
    route = [(i, i + distance) for i in range(count) if 0 <= i + distance < count]
    return lax.ppermute(block, LINE, route)


def turned(block, distance):
    count = lax.axis_size("far")
    return lax.ppermute(block, "far", [(i, (i + distance) % count) for i in range(count)])


def put_together(sources, moves, shape):
    count = len(moves())
    if any(size % 32 for _, _, size, _, _ in moves()):
        out = jnp.zeros(shape, sources[0].dtype)
        for source, start, size, row, column in moves():
            piece = lax.dynamic_slice_in_dim(sources[source], start, size, 0)
            out = lax.dynamic_update_slice(out, piece, (row, column))
        return out

    def rows_at(row, size):
        return pl.ds(row if isinstance(row, int) else pl.multiple_of(row, 32), size)

    def kernel(*refs):
        out, sems = refs[len(sources)], refs[len(sources) + 1]
        copies = []
        for i, (source, start, size, row, column) in enumerate(moves()):
            piece = refs[source].at[rows_at(start, size)]
            target = out.at[rows_at(row, size), pl.ds(column, sources[source].shape[1])]
            copies.append(pltpu.make_async_copy(piece, target, sems.at[i]))
        for copy in copies:
            copy.start()
        for copy in copies:
            copy.wait()

    size = 2 * math.prod(shape) * sources[0].dtype.itemsize
    return pl.pallas_call(
        kernel,
        out_shape=jax.ShapeDtypeStruct(shape, sources[0].dtype),
        in_specs=[pl.BlockSpec(memory_space=pl.ANY)] * len(sources),
        out_specs=pl.BlockSpec(memory_space=pltpu.VMEM),
        scratch_shapes=[pltpu.SemaphoreType.DMA((count,))],
        compiler_params=pltpu.CompilerParams(vmem_limit_bytes=size // 2 + 4 * 1024 * 1024),
        cost_estimate=pl.CostEstimate(flops=0, bytes_accessed=size, transcendentals=0),
    )(*sources)


def tie(*values):
    return lax.optimization_barrier(values)


class Stream:
    def __init__(self, **blocks):
        self.blocks = blocks

    def stop(self, work, finish=(), start=()):
        here = [self.blocks[name] for name in finish]
        sources = [[self.blocks[name] for name in names] for _, names, _ in start]
        work, here, sources = tie(work, here, sources)
        self.blocks.update(zip(finish, here))
        for (name, _, route), blocks in zip(start, sources):
            self.blocks[name] = route(*blocks)
        return work


def nested_slice(codes):
    values = codes.astype(jnp.float32)
    return (jnp.clip(jnp.floor((values + 8.0) / 16.0), -8.0, 7.0) * 16.0).astype(jnp.bfloat16)


def inverse_rms(values):
    return lax.rsqrt(jnp.mean(values * values, axis=-1, keepdims=True) + EPSILON)


def norm_back(source, inverse, gain, upstream):
    scaled = upstream * gain
    inner = jnp.mean(scaled * source, axis=-1, keepdims=True)
    back = inverse * scaled - source * (inverse * inverse * inverse) * inner
    return (back, jnp.sum(upstream * source * inverse, axis=0))


def phases(positions):
    freqs = 10000.0 ** (-2.0 * jnp.arange(HEAD_DIM // 2, dtype=jnp.float32) / HEAD_DIM)
    angle = positions.astype(jnp.float32)[:, None] * freqs[None, :]
    return (jnp.cos(angle), jnp.sin(angle))


def rotate(values, cosine, sine):
    half = values.shape[-1] // 2
    first = values[..., :half]
    second = values[..., half:]
    return jnp.concatenate([first * cosine - second * sine, second * cosine + first * sine], -1)


def spread(piece, total, offset):
    return lax.dynamic_update_slice_in_dim(jnp.zeros((total,), jnp.float32), piece, offset, 0)


def in_order(mine, other, place):
    return lax.dynamic_slice_in_dim(
        jnp.concatenate([other, mine, other], 0), (1 - place) * mine.shape[0], 2 * mine.shape[0], 0
    )


def half_of(block, place):
    size = block.shape[1] // 2
    return lax.dynamic_slice_in_dim(block, place * size, size, 1)


def unstopped(work):
    return work


def gather8(block, first, stop=unstopped):
    size, width = block.shape
    cut = size // 2
    left, right = block[:cut], block[cut:]
    left_p, right_r = swapped(left, first), swapped(right, "row")
    left_r, right_p = swapped(left, "row"), swapped(right, first)
    left_pr, right_pr = swapped(left_p, "row"), swapped(right_r, first)
    halves = [left, right, left_r, right_r, left_p, right_p, left_pr, right_pr]
    four = put_together(
        halves, lambda: [(i, 0, cut, i * cut, 0) for i in range(8)], (4 * size, width)
    )
    four = stop(four)
    return put_together(
        [four, swapped(four, "core")],
        lambda: [(i, 0, 4 * size, i * 4 * size, 0) for i in range(2)],
        (8 * size, width),
    )


def scatter8(terms, first, stop_one=unstopped, stop_two=unstopped):
    size = terms.shape[0] // 8
    four = terms[: 4 * size] + swapped(
        terms[4 * size :].astype(jnp.bfloat16), "core"
    ).astype(jnp.float32)
    four = stop_one(four)
    four = four.reshape(2, 2, size, terms.shape[1])
    cut = terms.shape[1] // 2
    left, right = four[..., :cut], four[..., cut:]
    left = left[0] + swapped(left[1].astype(jnp.bfloat16), first).astype(jnp.float32)
    right = right[:, 0] + swapped(right[:, 1].astype(jnp.bfloat16), "row").astype(jnp.float32)
    left, right = stop_two((left, right))
    left = left[0] + swapped(left[1].astype(jnp.bfloat16), "row").astype(jnp.float32)
    right = right[0] + swapped(right[1].astype(jnp.bfloat16), first).astype(jnp.float32)
    return jnp.concatenate([left, right], 1)


def blocks(rows, places):
    size = rows.shape[0] // len(places)
    return jnp.concatenate(
        [lax.dynamic_slice_in_dim(rows, place * size, size, 0) for place in places], 0
    )


def to_tokens(rows, pair, row, core):
    places = [
        ((c ^ core) * 4 + (p ^ pair) * 2 + (r ^ row))
        for p in range(2)
        for r in range(2)
        for c in range(2)
    ]
    return blocks(rows, places)


def from_tokens(rows, pair, row, core):
    places = [
        ((p ^ pair) * 4 + (r ^ row) * 2 + (c ^ core))
        for c in range(2)
        for p in range(2)
        for r in range(2)
    ]
    return blocks(rows, places)


def total(vector):
    for axis in ("core", "row", "pair"):
        vector = vector + swapped(vector, axis)
    count = lax.axis_size(LINE)
    step = 1
    while step < count:
        vector = vector + lax.ppermute(vector, LINE, [(i, i ^ step) for i in range(count)])
        step *= 2
    return vector


def across(left, right):
    return lax.dot_general(left, right, (((1,), (1,)), ((), ())), preferred_element_type=jnp.float32)

def attend(queries, keys, values, low, bq=512, bk=1024):
    rows, span = queries.shape[0], keys.shape[0]
    offset = span - rows
    first = jnp.min(low.reshape(rows // bq, bq), axis=1) // bk

    def kernel(first_ref, q_ref, k_ref, v_ref, low_ref, o_ref, lse_ref, sums, totals):
        block = pl.program_id(0)
        high = offset + block * bq + lax.broadcasted_iota(jnp.int32, (bq, 1), 0)
        sums[...] = jnp.zeros_like(sums)
        totals[...] = jnp.zeros_like(totals)

        def chunk(c, carry):
            at = pl.multiple_of(c * bk, bk)
            raw = across(q_ref[...], k_ref[pl.ds(at, bk), :])
            place = at + lax.broadcasted_iota(jnp.int32, (bq, bk), 1)
            seen = (place >= low_ref[...]) & (place <= high)
            expo = jnp.where(seen, jnp.exp(CAP * jnp.tanh(raw * (1.0 / CAP))), 0.0)
            totals[...] += jnp.sum(expo, axis=-1, keepdims=True)
            sums[...] += jnp.dot(expo.astype(jnp.bfloat16), v_ref[pl.ds(at, bk), :], preferred_element_type=jnp.float32)
            return carry

        lax.fori_loop(first_ref[block], (offset + (block + 1) * bq - 1) // bk + 1, chunk, 0)
        o_ref[...] = sums[...] / totals[...]
        lse_ref[...] = jnp.log(totals[...])

    whole = lambda i, *_: (0, 0)
    mine = lambda i, *_: (i, 0)
    return pl.pallas_call(
        kernel,
        out_shape=(jax.ShapeDtypeStruct((rows, HEAD_DIM), jnp.float32), jax.ShapeDtypeStruct((rows, 1), jnp.float32)),
        grid_spec=pltpu.PrefetchScalarGridSpec(
            num_scalar_prefetch=1, grid=(rows // bq,),
            in_specs=[pl.BlockSpec((bq, HEAD_DIM), mine), pl.BlockSpec((span, HEAD_DIM), whole), pl.BlockSpec((span, HEAD_DIM), whole), pl.BlockSpec((bq, 1), mine)],
            out_specs=(pl.BlockSpec((bq, HEAD_DIM), mine), pl.BlockSpec((bq, 1), mine)),
            scratch_shapes=[pltpu.VMEM((bq, HEAD_DIM), jnp.float32), pltpu.VMEM((bq, 1), jnp.float32)]),
        compiler_params=pltpu.CompilerParams(vmem_limit_bytes=40 * 1024 * 1024),
        cost_estimate=pl.CostEstimate(flops=4 * rows * span * HEAD_DIM, bytes_accessed=4 * span * HEAD_DIM, transcendentals=2 * rows * span),
    )(first, queries, keys, values, low)

def attend_back(queries, keys, values, low, lse, delta, upstream, bq=1024, bk=512):
    rows, span = queries.shape[0], keys.shape[0]
    offset = span - rows
    first = jnp.min(low.reshape(rows // bq, bq), axis=1) // bk

    def kernel(first_ref, q_ref, up_ref, k_ref, kt_ref, v_ref, low_ref, lse_ref, delta_ref, dq_ref, dk_ref, dv_ref):
        block = pl.program_id(0)
        high = offset + block * bq + lax.broadcasted_iota(jnp.int32, (1, bq), 1)

        @pl.when(block == 0)
        def clear():
            dk_ref[...] = jnp.zeros_like(dk_ref)
            dv_ref[...] = jnp.zeros_like(dv_ref)

        dq_ref[...] = jnp.zeros_like(dq_ref)

        def chunk(c, carry):
            at = pl.multiple_of(c * bk, bk)
            here = pl.ds(at, bk)
            ratio = jnp.tanh(across(k_ref[here, :], q_ref[...]) * (1.0 / CAP))
            place = at + lax.broadcasted_iota(jnp.int32, (bk, bq), 0)
            seen = (place >= low_ref[...]) & (place <= high)
            probs = jnp.where(seen, jnp.exp(CAP * ratio - lse_ref[...]), 0.0)
            dv_ref[here, :] += jnp.dot(probs.astype(jnp.bfloat16), up_ref[...], preferred_element_type=jnp.float32)
            dprobs = across(v_ref[here, :], up_ref[...])
            draw = (probs * (dprobs - delta_ref[...]) * (1.0 - ratio * ratio)).astype(jnp.bfloat16)
            dk_ref[here, :] += jnp.dot(draw, q_ref[...], preferred_element_type=jnp.float32)
            dq_ref[...] += jnp.dot(kt_ref[:, here], draw, preferred_element_type=jnp.float32)
            return carry

        lax.fori_loop(first_ref[block], (offset + (block + 1) * bq - 1) // bk + 1, chunk, 0)

    whole = lambda i, *_: (0, 0)
    mine = lambda i, *_: (i, 0)
    across_lanes = lambda i, *_: (0, i)
    return pl.pallas_call(
        kernel,
        out_shape=(jax.ShapeDtypeStruct((HEAD_DIM, rows), jnp.float32), jax.ShapeDtypeStruct((span, HEAD_DIM), jnp.float32), jax.ShapeDtypeStruct((span, HEAD_DIM), jnp.float32)),
        grid_spec=pltpu.PrefetchScalarGridSpec(
            num_scalar_prefetch=1, grid=(rows // bq,),
            in_specs=[pl.BlockSpec((bq, HEAD_DIM), mine), pl.BlockSpec((bq, HEAD_DIM), mine), pl.BlockSpec((span, HEAD_DIM), whole), pl.BlockSpec((HEAD_DIM, span), whole), pl.BlockSpec((span, HEAD_DIM), whole),
                      pl.BlockSpec((1, bq), across_lanes), pl.BlockSpec((1, bq), across_lanes), pl.BlockSpec((1, bq), across_lanes)],
            out_specs=(pl.BlockSpec((HEAD_DIM, bq), across_lanes), pl.BlockSpec((span, HEAD_DIM), whole), pl.BlockSpec((span, HEAD_DIM), whole))),
        compiler_params=pltpu.CompilerParams(vmem_limit_bytes=48 * 1024 * 1024),
        cost_estimate=pl.CostEstimate(flops=10 * rows * span * HEAD_DIM, bytes_accessed=12 * span * HEAD_DIM, transcendentals=2 * rows * span),
    )(first, queries, upstream, keys, keys.T, values, low.T, lse.T, delta.T)


def body(
    tokens,
    cotangent,
    query_weight,
    key_weight,
    value_weight,
    output_weight,
    gate_weight,
    up_weight,
    down_weight,
    query_scale,
    key_scale,
    value_scale,
    output_scale,
    gate_scale,
    up_scale,
    down_scale,
    pre_attention,
    post_attention,
    pre_feedforward,
    post_feedforward,
    positions,
):
    fars, lines = lax.axis_size("far"), lax.axis_size(LINE)
    far, near, pair = lax.axis_index("far"), lax.axis_index("near"), lax.axis_index("pair")
    row, core = lax.axis_index("row"), lax.axis_index("core")
    line, tp_index = far * 2 + near, row * 2 + core
    scale = 1.0 / math.sqrt(HEAD_DIM)
    even = pair == 0
    qcols = query_weight.shape[1] // 2
    kcols = key_weight.shape[1]
    ocols = output_weight.shape[0] // 2
    fcols = gate_weight.shape[1] // 2
    rows = 8 * tokens.shape[0]

    wq, wk, wv, wo, wg, wu, wd = (
        nested_slice(query_weight),
        nested_slice(key_weight),
        nested_slice(value_weight),
        nested_slice(output_weight.T),
        nested_slice(gate_weight),
        nested_slice(up_weight),
        nested_slice(down_weight.T),
    )

    def paired(keep, give):
        return in_order(keep, swapped(give, "pair"), pair)

    def over_line(block):
        return lax.all_gather(block, LINE, axis=0, tiled=True)

    def to_far(piece):
        return [turned(piece, distance) for distance in range(1, fars)]

    def to_pair(pieces):
        return jax.tree.map(lambda piece: swapped(piece, "pair"), pieces)

    def to_near(piece):
        return swapped(piece, "near")

    def far_of(name):
        return (name + "_far", [name], to_far)

    def pair_of(name):
        return (name + "_pair", [name], to_pair)

    def near_of(name):
        return (name + "_met", [name + "_give"], to_near)

    kv_block = paired(jnp.where(even, wk, wv), jnp.where(even, wv, wk))
    q_block = paired(half_of(wq, pair), half_of(wq, 1 - pair))
    o_block = paired(half_of(wo, pair), half_of(wo, 1 - pair))
    stream = Stream(q=q_block, o=o_block)
    for name, shard in (("g", wg), ("u", wu), ("d", wd)):
        stream.blocks[name + "_own"] = half_of(shard, near)
        stream.blocks[name + "_give"] = half_of(shard, 1 - near)

    def piece_rows(size):
        far, near, pair = lax.axis_index("far"), lax.axis_index("near"), lax.axis_index("pair")
        rows = []
        for distance in range(fars):
            source = lax.rem(far - distance + fars, fars)
            for p in (pair, 1 - pair):
                rows += [((source * 2 + n) * 2 + p) * size for n in (near, 1 - near)]
        return rows

    def assembled(name):
        own, met = stream.blocks[name + "_own"], stream.blocks[name + "_met"]
        pieces = [own, met, stream.blocks[name + "_own_pair"], stream.blocks[name + "_met_pair"]]
        for quarter in zip(*(stream.blocks[name + end] for end in FAR_PIECES)):
            pieces += quarter
        size, width = own.shape
        return put_together(
            pieces,
            lambda: [(i, 0, size, place, 0) for i, place in enumerate(piece_rows(size))],
            (len(pieces) * size, width),
        )

    q_at = tp_index * 2 * qcols + pair * qcols
    k_at = tp_index * kcols
    f_at = tp_index * 2 * fcols + near * fcols
    q_scale = lax.dynamic_slice_in_dim(query_scale, q_at, qcols, 0)
    k_scale = lax.dynamic_slice_in_dim(key_scale, k_at, kcols, 0)
    v_scale = lax.dynamic_slice_in_dim(value_scale, k_at, kcols, 0)
    kv_scale = jnp.where(even, k_scale, v_scale)
    g_scale = lax.dynamic_slice_in_dim(gate_scale, f_at, fcols, 0)
    u_scale = lax.dynamic_slice_in_dim(up_scale, f_at, fcols, 0)

    inputs = tokens.astype(jnp.float32)
    inverse_one = inverse_rms(inputs)
    h_local = (inputs * inverse_one * pre_attention).astype(jnp.bfloat16)
    stream.blocks["kv"] = kv_block
    h_local = stream.stop(
        h_local, start=[("w_kv", ["kv"], over_line), near_of("g"), pair_of("g_own")]
    )
    h_one = gather8(
        h_local,
        "pair",
        lambda four: stream.stop(
            four,
            finish=["w_kv", "g_met", "g_own_pair"],
            start=[far_of("g_own"), near_of("u"), pair_of("u_own")],
        ),
    )
    w_kv = stream.blocks["w_kv"]
    places = in_order(positions, swapped(positions, "pair"), pair)
    cosine, sine = phases(places)

    zkv = jnp.dot(h_one, w_kv, preferred_element_type=jnp.float32)
    zkv = to_tokens(zkv, pair, row, core)
    kv_rows = zkv * kv_scale
    kv_rows = jnp.where(even, rotate(kv_rows, cosine, sine), kv_rows).astype(jnp.bfloat16)

    kv_rows = stream.stop(
        kv_rows,
        finish=["g_own_far", "u_met", "u_own_pair"],
        start=[("w_q", ["q"], over_line), near_of("d"), pair_of("d_own")],
    )
    depth = min((WINDOW - 1 + rows - 1) // rows, lines - 1)
    stops = [
        (["d_met"], []),
        (["d_own_pair", "w_q"], [("w_o", ["o"], over_line)]),
        ([], [pair_of("g_met")]),
    ]
    kept, other = [kv_rows], [swapped(kv_rows, "pair")]
    for step in range(max(depth, len(stops))):
        if step < depth:
            kept.append(hop(kept[-1], 1))
        if step < len(stops):
            finish, start = stops[step]
            kept[-1], other = stream.stop((kept[-1], other), finish, start)
        if step < depth:
            other.append(swapped(kept[-1], "pair"))
    w_q = stream.blocks["w_q"]
    zq = jnp.dot(h_one, w_q, preferred_element_type=jnp.float32)
    zq = to_tokens(zq, pair, row, core)
    queries = (rotate(zq * q_scale, cosine, sine).astype(jnp.bfloat16) * scale).astype(jnp.bfloat16)
    queries, other = stream.stop(
        (queries, other),
        finish=["w_o", "g_met_pair"],
        start=[far_of("u_own"), pair_of("u_met"), pair_of("g_own_far")],
    )
    w_o = stream.blocks["w_o"]
    kept, other = jnp.concatenate(kept[::-1], 0), jnp.concatenate(other[::-1], 0)
    keys = jnp.where(even, kept, other)
    values = jnp.where(even, other, kept)
    low = depth * rows + jnp.arange(rows, dtype=jnp.int32) - jnp.minimum(places, WINDOW - 1)
    low = low[:, None]
    attended_wide, lse = attend(queries, keys, values, low)
    attended = attended_wide.astype(jnp.bfloat16)
    attended = from_tokens(attended, pair, row, core)
    zo = scatter8(
        jnp.einsum("tc,dc->td", attended, w_o, preferred_element_type=jnp.float32),
        "pair",
        lambda work: stream.stop(
            work,
            finish=["u_own_far", "u_met_pair", "g_own_far_pair"],
            start=[far_of("g_met"), pair_of("u_own_far")],
        ),
    )
    zo = stream.stop(
        zo,
        finish=["g_met_far", "u_own_far_pair"],
        start=[far_of("u_met"), pair_of("g_met_far"), pair_of("d_met")],
    )
    after_attention = zo * output_scale
    inverse_two = inverse_rms(after_attention)
    middle = inputs + after_attention * inverse_two * post_attention
    inverse_three = inverse_rms(middle)
    h_two = gather8(
        (middle * inverse_three * pre_feedforward).astype(jnp.bfloat16),
        "near",
        lambda four: stream.stop(
            four,
            finish=["u_met_far", "g_met_far_pair", "d_met_pair"],
            start=[far_of("d_own"), pair_of("u_met_far")],
        ),
    )
    w_g = assembled("g")
    zg = jnp.dot(h_two, w_g, preferred_element_type=jnp.float32)
    zg = stream.stop(
        zg,
        finish=["d_own_far", "u_met_far_pair"],
        start=[far_of("d_met"), pair_of("d_own_far")],
    )
    w_u = assembled("u")
    zu = jnp.dot(h_two, w_u, preferred_element_type=jnp.float32)
    gate_in = zg * g_scale
    up_in = zu * u_scale
    hidden = (jax.nn.gelu(gate_in, approximate=True) * up_in).astype(jnp.bfloat16)
    hidden = stream.stop(
        hidden, finish=["d_met_far", "d_own_far_pair"], start=[pair_of("d_met_far")]
    )
    w_d = assembled("d")
    zd = scatter8(
        jnp.einsum("tf,df->td", hidden, w_d, preferred_element_type=jnp.float32), "near"
    )
    fed = zd * down_scale
    inverse_four = inverse_rms(fed)
    block_out = middle + fed * inverse_four * post_feedforward

    upstream = cotangent.astype(jnp.float32)
    dfed, gain_four_grad = norm_back(fed, inverse_four, post_feedforward, upstream)
    down_scale_sum = jnp.sum(dfed * zd, axis=0)
    dzd = gather8((dfed * down_scale).astype(jnp.bfloat16), "near")

    def shared(term):
        part = lax.psum_scatter(term.astype(jnp.bfloat16), LINE, scatter_dimension=0, tiled=True)
        size = part.shape[0] // 2
        keep = lax.dynamic_slice_in_dim(part, pair * size, size, 0)
        give = lax.dynamic_slice_in_dim(part, (1 - pair) * size, size, 0)
        return (keep.astype(jnp.float32), swapped(give, "pair").astype(jnp.float32))

    def side_by_side(keep, got, first):
        return jnp.where(
            first, jnp.concatenate([keep, got], 1), jnp.concatenate([got, keep], 1)
        )

    def part(term, distance, n, p):
        size = term.shape[0] // (fars * 4)
        place = lax.rem(far + distance, fars) * 2 + n
        return lax.dynamic_slice_in_dim(term, (place * 2 + p) * size, size, 0)

    def wide(piece):
        return piece.astype(jnp.float32)

    def step_of(kind, name):
        at = (1 - near, near)[int(kind[1:] or 0)]
        end = kind[1:]

        def give(term, distance):
            return swapped(part(term, distance, at, 1 - pair), "pair")

        def far_back(term, gots):
            return [
                turned((wide(part(term, i, at, pair)) + wide(got)).astype(jnp.bfloat16), i)
                for i, got in enumerate(gots, 1)
            ]

        def near_back(term, got, others):
            return to_near(here_sum(term, at, got, others).astype(jnp.bfloat16))

        if kind[0] == "a":
            return (name + kind, [name], lambda term: [give(term, i) for i in range(1, fars)])
        if kind[0] == "b":
            return (name + kind, [name], lambda term: give(term, 0))
        if kind[0] == "f":
            return (name + kind, [name, name + "a" + end], far_back)
        return (name + kind, [name, name + "b0", name + "f0"], near_back)

    def here_sum(term, n, got, others):
        return sum((wide(piece) for piece in others), wide(part(term, 0, n, pair)) + wide(got))

    def steps(text):
        return [step_of(word[1:], word[0].upper()) for word in text.split()]

    def ended(text):
        return [word[0].upper() + word[1:] for word in text.split()]

    def result(name):
        blocks = stream.blocks
        keep = here_sum(blocks[name], near, blocks[name + "b1"], blocks[name + "f1"])
        return side_by_side(keep, wide(blocks[name + "n"]), near == 0)

    def term_of(left, right):
        return jnp.einsum("td,tf->df", left, right, preferred_element_type=jnp.float32).astype(
            jnp.bfloat16
        )

    stream.blocks["D"] = term_of(dzd, hidden)
    dzd = stream.stop(dzd, ["D"], steps("da0 da1"))
    dhidden = jnp.dot(dzd, w_d, preferred_element_type=jnp.float32)
    unused, pull = jax.vjp(
        lambda left, right: jax.nn.gelu(left, approximate=True) * right, gate_in, up_in
    )
    dgate, dup = pull(dhidden)
    gate_scale_sum = jnp.sum(dgate * zg, axis=0)
    up_scale_sum = jnp.sum(dup * zu, axis=0)
    dzg = (dgate * g_scale).astype(jnp.bfloat16)
    dzu = (dup * u_scale).astype(jnp.bfloat16)
    dzg, dzu = stream.stop((dzg, dzu), ended("da0 da1"), steps("df0 db0 db1"))
    stream.blocks["G"] = term_of(h_two, dzg)
    stream.blocks["U"] = term_of(h_two, dzu)
    dzg, dzu = stream.stop(
        (dzg, dzu), ["G", "U"] + ended("df0 db0 db1"), steps("df1 dn ga0 ga1")
    )
    dh_mid = jnp.einsum("tf,df->td", dzg, w_g, preferred_element_type=jnp.float32) + jnp.einsum(
        "tf,df->td", dzu, w_u, preferred_element_type=jnp.float32
    )
    dh_mid = stream.stop(dh_mid, ended("df1 dn ga0 ga1"), steps("gf0 ua0 ua1"))
    dh_mid = scatter8(dh_mid, "near")
    dh_mid = stream.stop(dh_mid, ended("gf0 ua0 ua1"), steps("gf1 gb0"))
    dmid_norm, gain_three_grad = norm_back(middle, inverse_three, pre_feedforward, dh_mid)
    dmiddle = upstream + dmid_norm
    dafter, gain_two_grad = norm_back(after_attention, inverse_two, post_attention, dmiddle)
    output_scale_sum = jnp.sum(dafter * zo, axis=0)
    dzo = gather8((dafter * output_scale).astype(jnp.bfloat16), "pair")
    dzo = stream.stop(dzo, ended("gf1 gb0"), steps("uf0 gb1 ub0"))
    stream.blocks["O"] = term_of(dzo, attended)
    dattended = jnp.dot(dzo, w_o, preferred_element_type=jnp.float32).astype(jnp.bfloat16)
    dattended = to_tokens(dattended, pair, row, core)
    dattended = stream.stop(dattended, ["O"] + ended("uf0 gb1 ub0"), steps("uf1 ub1 gn"))
    output_grad = side_by_side(*shared(stream.blocks["O"]), even).T

    delta = jnp.sum(dattended.astype(jnp.float32) * attended_wide, axis=-1, keepdims=True)
    dqueries, dkeys, dvalues = attend_back(queries, keys, values, low, lse, delta, dattended)
    dqueries = dqueries.T * scale

    early = (
        output_scale_sum,
        spread(gate_scale_sum, gate_scale.shape[0], f_at),
        spread(up_scale_sum, up_scale.shape[0], f_at),
        down_scale_sum,
        gain_two_grad,
        gain_three_grad,
        gain_four_grad,
    )
    (dqueries, dkeys, dvalues), early = stream.stop(
        ((dqueries, dkeys, dvalues), early), ended("uf1 ub1 gn"), steps("un")
    )
    down_grad = result("D").T
    keep = jnp.where(even, dkeys, dvalues)
    give = jnp.where(even, dvalues, dkeys).astype(jnp.bfloat16)
    got = [swapped(give[i * rows : (i + 1) * rows], "pair") for i in range(depth + 1)]
    equery = rotate(dqueries, cosine, -sine)
    query_scale_sum = jnp.sum(equery * zq, axis=0)
    dzq = from_tokens((equery * q_scale).astype(jnp.bfloat16), pair, row, core)
    q_term = jnp.einsum("td,tc->dc", h_one, dzq, preferred_element_type=jnp.float32)
    got[0], q_term = tie(got[0], q_term.astype(jnp.bfloat16))
    q_keep, q_got = shared(q_term)
    query_grad = side_by_side(q_keep, q_got, even)
    stops = [("", ""), ("un", "")]
    dkv = None
    for i in range(depth + 1):
        block = keep[i * rows : (i + 1) * rows] + got[i].astype(jnp.float32)
        if dkv is not None:
            block = block + hop(dkv.astype(jnp.bfloat16), -1).astype(jnp.float32)
        if i < len(stops):
            block = stream.stop(block, ended(stops[i][0]), steps(stops[i][1]))
        dkv = block
    ekv = jnp.where(even, rotate(dkv, cosine, -sine), dkv)
    kv_scale_sum = jnp.sum(ekv * zkv, axis=0)
    dzkv = from_tokens((ekv * kv_scale).astype(jnp.bfloat16), pair, row, core)
    kv_term = jnp.einsum("td,tc->dc", h_one, dzkv, preferred_element_type=jnp.float32)
    dzkv, kv_term = tie(dzkv, kv_term.astype(jnp.bfloat16))
    kv_keep, kv_got = shared(kv_term)
    key_grad = jnp.where(even, kv_keep, kv_got)
    value_grad = jnp.where(even, kv_got, kv_keep)
    gate_grad, up_grad = result("G"), result("U")
    dh_local = scatter8(
        jnp.einsum("tc,dc->td", dzq, w_q, preferred_element_type=jnp.float32)
        + jnp.einsum("tc,dc->td", dzkv, w_kv, preferred_element_type=jnp.float32),
        "pair",
    )
    dinput_norm, gain_one_grad = norm_back(inputs, inverse_one, pre_attention, dh_local)
    token_grad = dmiddle + dinput_norm

    late = (
        spread(query_scale_sum, query_scale.shape[0], q_at),
        spread(jnp.where(even, kv_scale_sum, 0.0), key_scale.shape[0], k_at),
        spread(jnp.where(even, 0.0, kv_scale_sum), value_scale.shape[0], k_at),
        gain_one_grad,
    )

    def summed(vectors):
        flat = total(jnp.concatenate(vectors))
        cuts, at = [], 0
        for vector in vectors:
            cuts.append(flat[at : at + vector.shape[0]])
            at += vector.shape[0]
        return cuts

    o_sum, g_sum, u_sum, d_sum, two_sum, three_sum, four_sum = summed(early)
    q_sum, k_sum, v_sum, one_sum = summed(late)
    return (
        block_out,
        token_grad,
        query_grad,
        key_grad,
        value_grad,
        output_grad,
        gate_grad,
        up_grad,
        down_grad,
        q_sum,
        k_sum,
        v_sum,
        o_sum,
        g_sum,
        u_sum,
        d_sum,
        one_sum,
        two_sum,
        three_sum,
        four_sum,
    )


def solution(mesh):
    seq_count, tp_count = mesh.shape["seq"], mesh.shape["tp"]
    wide = Mesh(mesh.devices.reshape(seq_count // 4, 2, 2, tp_count // 2, 2), EVERY)
    seq, tp = LINE + ("pair",), ("row", "core")
    return jax.shard_map(
        body,
        mesh=wide,
        in_specs=(P(EVERY, None),) * 2
        + (P(seq, tp),) * 3
        + (P(tp, seq),)
        + (P(seq, tp),) * 2
        + (P(tp, seq),)
        + (P(),) * 11
        + (P(seq),),
        out_specs=(P(EVERY, None),) * 2
        + (P(seq, tp),) * 3
        + (P(tp, seq),)
        + (P(seq, tp),) * 2
        + (P(tp, seq),)
        + (P(),) * 11,
        check_vma=False,
    )
```

```python
import math

import jax
import jax.numpy as jnp
from jax import lax
from jax.experimental import pallas as pl
from jax.experimental.pallas import tpu as pltpu
from jax.sharding import Mesh
from jax.sharding import PartitionSpec as P

HEAD_DIM = 256
WINDOW = 4096
CAP = 50
EPSILON = 1e-06

EVERY = ("line", "pair", "row", "core")
SWAP = [(0, 1), (1, 0)]


def swapped(block, axis):
    return lax.ppermute(block, axis, SWAP)


def hop(block, distance):
    count = lax.axis_size("line")
    route = [(i, i + distance) for i in range(count) if 0 <= i + distance < count]
    return lax.ppermute(block, "line", route)


def put_together(sources, moves, shape):
    count = len(moves())
    if any(size % 16 for _, _, size, _, _ in moves()):
        out = jnp.zeros(shape, sources[0].dtype)
        for source, start, size, row, column in moves():
            piece = lax.dynamic_slice_in_dim(sources[source], start, size, 0)
            out = lax.dynamic_update_slice(out, piece, (row, column))
        return out

    def rows_at(row, size):
        return pl.ds(row if isinstance(row, int) else pl.multiple_of(row, 16), size)

    def kernel(*refs):
        out, sems = refs[len(sources)], refs[len(sources) + 1]
        copies = []
        for i, (source, start, size, row, column) in enumerate(moves()):
            piece = refs[source].at[rows_at(start, size)]
            target = out.at[rows_at(row, size), pl.ds(column, sources[source].shape[1])]
            copies.append(pltpu.make_async_copy(piece, target, sems.at[i]))
        for copy in copies:
            copy.start()
        for copy in copies:
            copy.wait()

    size = 2 * math.prod(shape) * sources[0].dtype.itemsize
    return pl.pallas_call(
        kernel,
        out_shape=jax.ShapeDtypeStruct(shape, sources[0].dtype),
        in_specs=[pl.BlockSpec(memory_space=pl.ANY)] * len(sources),
        out_specs=pl.BlockSpec(memory_space=pltpu.VMEM),
        scratch_shapes=[pltpu.SemaphoreType.DMA((count,))],
        compiler_params=pltpu.CompilerParams(vmem_limit_bytes=size // 2 + 4 * 1024 * 1024),
        cost_estimate=pl.CostEstimate(flops=0, bytes_accessed=size, transcendentals=0),
    )(*sources)


def tie(*values):
    return lax.optimization_barrier(values)


class Stream:
    def __init__(self, **blocks):
        self.blocks = blocks

    def stop(self, work, finish=(), start=()):
        here = [self.blocks[name] for name in finish]
        sources = [[self.blocks[name] for name in names] for _, names, _ in start]
        work, here, sources = tie(work, here, sources)
        self.blocks.update(zip(finish, here))
        for (name, _, route), blocks in zip(start, sources):
            self.blocks[name] = route(*blocks)
        return work


def nested_slice(codes):
    values = codes.astype(jnp.float32)
    return (jnp.clip(jnp.floor((values + 8.0) / 16.0), -8.0, 7.0) * 16.0).astype(jnp.bfloat16)


def inverse_rms(values):
    return lax.rsqrt(jnp.mean(values * values, axis=-1, keepdims=True) + EPSILON)


def norm_back(source, inverse, gain, upstream):
    scaled = upstream * gain
    inner = jnp.mean(scaled * source, axis=-1, keepdims=True)
    back = inverse * scaled - source * (inverse * inverse * inverse) * inner
    return (back, jnp.sum(upstream * source * inverse, axis=0))


def phases(positions):
    freqs = 10000.0 ** (-2.0 * jnp.arange(HEAD_DIM // 2, dtype=jnp.float32) / HEAD_DIM)
    angle = positions.astype(jnp.float32)[:, None] * freqs[None, :]
    return (jnp.cos(angle), jnp.sin(angle))


def rotate(values, cosine, sine):
    half = values.shape[-1] // 2
    first = values[..., :half]
    second = values[..., half:]
    return jnp.concatenate([first * cosine - second * sine, second * cosine + first * sine], -1)


def spread(piece, total, offset):
    return lax.dynamic_update_slice_in_dim(jnp.zeros((total,), jnp.float32), piece, offset, 0)


def in_order(mine, other, place):
    return lax.dynamic_slice_in_dim(
        jnp.concatenate([other, mine, other], 0), (1 - place) * mine.shape[0], 2 * mine.shape[0], 0
    )


def half_of(block, place):
    size = block.shape[1] // 2
    return lax.dynamic_slice_in_dim(block, place * size, size, 1)


def unstopped(work):
    return work


def gather8(block, stop=unstopped):
    size, width = block.shape
    cut = size // 2
    left, right = block[:cut], block[cut:]
    left_p, right_r = swapped(left, "pair"), swapped(right, "row")
    left_r, right_p = swapped(left, "row"), swapped(right, "pair")
    left_pr, right_pr = swapped(left_p, "row"), swapped(right_r, "pair")
    halves = [left, right, left_r, right_r, left_p, right_p, left_pr, right_pr]
    four = put_together(
        halves, lambda: [(i, 0, cut, i * cut, 0) for i in range(8)], (4 * size, width)
    )
    four = stop(four)
    return put_together(
        [four, swapped(four, "core")],
        lambda: [(i, 0, 4 * size, i * 4 * size, 0) for i in range(2)],
        (8 * size, width),
    )


def scatter8(terms, stop=unstopped, stop_two=unstopped):
    size = terms.shape[0] // 8

    def summed(keep, give, axis):
        return keep + swapped(give.astype(jnp.bfloat16), axis).astype(jnp.float32)

    four = summed(terms[: 4 * size], terms[4 * size :], "core")
    four = stop(four).reshape(2, 2, size, terms.shape[1])
    cut = terms.shape[1] // 2
    left, right = four[..., :cut], four[..., cut:]
    left = summed(left[0], left[1], "pair")
    right = summed(right[:, 0], right[:, 1], "row")
    left, right = stop_two((left, right))
    left = summed(left[0], left[1], "row")
    right = summed(right[0], right[1], "pair")
    return jnp.concatenate([left, right], 1)


def blocks(rows, places):
    size = rows.shape[0] // len(places)
    return jnp.concatenate(
        [lax.dynamic_slice_in_dim(rows, place * size, size, 0) for place in places], 0
    )


def to_tokens(rows, pair, row, core):
    places = [
        ((c ^ core) * 4 + (p ^ pair) * 2 + (r ^ row))
        for p in range(2)
        for r in range(2)
        for c in range(2)
    ]
    return blocks(rows, places)


def from_tokens(rows, pair, row, core):
    places = [
        ((p ^ pair) * 4 + (r ^ row) * 2 + (c ^ core))
        for c in range(2)
        for p in range(2)
        for r in range(2)
    ]
    return blocks(rows, places)


def exchanged(vector, axis):
    if isinstance(axis, str):
        return swapped(vector, axis)
    count = lax.axis_size("line")
    return lax.ppermute(vector, "line", [(i, i ^ axis) for i in range(count)])


def across(left, right):
    return lax.dot_general(left, right, (((1,), (1,)), ((), ())), preferred_element_type=jnp.float32)

def attend(queries, keys, values, low, bq=512, bk=1024):
    rows, span = queries.shape[0], keys.shape[0]
    offset = span - rows
    first = jnp.min(low.reshape(rows // bq, bq), axis=1) // bk

    def kernel(first_ref, q_ref, k_ref, v_ref, low_ref, o_ref, lse_ref, sums, totals):
        block = pl.program_id(0)
        high = offset + block * bq + lax.broadcasted_iota(jnp.int32, (bq, 1), 0)
        sums[...] = jnp.zeros_like(sums)
        totals[...] = jnp.zeros_like(totals)

        def chunk(c, carry):
            at = pl.multiple_of(c * bk, bk)
            raw = across(q_ref[...], k_ref[pl.ds(at, bk), :])
            place = at + lax.broadcasted_iota(jnp.int32, (bq, bk), 1)
            seen = (place >= low_ref[...]) & (place <= high)
            expo = jnp.where(seen, jnp.exp(CAP * jnp.tanh(raw * (1.0 / CAP))), 0.0)
            totals[...] += jnp.sum(expo, axis=-1, keepdims=True)
            sums[...] += jnp.dot(expo.astype(jnp.bfloat16), v_ref[pl.ds(at, bk), :], preferred_element_type=jnp.float32)
            return carry

        lax.fori_loop(first_ref[block], (offset + (block + 1) * bq - 1) // bk + 1, chunk, 0)
        o_ref[...] = sums[...] / totals[...]
        lse_ref[...] = jnp.log(totals[...])

    whole = lambda i, *_: (0, 0)
    mine = lambda i, *_: (i, 0)
    return pl.pallas_call(
        kernel,
        out_shape=(jax.ShapeDtypeStruct((rows, HEAD_DIM), jnp.float32), jax.ShapeDtypeStruct((rows, 1), jnp.float32)),
        grid_spec=pltpu.PrefetchScalarGridSpec(
            num_scalar_prefetch=1, grid=(rows // bq,),
            in_specs=[pl.BlockSpec((bq, HEAD_DIM), mine), pl.BlockSpec((span, HEAD_DIM), whole), pl.BlockSpec((span, HEAD_DIM), whole), pl.BlockSpec((bq, 1), mine)],
            out_specs=(pl.BlockSpec((bq, HEAD_DIM), mine), pl.BlockSpec((bq, 1), mine)),
            scratch_shapes=[pltpu.VMEM((bq, HEAD_DIM), jnp.float32), pltpu.VMEM((bq, 1), jnp.float32)]),
        compiler_params=pltpu.CompilerParams(vmem_limit_bytes=40 * 1024 * 1024),
        cost_estimate=pl.CostEstimate(flops=4 * rows * span * HEAD_DIM, bytes_accessed=4 * span * HEAD_DIM, transcendentals=2 * rows * span),
    )(first, queries, keys, values, low)

def attend_back(queries, keys, values, low, lse, delta, upstream, bq=1024, bk=512):
    rows, span = queries.shape[0], keys.shape[0]
    offset = span - rows
    first = jnp.min(low.reshape(rows // bq, bq), axis=1) // bk

    def kernel(first_ref, q_ref, up_ref, k_ref, kt_ref, v_ref, low_ref, lse_ref, delta_ref, dq_ref, dk_ref, dv_ref):
        block = pl.program_id(0)
        high = offset + block * bq + lax.broadcasted_iota(jnp.int32, (1, bq), 1)

        @pl.when(block == 0)
        def clear():
            dk_ref[...] = jnp.zeros_like(dk_ref)
            dv_ref[...] = jnp.zeros_like(dv_ref)

        dq_ref[...] = jnp.zeros_like(dq_ref)

        def chunk(c, carry):
            at = pl.multiple_of(c * bk, bk)
            here = pl.ds(at, bk)
            ratio = jnp.tanh(across(k_ref[here, :], q_ref[...]) * (1.0 / CAP))
            place = at + lax.broadcasted_iota(jnp.int32, (bk, bq), 0)
            seen = (place >= low_ref[...]) & (place <= high)
            probs = jnp.where(seen, jnp.exp(CAP * ratio - lse_ref[...]), 0.0)
            dv_ref[here, :] += jnp.dot(probs.astype(jnp.bfloat16), up_ref[...], preferred_element_type=jnp.float32)
            dprobs = across(v_ref[here, :], up_ref[...])
            draw = (probs * (dprobs - delta_ref[...]) * (1.0 - ratio * ratio)).astype(jnp.bfloat16)
            dk_ref[here, :] += jnp.dot(draw, q_ref[...], preferred_element_type=jnp.float32)
            dq_ref[...] += jnp.dot(kt_ref[:, here], draw, preferred_element_type=jnp.float32)
            return carry

        lax.fori_loop(first_ref[block], (offset + (block + 1) * bq - 1) // bk + 1, chunk, 0)

    whole = lambda i, *_: (0, 0)
    mine = lambda i, *_: (i, 0)
    across_lanes = lambda i, *_: (0, i)
    return pl.pallas_call(
        kernel,
        out_shape=(jax.ShapeDtypeStruct((HEAD_DIM, rows), jnp.float32), jax.ShapeDtypeStruct((span, HEAD_DIM), jnp.float32), jax.ShapeDtypeStruct((span, HEAD_DIM), jnp.float32)),
        grid_spec=pltpu.PrefetchScalarGridSpec(
            num_scalar_prefetch=1, grid=(rows // bq,),
            in_specs=[pl.BlockSpec((bq, HEAD_DIM), mine), pl.BlockSpec((bq, HEAD_DIM), mine), pl.BlockSpec((span, HEAD_DIM), whole), pl.BlockSpec((HEAD_DIM, span), whole), pl.BlockSpec((span, HEAD_DIM), whole),
                      pl.BlockSpec((1, bq), across_lanes), pl.BlockSpec((1, bq), across_lanes), pl.BlockSpec((1, bq), across_lanes)],
            out_specs=(pl.BlockSpec((HEAD_DIM, bq), across_lanes), pl.BlockSpec((span, HEAD_DIM), whole), pl.BlockSpec((span, HEAD_DIM), whole))),
        compiler_params=pltpu.CompilerParams(vmem_limit_bytes=48 * 1024 * 1024),
        cost_estimate=pl.CostEstimate(flops=10 * rows * span * HEAD_DIM, bytes_accessed=12 * span * HEAD_DIM, transcendentals=2 * rows * span),
    )(first, queries, upstream, keys, keys.T, values, low.T, lse.T, delta.T)


def body(
    tokens,
    cotangent,
    query_weight,
    key_weight,
    value_weight,
    output_weight,
    gate_weight,
    up_weight,
    down_weight,
    query_scale,
    key_scale,
    value_scale,
    output_scale,
    gate_scale,
    up_scale,
    down_scale,
    pre_attention,
    post_attention,
    pre_feedforward,
    post_feedforward,
    positions,
):
    lines = lax.axis_size("line")
    line, pair = lax.axis_index("line"), lax.axis_index("pair")
    row, core = lax.axis_index("row"), lax.axis_index("core")
    tp_index = row * 2 + core
    scale = 1.0 / math.sqrt(HEAD_DIM)
    even = pair == 0
    qcols = query_weight.shape[1] // 2
    kcols = key_weight.shape[1]
    ocols = output_weight.shape[0] // 2
    fcols = gate_weight.shape[1] // 2
    rows = 8 * tokens.shape[0]

    wq, wk, wv, wo, wg, wu, wd = (
        nested_slice(query_weight),
        nested_slice(key_weight),
        nested_slice(value_weight),
        nested_slice(output_weight.T),
        nested_slice(gate_weight),
        nested_slice(up_weight),
        nested_slice(down_weight.T),
    )

    def paired(keep, give):
        return in_order(keep, swapped(give, "pair"), pair)

    def over_line(block):
        return lax.all_gather(block, "line", axis=0, tiled=True)

    def shared_out(shard):
        return paired(half_of(shard, pair), half_of(shard, 1 - pair))

    kv_block = paired(jnp.where(even, wk, wv), jnp.where(even, wv, wk))
    stream = Stream(
        qkvo=jnp.concatenate([shared_out(wq), kv_block, shared_out(wo)], 1),
        gu=jnp.concatenate([shared_out(wg), shared_out(wu)], 1),
        d=shared_out(wd),
    )

    q_at = tp_index * 2 * qcols + pair * qcols
    k_at = tp_index * kcols
    f_at = tp_index * 2 * fcols + pair * fcols
    q_scale = lax.dynamic_slice_in_dim(query_scale, q_at, qcols, 0)
    k_scale = lax.dynamic_slice_in_dim(key_scale, k_at, kcols, 0)
    v_scale = lax.dynamic_slice_in_dim(value_scale, k_at, kcols, 0)
    kv_scale = jnp.where(even, k_scale, v_scale)
    g_scale = lax.dynamic_slice_in_dim(gate_scale, f_at, fcols, 0)
    u_scale = lax.dynamic_slice_in_dim(up_scale, f_at, fcols, 0)

    inputs = tokens.astype(jnp.float32)
    inverse_one = inverse_rms(inputs)
    h_local = (inputs * inverse_one * pre_attention).astype(jnp.bfloat16)
    h_local = stream.stop(h_local, start=[("w_qkvo", ["qkvo"], over_line)])
    h_one = gather8(h_local)
    h_one = stream.stop(h_one, ["w_qkvo"], [("w_gu", ["gu"], over_line)])
    w_qkv = stream.blocks["w_qkvo"][:, : qcols + kcols]
    w_o = stream.blocks["w_qkvo"][:, qcols + kcols :]
    places = in_order(positions, swapped(positions, "pair"), pair)
    cosine, sine = phases(places)

    z_qkv = jnp.dot(h_one, w_qkv, preferred_element_type=jnp.float32)
    z_qkv = to_tokens(z_qkv, pair, row, core)
    zq, zkv = z_qkv[:, :qcols], z_qkv[:, qcols:]
    kv_rows = zkv * kv_scale
    kv_rows = jnp.where(even, rotate(kv_rows, cosine, sine), kv_rows).astype(jnp.bfloat16)
    depth = min((WINDOW - 1 + rows - 1) // rows, lines - 1)
    kept, other = [kv_rows], [swapped(kv_rows, "pair")]
    for step in range(depth):
        kept.append(hop(kept[-1], 1))
        kept[-1], other = stream.stop((kept[-1], other))
        other.append(swapped(kept[-1], "pair"))
    queries = (rotate(zq * q_scale, cosine, sine).astype(jnp.bfloat16) * scale).astype(jnp.bfloat16)
    kept, other = jnp.concatenate(kept[::-1], 0), jnp.concatenate(other[::-1], 0)
    keys = jnp.where(even, kept, other)
    values = jnp.where(even, other, kept)
    low = depth * rows + jnp.arange(rows, dtype=jnp.int32) - jnp.minimum(places, WINDOW - 1)
    low = low[:, None]
    attended_wide, lse = attend(queries, keys, values, low)
    attended = attended_wide.astype(jnp.bfloat16)
    attended = from_tokens(attended, pair, row, core)
    zo = jnp.einsum("tc,dc->td", attended, w_o, preferred_element_type=jnp.float32)
    zo = scatter8(zo)
    zo = stream.stop(zo, ["w_gu"], [("w_d", ["d"], over_line)])
    w_gu, w_d = stream.blocks["w_gu"], stream.blocks["w_d"]
    after_attention = zo * output_scale
    inverse_two = inverse_rms(after_attention)
    middle = inputs + after_attention * inverse_two * post_attention
    inverse_three = inverse_rms(middle)
    h_two = gather8((middle * inverse_three * pre_feedforward).astype(jnp.bfloat16))
    z_gu = jnp.dot(h_two, w_gu, preferred_element_type=jnp.float32)
    zg, zu = z_gu[:, :fcols], z_gu[:, fcols:]
    gate_in = zg * g_scale
    up_in = zu * u_scale
    hidden = (jax.nn.gelu(gate_in, approximate=True) * up_in).astype(jnp.bfloat16)
    zd = scatter8(jnp.einsum("tf,df->td", hidden, w_d, preferred_element_type=jnp.float32))
    fed = zd * down_scale
    inverse_four = inverse_rms(fed)
    block_out = middle + fed * inverse_four * post_feedforward

    upstream = cotangent.astype(jnp.float32)
    dfed, gain_four_grad = norm_back(fed, inverse_four, post_feedforward, upstream)
    down_scale_sum = jnp.sum(dfed * zd, axis=0)
    dzd = gather8((dfed * down_scale).astype(jnp.bfloat16))

    def over_line_sum(term):
        return lax.psum_scatter(term, "line", scatter_dimension=0, tiled=True)

    def rows_for(part, place):
        size = part.shape[0] // 2
        return lax.dynamic_slice_in_dim(part, place * size, size, 0).astype(jnp.float32)

    def swap_of(name):
        def route(part):
            return swapped(rows_for(part, 1 - pair).astype(jnp.bfloat16), "pair")

        return (name + "_got", [name + "_sum"], route)

    def shared(name):
        return rows_for(stream.blocks[name + "_sum"], pair), stream.blocks[name + "_got"].astype(
            jnp.float32
        )

    def side_by_side(keep, got, first):
        return jnp.where(
            first, jnp.concatenate([keep, got], 1), jnp.concatenate([got, keep], 1)
        )

    def term_of(left, right):
        return jnp.einsum("td,tf->df", left, right, preferred_element_type=jnp.float32).astype(
            jnp.bfloat16
        )

    stream.blocks["D"] = term_of(dzd, hidden)
    dzd = stream.stop(dzd, ["D"], [("D_sum", ["D"], over_line_sum)])
    dhidden = jnp.dot(dzd, w_d, preferred_element_type=jnp.float32)
    unused, pull = jax.vjp(
        lambda left, right: jax.nn.gelu(left, approximate=True) * right, gate_in, up_in
    )
    dgate, dup = pull(dhidden)
    gate_scale_sum = jnp.sum(dgate * zg, axis=0)
    up_scale_sum = jnp.sum(dup * zu, axis=0)
    dzg = (dgate * g_scale).astype(jnp.bfloat16)
    dzu = (dup * u_scale).astype(jnp.bfloat16)
    dh_mid = (
        jnp.einsum("tf,df->td", dzg, w_gu[:, :fcols], preferred_element_type=jnp.float32)
        + jnp.einsum("tf,df->td", dzu, w_gu[:, fcols:], preferred_element_type=jnp.float32)
    )
    stream.blocks["GU"] = jnp.concatenate([term_of(h_two, dzg), term_of(h_two, dzu)], 1)
    dh_mid = scatter8(
        dh_mid,
        lambda work: stream.stop(
            work, ["GU", "D_sum"], [("GU_sum", ["GU"], over_line_sum), swap_of("D")]
        ),
    )
    dmid_norm, gain_three_grad = norm_back(middle, inverse_three, pre_feedforward, dh_mid)
    dmiddle = upstream + dmid_norm
    dafter, gain_two_grad = norm_back(after_attention, inverse_two, post_attention, dmiddle)
    output_scale_sum = jnp.sum(dafter * zo, axis=0)
    early = (
        output_scale_sum,
        spread(gate_scale_sum, gate_scale.shape[0], f_at),
        spread(up_scale_sum, up_scale.shape[0], f_at),
        down_scale_sum,
        gain_two_grad,
        gain_three_grad,
        gain_four_grad,
    )
    dzo = gather8((dafter * output_scale).astype(jnp.bfloat16))
    o_term = term_of(dzo, attended)
    dattended = jnp.dot(dzo, w_o, preferred_element_type=jnp.float32).astype(jnp.bfloat16)
    dattended = to_tokens(dattended, pair, row, core)
    delta = jnp.sum(dattended.astype(jnp.float32) * attended_wide, axis=-1, keepdims=True)
    dqueries, dkeys, dvalues = attend_back(queries, keys, values, low, lse, delta, dattended)
    dqueries = dqueries.T * scale

    keep = jnp.where(even, dkeys, dvalues)
    give = jnp.where(even, dvalues, dkeys).astype(jnp.bfloat16)
    got = [swapped(give[i * rows : (i + 1) * rows], "pair") for i in range(depth + 1)]
    equery = rotate(dqueries, cosine, -sine)
    query_scale_sum = jnp.sum(equery * zq, axis=0)
    dzq = from_tokens((equery * q_scale).astype(jnp.bfloat16), pair, row, core)
    q_term = term_of(h_one, dzq)
    got[0], q_term, o_term = stream.stop((got[0], q_term, o_term))
    dkv = None
    for i in range(depth + 1):
        block = keep[i * rows : (i + 1) * rows] + got[i].astype(jnp.float32)
        if dkv is not None:
            block = block + hop(dkv.astype(jnp.bfloat16), -1).astype(jnp.float32)
        dkv = block
    dkv = stream.stop(dkv, ["GU_sum"], [swap_of("GU")])
    ekv = jnp.where(even, rotate(dkv, cosine, -sine), dkv)
    kv_scale_sum = jnp.sum(ekv * zkv, axis=0)
    dzkv = from_tokens((ekv * kv_scale).astype(jnp.bfloat16), pair, row, core)
    kv_term = term_of(h_one, dzkv)
    stream.blocks["QKVO"] = jnp.concatenate([q_term, kv_term, o_term], 1)
    dzkv = stream.stop(
        dzkv, ["QKVO", "D_got"], [("QKVO_sum", ["QKVO"], over_line_sum)]
    )
    dh_one = jnp.einsum(
        "tc,dc->td",
        jnp.concatenate([dzq, dzkv], 1),
        w_qkv,
        preferred_element_type=jnp.float32,
    )
    gain_one_part = jnp.sum(dh_one * h_one.astype(jnp.float32), axis=0) / pre_attention
    late = (
        spread(query_scale_sum, query_scale.shape[0], q_at),
        spread(jnp.where(even, kv_scale_sum, 0.0), key_scale.shape[0], k_at),
        spread(jnp.where(even, 0.0, kv_scale_sum), value_scale.shape[0], k_at),
        gain_one_part,
    )
    sums = jnp.concatenate(early + late)
    dh_one, sums = stream.stop((dh_one, sums), ["GU_got"])
    for axis in ["core", "row", "pair"] + [1 << i for i in range(lines.bit_length() - 1)]:
        sums = sums + exchanged(sums, axis)
    stream.blocks["sums"] = sums
    dh_local = scatter8(
        dh_one,
        stop_two=lambda work: stream.stop(work, ["QKVO_sum", "sums"], [swap_of("QKVO")]),
    )
    sums = stream.blocks["sums"]
    dinput_norm, unused = norm_back(inputs, inverse_one, pre_attention, dh_local)
    token_grad = dmiddle + dinput_norm
    d_keep, d_got = shared("D")
    down_grad = side_by_side(d_keep, d_got, even).T
    gu_keep, gu_got = shared("GU")
    gate_grad = side_by_side(gu_keep[:, :fcols], gu_got[:, :fcols], even)
    up_grad = side_by_side(gu_keep[:, fcols:], gu_got[:, fcols:], even)
    keep, got = shared("QKVO")
    query_grad = side_by_side(keep[:, :qcols], got[:, :qcols], even)
    kv_keep, kv_got = keep[:, qcols : qcols + kcols], got[:, qcols : qcols + kcols]
    key_grad = jnp.where(even, kv_keep, kv_got)
    value_grad = jnp.where(even, kv_got, kv_keep)
    output_grad = side_by_side(keep[:, qcols + kcols :], got[:, qcols + kcols :], even).T

    cuts, at = [], 0
    for vector in early + late:
        cuts.append(sums[at : at + vector.shape[0]])
        at += vector.shape[0]
    o_sum, g_sum, u_sum, d_sum, two_sum, three_sum, four_sum, q_sum, k_sum, v_sum, one_sum = cuts
    return (
        block_out,
        token_grad,
        query_grad,
        key_grad,
        value_grad,
        output_grad,
        gate_grad,
        up_grad,
        down_grad,
        q_sum,
        k_sum,
        v_sum,
        o_sum,
        g_sum,
        u_sum,
        d_sum,
        one_sum,
        two_sum,
        three_sum,
        four_sum,
    )


def solution(mesh):
    seq_count, tp_count = mesh.shape["seq"], mesh.shape["tp"]
    wide = Mesh(mesh.devices.reshape(seq_count // 2, 2, tp_count // 2, 2), EVERY)
    seq, tp = ("line", "pair"), ("row", "core")
    return jax.shard_map(
        body,
        mesh=wide,
        in_specs=(P(EVERY, None),) * 2
        + (P(seq, tp),) * 3
        + (P(tp, seq),)
        + (P(seq, tp),) * 2
        + (P(tp, seq),)
        + (P(),) * 11
        + (P(seq),),
        out_specs=(P(EVERY, None),) * 2
        + (P(seq, tp),) * 3
        + (P(tp, seq),)
        + (P(seq, tp),) * 2
        + (P(tp, seq),)
        + (P(),) * 11,
        check_vma=False,
    )
```

```python
import math

import jax
import jax.numpy as jnp
from jax import lax
from jax.experimental import pallas as pl
from jax.experimental.pallas import tpu as pltpu
from jax.sharding import Mesh
from jax.sharding import PartitionSpec as P

HEAD_DIM = 256
WINDOW = 4096
CAP = 50
EPSILON = 1e-06

EVERY = ("line", "pair", "row", "core")
SWAP = [(0, 1), (1, 0)]


def swapped(block, axis):
    return lax.ppermute(block, axis, SWAP)


def hop(block, distance):
    count = lax.axis_size("line")
    route = [(i, i + distance) for i in range(count) if 0 <= i + distance < count]
    return lax.ppermute(block, "line", route)


def put_together(sources, moves, shape):
    count = len(moves())
    if any(size % 16 for _, _, size, _, _ in moves()):
        out = jnp.zeros(shape, sources[0].dtype)
        for source, start, size, row, column in moves():
            piece = lax.dynamic_slice_in_dim(sources[source], start, size, 0)
            out = lax.dynamic_update_slice(out, piece, (row, column))
        return out

    def rows_at(row, size):
        return pl.ds(row if isinstance(row, int) else pl.multiple_of(row, 16), size)

    def kernel(*refs):
        out, sems = refs[len(sources)], refs[len(sources) + 1]
        copies = []
        for i, (source, start, size, row, column) in enumerate(moves()):
            piece = refs[source].at[rows_at(start, size)]
            target = out.at[rows_at(row, size), pl.ds(column, sources[source].shape[1])]
            copies.append(pltpu.make_async_copy(piece, target, sems.at[i]))
        for copy in copies:
            copy.start()
        for copy in copies:
            copy.wait()

    size = 2 * math.prod(shape) * sources[0].dtype.itemsize
    return pl.pallas_call(
        kernel,
        out_shape=jax.ShapeDtypeStruct(shape, sources[0].dtype),
        in_specs=[pl.BlockSpec(memory_space=pl.ANY)] * len(sources),
        out_specs=pl.BlockSpec(memory_space=pltpu.VMEM),
        scratch_shapes=[pltpu.SemaphoreType.DMA((count,))],
        compiler_params=pltpu.CompilerParams(vmem_limit_bytes=size // 2 + 4 * 1024 * 1024),
        cost_estimate=pl.CostEstimate(flops=0, bytes_accessed=size, transcendentals=0),
    )(*sources)


def tie(*values):
    return lax.optimization_barrier(values)


class Stream:
    def __init__(self, **blocks):
        self.blocks = blocks

    def stop(self, work, finish=(), start=()):
        here = [self.blocks[name] for name in finish]
        sources = [[self.blocks[name] for name in names] for _, names, _ in start]
        work, here, sources = tie(work, here, sources)
        self.blocks.update(zip(finish, here))
        for (name, _, route), blocks in zip(start, sources):
            self.blocks[name] = route(*blocks)
        return work


def nested_slice(codes):
    values = codes.astype(jnp.float32)
    return (jnp.clip(jnp.floor((values + 8.0) / 16.0), -8.0, 7.0) * 16.0).astype(jnp.bfloat16)


def inverse_rms(values):
    return lax.rsqrt(jnp.mean(values * values, axis=-1, keepdims=True) + EPSILON)


def norm_back(source, inverse, gain, upstream):
    scaled = upstream * gain
    inner = jnp.mean(scaled * source, axis=-1, keepdims=True)
    back = inverse * scaled - source * (inverse * inverse * inverse) * inner
    return (back, jnp.sum(upstream * source * inverse, axis=0))


def phases(positions):
    freqs = 10000.0 ** (-2.0 * jnp.arange(HEAD_DIM // 2, dtype=jnp.float32) / HEAD_DIM)
    angle = positions.astype(jnp.float32)[:, None] * freqs[None, :]
    return (jnp.cos(angle), jnp.sin(angle))


def rotate(values, cosine, sine):
    half = values.shape[-1] // 2
    first = values[..., :half]
    second = values[..., half:]
    return jnp.concatenate([first * cosine - second * sine, second * cosine + first * sine], -1)


def spread(piece, total, offset):
    return lax.dynamic_update_slice_in_dim(jnp.zeros((total,), jnp.float32), piece, offset, 0)


def in_order(mine, other, place):
    return lax.dynamic_slice_in_dim(
        jnp.concatenate([other, mine, other], 0), (1 - place) * mine.shape[0], 2 * mine.shape[0], 0
    )


def half_of(block, place):
    size = block.shape[1] // 2
    return lax.dynamic_slice_in_dim(block, place * size, size, 1)


def unstopped(work):
    return work


def gather8(block, with_halves=None):
    size, width = block.shape
    cut = size // 2
    left, right = block[:cut], block[cut:]
    left_p, right_r = swapped(left, "pair"), swapped(right, "row")
    left_r, right_p = swapped(left, "row"), swapped(right, "pair")
    left_pr, right_pr = swapped(left_p, "row"), swapped(right_r, "pair")
    halves = [left, right, left_r, right_r, left_p, right_p, left_pr, right_pr]
    four = put_together(
        halves, lambda: [(i, 0, cut, i * cut, 0) for i in range(8)], (4 * size, width)
    )
    other = swapped(four, "core")
    if with_halves is not None:
        four, other = with_halves(four, other)
    return put_together(
        [four, other],
        lambda: [(i, 0, 4 * size, i * 4 * size, 0) for i in range(2)],
        (8 * size, width),
    )


def summed(keep, got):
    return keep + got.astype(jnp.float32)


def sent(piece, axis):
    return swapped(piece.astype(jnp.bfloat16), axis)


def scatter8(terms, stop=unstopped):
    mine, others = terms
    size, width = mine.shape[0] // 4, mine.shape[1]
    mine, got = tie(mine, sent(others, "core"))
    four = stop(summed(mine, got)).reshape(2, 2, size, width)
    left, right = four[..., : width // 2], four[..., width // 2 :]
    left = summed(left[0], sent(left[1], "pair"))
    right = summed(right[:, 0], sent(right[:, 1], "row"))
    left = summed(left[0], sent(left[1], "row"))
    right = summed(right[0], sent(right[1], "pair"))
    return jnp.concatenate([left, right], 1)


def scatter8_last(terms, stop):
    mine, others = terms
    size, width = mine.shape[0] // 4, mine.shape[1]
    four = summed(mine, sent(others, "core")).reshape(2, 2, size, width)
    two = stop(summed(four[0], sent(four[1], "pair")))
    return summed(two[0], sent(two[1], "row"))


def blocks(rows, places):
    size = rows.shape[0] // len(places)
    return jnp.concatenate(
        [lax.dynamic_slice_in_dim(rows, place * size, size, 0) for place in places], 0
    )


def to_tokens(rows, pair, row, core):
    places = [
        ((c ^ core) * 4 + (p ^ pair) * 2 + (r ^ row))
        for p in range(2)
        for r in range(2)
        for c in range(2)
    ]
    return blocks(rows, places)


def from_tokens(rows, pair, row, core):
    places = [
        ((p ^ pair) * 4 + (r ^ row) * 2 + (c ^ core))
        for c in range(2)
        for p in range(2)
        for r in range(2)
    ]
    return blocks(rows, places)


def exchanged(vector, axis):
    if isinstance(axis, str):
        return swapped(vector, axis)
    count = lax.axis_size("line")
    return lax.ppermute(vector, "line", [(i, i ^ axis) for i in range(count)])


def across(left, right):
    return lax.dot_general(left, right, (((1,), (1,)), ((), ())), preferred_element_type=jnp.float32)

def attend(queries, keys, values, low, bq=512, bk=1024):
    rows, span = queries.shape[0], keys.shape[0]
    offset = span - rows
    first = jnp.min(low.reshape(rows // bq, bq), axis=1) // bk

    def kernel(first_ref, q_ref, k_ref, v_ref, low_ref, o_ref, lse_ref, sums, totals):
        block = pl.program_id(0)
        high = offset + block * bq + lax.broadcasted_iota(jnp.int32, (bq, 1), 0)
        sums[...] = jnp.zeros_like(sums)
        totals[...] = jnp.zeros_like(totals)

        def chunk(c, carry):
            at = pl.multiple_of(c * bk, bk)
            raw = across(q_ref[...], k_ref[pl.ds(at, bk), :])
            place = at + lax.broadcasted_iota(jnp.int32, (bq, bk), 1)
            seen = (place >= low_ref[...]) & (place <= high)
            expo = jnp.where(seen, jnp.exp(CAP * jnp.tanh(raw * (1.0 / CAP))), 0.0)
            totals[...] += jnp.sum(expo, axis=-1, keepdims=True)
            sums[...] += jnp.dot(expo.astype(jnp.bfloat16), v_ref[pl.ds(at, bk), :], preferred_element_type=jnp.float32)
            return carry

        lax.fori_loop(first_ref[block], (offset + (block + 1) * bq - 1) // bk + 1, chunk, 0)
        o_ref[...] = sums[...] / totals[...]
        lse_ref[...] = jnp.log(totals[...])

    whole = lambda i, *_: (0, 0)
    mine = lambda i, *_: (i, 0)
    return pl.pallas_call(
        kernel,
        out_shape=(jax.ShapeDtypeStruct((rows, HEAD_DIM), jnp.float32), jax.ShapeDtypeStruct((rows, 1), jnp.float32)),
        grid_spec=pltpu.PrefetchScalarGridSpec(
            num_scalar_prefetch=1, grid=(rows // bq,),
            in_specs=[pl.BlockSpec((bq, HEAD_DIM), mine), pl.BlockSpec((span, HEAD_DIM), whole), pl.BlockSpec((span, HEAD_DIM), whole), pl.BlockSpec((bq, 1), mine)],
            out_specs=(pl.BlockSpec((bq, HEAD_DIM), mine), pl.BlockSpec((bq, 1), mine)),
            scratch_shapes=[pltpu.VMEM((bq, HEAD_DIM), jnp.float32), pltpu.VMEM((bq, 1), jnp.float32)]),
        compiler_params=pltpu.CompilerParams(vmem_limit_bytes=40 * 1024 * 1024),
        cost_estimate=pl.CostEstimate(flops=4 * rows * span * HEAD_DIM, bytes_accessed=4 * span * HEAD_DIM, transcendentals=2 * rows * span),
    )(first, queries, keys, values, low)

def attend_back(queries, keys, values, low, lse, delta, upstream, bq=1024, bk=512):
    rows, span = queries.shape[0], keys.shape[0]
    offset = span - rows
    first = jnp.min(low.reshape(rows // bq, bq), axis=1) // bk

    def kernel(first_ref, q_ref, up_ref, k_ref, kt_ref, v_ref, low_ref, lse_ref, delta_ref, dq_ref, dk_ref, dv_ref):
        block = pl.program_id(0)
        high = offset + block * bq + lax.broadcasted_iota(jnp.int32, (1, bq), 1)

        @pl.when(block == 0)
        def clear():
            dk_ref[...] = jnp.zeros_like(dk_ref)
            dv_ref[...] = jnp.zeros_like(dv_ref)

        dq_ref[...] = jnp.zeros_like(dq_ref)

        def chunk(c, carry):
            at = pl.multiple_of(c * bk, bk)
            here = pl.ds(at, bk)
            ratio = jnp.tanh(across(k_ref[here, :], q_ref[...]) * (1.0 / CAP))
            place = at + lax.broadcasted_iota(jnp.int32, (bk, bq), 0)
            seen = (place >= low_ref[...]) & (place <= high)
            probs = jnp.where(seen, jnp.exp(CAP * ratio - lse_ref[...]), 0.0)
            dv_ref[here, :] += jnp.dot(probs.astype(jnp.bfloat16), up_ref[...], preferred_element_type=jnp.float32)
            dprobs = across(v_ref[here, :], up_ref[...])
            draw = (probs * (dprobs - delta_ref[...]) * (1.0 - ratio * ratio)).astype(jnp.bfloat16)
            dk_ref[here, :] += jnp.dot(draw, q_ref[...], preferred_element_type=jnp.float32)
            dq_ref[...] += jnp.dot(kt_ref[:, here], draw, preferred_element_type=jnp.float32)
            return carry

        lax.fori_loop(first_ref[block], (offset + (block + 1) * bq - 1) // bk + 1, chunk, 0)

    whole = lambda i, *_: (0, 0)
    mine = lambda i, *_: (i, 0)
    across_lanes = lambda i, *_: (0, i)
    return pl.pallas_call(
        kernel,
        out_shape=(jax.ShapeDtypeStruct((HEAD_DIM, rows), jnp.float32), jax.ShapeDtypeStruct((span, HEAD_DIM), jnp.float32), jax.ShapeDtypeStruct((span, HEAD_DIM), jnp.float32)),
        grid_spec=pltpu.PrefetchScalarGridSpec(
            num_scalar_prefetch=1, grid=(rows // bq,),
            in_specs=[pl.BlockSpec((bq, HEAD_DIM), mine), pl.BlockSpec((bq, HEAD_DIM), mine), pl.BlockSpec((span, HEAD_DIM), whole), pl.BlockSpec((HEAD_DIM, span), whole), pl.BlockSpec((span, HEAD_DIM), whole),
                      pl.BlockSpec((1, bq), across_lanes), pl.BlockSpec((1, bq), across_lanes), pl.BlockSpec((1, bq), across_lanes)],
            out_specs=(pl.BlockSpec((HEAD_DIM, bq), across_lanes), pl.BlockSpec((span, HEAD_DIM), whole), pl.BlockSpec((span, HEAD_DIM), whole))),
        compiler_params=pltpu.CompilerParams(vmem_limit_bytes=48 * 1024 * 1024),
        cost_estimate=pl.CostEstimate(flops=10 * rows * span * HEAD_DIM, bytes_accessed=12 * span * HEAD_DIM, transcendentals=2 * rows * span),
    )(first, queries, upstream, keys, keys.T, values, low.T, lse.T, delta.T)


def body(
    tokens,
    cotangent,
    query_weight,
    key_weight,
    value_weight,
    output_weight,
    gate_weight,
    up_weight,
    down_weight,
    query_scale,
    key_scale,
    value_scale,
    output_scale,
    gate_scale,
    up_scale,
    down_scale,
    pre_attention,
    post_attention,
    pre_feedforward,
    post_feedforward,
    positions,
):
    lines = lax.axis_size("line")
    line, pair = lax.axis_index("line"), lax.axis_index("pair")
    row, core = lax.axis_index("row"), lax.axis_index("core")
    tp_index = row * 2 + core
    scale = 1.0 / math.sqrt(HEAD_DIM)
    even = pair == 0
    qcols = query_weight.shape[1] // 2
    kcols = key_weight.shape[1]
    ocols = output_weight.shape[0] // 2
    fcols = gate_weight.shape[1] // 2
    rows = 8 * tokens.shape[0]

    wq, wk, wv, wo, wg, wu, wd = (
        nested_slice(query_weight),
        nested_slice(key_weight),
        nested_slice(value_weight),
        nested_slice(output_weight.T),
        nested_slice(gate_weight),
        nested_slice(up_weight),
        nested_slice(down_weight.T),
    )

    def paired(keep, give):
        return in_order(keep, swapped(give, "pair"), pair)

    def over_line(block):
        return lax.all_gather(block, "line", axis=0, tiled=True)

    def shared_out(shard):
        return paired(half_of(shard, pair), half_of(shard, 1 - pair))

    kv_block = paired(jnp.where(even, wk, wv), jnp.where(even, wv, wk))
    stream = Stream(
        qkvo=jnp.concatenate([shared_out(wq), kv_block, shared_out(wo)], 1),
        gu=jnp.concatenate([shared_out(wg), shared_out(wu)], 1),
        d=shared_out(wd),
    )

    q_at = tp_index * 2 * qcols + pair * qcols
    k_at = tp_index * kcols
    f_at = tp_index * 2 * fcols + pair * fcols
    q_scale = lax.dynamic_slice_in_dim(query_scale, q_at, qcols, 0)
    k_scale = lax.dynamic_slice_in_dim(key_scale, k_at, kcols, 0)
    v_scale = lax.dynamic_slice_in_dim(value_scale, k_at, kcols, 0)
    kv_scale = jnp.where(even, k_scale, v_scale)
    g_scale = lax.dynamic_slice_in_dim(gate_scale, f_at, fcols, 0)
    u_scale = lax.dynamic_slice_in_dim(up_scale, f_at, fcols, 0)

    inputs = tokens.astype(jnp.float32)
    inverse_one = inverse_rms(inputs)
    h_local = (inputs * inverse_one * pre_attention).astype(jnp.bfloat16)
    h_local = stream.stop(h_local, start=[("w_qkvo", ["qkvo"], over_line)])
    h_one = gather8(h_local)
    h_one = stream.stop(h_one, ["w_qkvo"], [("w_gu", ["gu"], over_line)])
    w_qkv = stream.blocks["w_qkvo"][:, : qcols + kcols]
    w_o = stream.blocks["w_qkvo"][:, qcols + kcols :]
    places = in_order(positions, swapped(positions, "pair"), pair)
    cosine, sine = phases(places)

    z_qkv = jnp.dot(h_one, w_qkv, preferred_element_type=jnp.float32)
    z_qkv = to_tokens(z_qkv, pair, row, core)
    zq, zkv = z_qkv[:, :qcols], z_qkv[:, qcols:]
    kv_rows = zkv * kv_scale
    kv_rows = jnp.where(even, rotate(kv_rows, cosine, sine), kv_rows).astype(jnp.bfloat16)
    depth = min((WINDOW - 1 + rows - 1) // rows, lines - 1)
    kept, other = [kv_rows], [swapped(kv_rows, "pair")]
    for step in range(depth):
        kept.append(hop(kept[-1], 1))
        kept[-1], other = stream.stop((kept[-1], other))
        other.append(swapped(kept[-1], "pair"))
    queries = (rotate(zq * q_scale, cosine, sine).astype(jnp.bfloat16) * scale).astype(jnp.bfloat16)
    kept, other = jnp.concatenate(kept[::-1], 0), jnp.concatenate(other[::-1], 0)
    keys = jnp.where(even, kept, other)
    values = jnp.where(even, other, kept)
    low = depth * rows + jnp.arange(rows, dtype=jnp.int32) - jnp.minimum(places, WINDOW - 1)
    low = low[:, None]
    attended_wide, lse = attend(queries, keys, values, low)
    attended = attended_wide.astype(jnp.bfloat16)
    attended = from_tokens(attended, pair, row, core)
    def by_core(left, right):
        half_rows = left.shape[0] // 2
        mine, others = left[:half_rows], left[half_rows:]
        others = jnp.einsum("tc,dc->td", others, right, preferred_element_type=jnp.float32)
        mine, others = tie(mine, others.astype(jnp.bfloat16))
        mine = jnp.einsum("tc,dc->td", mine, right, preferred_element_type=jnp.float32)
        return mine, others

    zo = scatter8(by_core(attended, w_o))
    zo = stream.stop(zo, ["w_gu"], [("w_d", ["d"], over_line)])
    w_gu, w_d = stream.blocks["w_gu"], stream.blocks["w_d"]
    after_attention = zo * output_scale
    inverse_two = inverse_rms(after_attention)
    middle = inputs + after_attention * inverse_two * post_attention
    inverse_three = inverse_rms(middle)
    h_two = gather8((middle * inverse_three * pre_feedforward).astype(jnp.bfloat16))
    z_gu = jnp.dot(h_two, w_gu, preferred_element_type=jnp.float32)
    zg, zu = z_gu[:, :fcols], z_gu[:, fcols:]
    gate_in = zg * g_scale
    up_in = zu * u_scale
    hidden = (jax.nn.gelu(gate_in, approximate=True) * up_in).astype(jnp.bfloat16)
    zd = scatter8(by_core(hidden, w_d))
    fed = zd * down_scale
    inverse_four = inverse_rms(fed)
    block_out = middle + fed * inverse_four * post_feedforward

    upstream = cotangent.astype(jnp.float32)
    dfed, gain_four_grad = norm_back(fed, inverse_four, post_feedforward, upstream)
    down_scale_sum = jnp.sum(dfed * zd, axis=0)
    def over_line_sum(term):
        return lax.psum_scatter(term, "line", scatter_dimension=0, tiled=True)

    def rows_for(part, place):
        size = part.shape[0] // 2
        return lax.dynamic_slice_in_dim(part, place * size, size, 0).astype(jnp.float32)

    def swap_of(name):
        def route(part):
            return swapped(rows_for(part, 1 - pair).astype(jnp.bfloat16), "pair")

        return (name + "_got", [name + "_sum"], route)

    def shared(name):
        return rows_for(stream.blocks[name + "_sum"], pair), stream.blocks[name + "_got"].astype(
            jnp.float32
        )

    def side_by_side(keep, got, first):
        return jnp.where(
            first, jnp.concatenate([keep, got], 1), jnp.concatenate([got, keep], 1)
        )

    def term_of(left, right):
        return jnp.einsum("td,tf->df", left, right, preferred_element_type=jnp.float32).astype(
            jnp.bfloat16
        )

    def down_term(four, other):
        mine = jnp.einsum("td,tf->df", four, hidden[: rows // 2], preferred_element_type=jnp.float32)
        mine, other = tie(mine, other)
        others = jnp.einsum(
            "td,tf->df", other, hidden[rows // 2 :], preferred_element_type=jnp.float32
        )
        stream.blocks["D"] = (mine + others).astype(jnp.bfloat16)
        return stream.stop((four, other), ["D"], [("D_sum", ["D"], over_line_sum)])

    dzd = gather8((dfed * down_scale).astype(jnp.bfloat16), down_term)
    dhidden = jnp.dot(dzd, w_d, preferred_element_type=jnp.float32)
    unused, pull = jax.vjp(
        lambda left, right: jax.nn.gelu(left, approximate=True) * right, gate_in, up_in
    )
    dgate, dup = pull(dhidden)
    gate_scale_sum = jnp.sum(dgate * zg, axis=0)
    up_scale_sum = jnp.sum(dup * zu, axis=0)
    dzg = (dgate * g_scale).astype(jnp.bfloat16)
    dzu = (dup * u_scale).astype(jnp.bfloat16)
    dh_mid = (
        jnp.einsum("tf,df->td", dzg, w_gu[:, :fcols], preferred_element_type=jnp.float32)
        + jnp.einsum("tf,df->td", dzu, w_gu[:, fcols:], preferred_element_type=jnp.float32)
    )
    stream.blocks["GU"] = jnp.concatenate([term_of(h_two, dzg), term_of(h_two, dzu)], 1)
    dh_mid = scatter8(
        jnp.split(dh_mid, 2),
        lambda work: stream.stop(
            work, ["GU", "D_sum"], [("GU_sum", ["GU"], over_line_sum), swap_of("D")]
        ),
    )
    dmid_norm, gain_three_grad = norm_back(middle, inverse_three, pre_feedforward, dh_mid)
    dmiddle = upstream + dmid_norm
    dafter, gain_two_grad = norm_back(after_attention, inverse_two, post_attention, dmiddle)
    output_scale_sum = jnp.sum(dafter * zo, axis=0)
    early = (
        output_scale_sum,
        spread(gate_scale_sum, gate_scale.shape[0], f_at),
        spread(up_scale_sum, up_scale.shape[0], f_at),
        down_scale_sum,
        gain_two_grad,
        gain_three_grad,
        gain_four_grad,
    )
    dzo = gather8((dafter * output_scale).astype(jnp.bfloat16))
    o_term = term_of(dzo, attended)
    dattended = jnp.dot(dzo, w_o, preferred_element_type=jnp.float32).astype(jnp.bfloat16)
    dattended = to_tokens(dattended, pair, row, core)
    delta = jnp.sum(dattended.astype(jnp.float32) * attended_wide, axis=-1, keepdims=True)
    dqueries, dkeys, dvalues = attend_back(queries, keys, values, low, lse, delta, dattended)
    dqueries = dqueries.T * scale

    keep = jnp.where(even, dkeys, dvalues)
    give = jnp.where(even, dvalues, dkeys).astype(jnp.bfloat16)
    got = [swapped(give[i * rows : (i + 1) * rows], "pair") for i in range(depth + 1)]
    equery = rotate(dqueries, cosine, -sine)
    query_scale_sum = jnp.sum(equery * zq, axis=0)
    dzq = from_tokens((equery * q_scale).astype(jnp.bfloat16), pair, row, core)
    q_term = term_of(h_one, dzq)
    got[0], q_term, o_term = stream.stop((got[0], q_term, o_term))
    dkv = None
    for i in range(depth + 1):
        block = keep[i * rows : (i + 1) * rows] + got[i].astype(jnp.float32)
        if dkv is not None:
            block = block + hop(dkv.astype(jnp.bfloat16), -1).astype(jnp.float32)
        dkv = block
    dkv = stream.stop(dkv, ["GU_sum"], [swap_of("GU")])
    ekv = jnp.where(even, rotate(dkv, cosine, -sine), dkv)
    kv_scale_sum = jnp.sum(ekv * zkv, axis=0)
    dzkv = from_tokens((ekv * kv_scale).astype(jnp.bfloat16), pair, row, core)
    kv_term = term_of(h_one, dzkv)
    stream.blocks["QKVO"] = jnp.concatenate([q_term, kv_term, o_term], 1)
    dzkv = stream.stop(
        dzkv, ["QKVO", "D_got"], [("QKVO_sum", ["QKVO"], over_line_sum)]
    )
    dh_one = jnp.einsum(
        "tc,dc->td",
        jnp.concatenate([dzq, dzkv], 1),
        w_qkv,
        preferred_element_type=jnp.float32,
    )
    gain_one_part = jnp.sum(dh_one * h_one.astype(jnp.float32), axis=0) / pre_attention
    late = (
        spread(query_scale_sum, query_scale.shape[0], q_at),
        spread(jnp.where(even, kv_scale_sum, 0.0), key_scale.shape[0], k_at),
        spread(jnp.where(even, 0.0, kv_scale_sum), value_scale.shape[0], k_at),
        gain_one_part,
    )
    sums = jnp.concatenate(early + late)
    dh_one, sums = stream.stop((dh_one, sums), ["GU_got"])
    for axis in ["core", "row", "pair"] + [1 << i for i in range(lines.bit_length() - 1)]:
        sums = sums + exchanged(sums, axis)
    stream.blocks["sums"] = sums
    dh_local = scatter8_last(
        jnp.split(dh_one, 2),
        lambda work: stream.stop(work, ["QKVO_sum", "sums"], [swap_of("QKVO")]),
    )
    sums = stream.blocks["sums"]
    dinput_norm, unused = norm_back(inputs, inverse_one, pre_attention, dh_local)
    token_grad = dmiddle + dinput_norm
    d_keep, d_got = shared("D")
    down_grad = side_by_side(d_keep, d_got, even).T
    gu_keep, gu_got = shared("GU")
    gate_grad = side_by_side(gu_keep[:, :fcols], gu_got[:, :fcols], even)
    up_grad = side_by_side(gu_keep[:, fcols:], gu_got[:, fcols:], even)
    keep, got = shared("QKVO")
    query_grad = side_by_side(keep[:, :qcols], got[:, :qcols], even)
    kv_keep, kv_got = keep[:, qcols : qcols + kcols], got[:, qcols : qcols + kcols]
    key_grad = jnp.where(even, kv_keep, kv_got)
    value_grad = jnp.where(even, kv_got, kv_keep)
    output_grad = side_by_side(keep[:, qcols + kcols :], got[:, qcols + kcols :], even).T

    cuts, at = [], 0
    for vector in early + late:
        cuts.append(sums[at : at + vector.shape[0]])
        at += vector.shape[0]
    o_sum, g_sum, u_sum, d_sum, two_sum, three_sum, four_sum, q_sum, k_sum, v_sum, one_sum = cuts
    return (
        block_out,
        token_grad,
        query_grad,
        key_grad,
        value_grad,
        output_grad,
        gate_grad,
        up_grad,
        down_grad,
        q_sum,
        k_sum,
        v_sum,
        o_sum,
        g_sum,
        u_sum,
        d_sum,
        one_sum,
        two_sum,
        three_sum,
        four_sum,
    )


def solution(mesh):
    seq_count, tp_count = mesh.shape["seq"], mesh.shape["tp"]
    wide = Mesh(mesh.devices.reshape(seq_count // 2, 2, tp_count // 2, 2), EVERY)
    seq, tp = ("line", "pair"), ("row", "core")
    return jax.shard_map(
        body,
        mesh=wide,
        in_specs=(P(EVERY, None),) * 2
        + (P(seq, tp),) * 3
        + (P(tp, seq),)
        + (P(seq, tp),) * 2
        + (P(tp, seq),)
        + (P(),) * 11
        + (P(seq),),
        out_specs=(P(EVERY, None),) * 2
        + (P(seq, tp),) * 3
        + (P(tp, seq),)
        + (P(seq, tp),) * 2
        + (P(tp, seq),)
        + (P(),) * 11,
        check_vma=False,
    )
```

```python
import math

import jax
import jax.numpy as jnp
from jax import lax
from jax.experimental import pallas as pl
from jax.experimental.pallas import tpu as pltpu
from jax.sharding import Mesh
from jax.sharding import PartitionSpec as P

HEAD_DIM = 256
WINDOW = 4096
CAP = 50
EPSILON = 1e-06

EVERY = ("line", "pair", "row", "core")
SWAP = [(0, 1), (1, 0)]


def swapped(block, axis):
    return lax.ppermute(block, axis, SWAP)


def hop(block, distance, first):
    count = lax.axis_size("line")
    route = [(i, i + distance) for i in range(first, count) if 0 <= i + distance < count]
    return lax.ppermute(block, "line", route)


def put_together(sources, moves, shape):
    count = len(moves())
    if any(size % 16 for _, _, size, _, _ in moves()):
        out = jnp.zeros(shape, sources[0].dtype)
        for source, start, size, row, column in moves():
            piece = lax.dynamic_slice_in_dim(sources[source], start, size, 0)
            out = lax.dynamic_update_slice(out, piece, (row, column))
        return out

    def rows_at(row, size):
        return pl.ds(row if isinstance(row, int) else pl.multiple_of(row, 16), size)

    def kernel(*refs):
        out, sems = refs[len(sources)], refs[len(sources) + 1]
        copies = []
        for i, (source, start, size, row, column) in enumerate(moves()):
            piece = refs[source].at[rows_at(start, size)]
            target = out.at[rows_at(row, size), pl.ds(column, sources[source].shape[1])]
            copies.append(pltpu.make_async_copy(piece, target, sems.at[i]))
        for copy in copies:
            copy.start()
        for copy in copies:
            copy.wait()

    size = 2 * math.prod(shape) * sources[0].dtype.itemsize
    return pl.pallas_call(
        kernel,
        out_shape=jax.ShapeDtypeStruct(shape, sources[0].dtype),
        in_specs=[pl.BlockSpec(memory_space=pl.ANY)] * len(sources),
        out_specs=pl.BlockSpec(memory_space=pltpu.VMEM),
        scratch_shapes=[pltpu.SemaphoreType.DMA((count,))],
        compiler_params=pltpu.CompilerParams(vmem_limit_bytes=size // 2 + 4 * 1024 * 1024),
        cost_estimate=pl.CostEstimate(flops=0, bytes_accessed=size, transcendentals=0),
    )(*sources)


def tie(*values):
    return lax.optimization_barrier(values)


class Stream:
    def __init__(self, **blocks):
        self.blocks = blocks

    def stop(self, work, finish=(), start=()):
        here = [self.blocks[name] for name in finish]
        sources = [[self.blocks[name] for name in names] for _, names, _ in start]
        work, here, sources = tie(work, here, sources)
        self.blocks.update(zip(finish, here))
        for (name, _, route), blocks in zip(start, sources):
            self.blocks[name] = route(*blocks)
        return work


def nested_slice(codes):
    values = codes.astype(jnp.float32)
    return (jnp.clip(jnp.floor((values + 8.0) / 16.0), -8.0, 7.0) * 16.0).astype(jnp.bfloat16)


def inverse_rms(values):
    return lax.rsqrt(jnp.mean(values * values, axis=-1, keepdims=True) + EPSILON)


def norm_back(source, inverse, gain, upstream):
    scaled = upstream * gain
    inner = jnp.mean(scaled * source, axis=-1, keepdims=True)
    back = inverse * scaled - source * (inverse * inverse * inverse) * inner
    return (back, jnp.sum(upstream * source * inverse, axis=0))


def phases(positions):
    freqs = 10000.0 ** (-2.0 * jnp.arange(HEAD_DIM // 2, dtype=jnp.float32) / HEAD_DIM)
    angle = positions.astype(jnp.float32)[:, None] * freqs[None, :]
    return (jnp.cos(angle), jnp.sin(angle))


def rotate(values, cosine, sine):
    half = values.shape[-1] // 2
    first = values[..., :half]
    second = values[..., half:]
    return jnp.concatenate([first * cosine - second * sine, second * cosine + first * sine], -1)


def spread(piece, total, offset):
    return lax.dynamic_update_slice_in_dim(jnp.zeros((total,), jnp.float32), piece, offset, 0)


def in_order(mine, other, place):
    return lax.dynamic_slice_in_dim(
        jnp.concatenate([other, mine, other], 0), (1 - place) * mine.shape[0], 2 * mine.shape[0], 0
    )


def half_of(block, place):
    size = block.shape[1] // 2
    return lax.dynamic_slice_in_dim(block, place * size, size, 1)


def unstopped(work):
    return work


def gather8(block, with_halves=None):
    size, width = block.shape
    cut = size // 2
    left, right = block[:cut], block[cut:]
    left_p, right_r = swapped(left, "pair"), swapped(right, "row")
    left_r, right_p = swapped(left, "row"), swapped(right, "pair")
    left_pr, right_pr = swapped(left_p, "row"), swapped(right_r, "pair")
    halves = [left, right, left_r, right_r, left_p, right_p, left_pr, right_pr]
    four = put_together(
        halves, lambda: [(i, 0, cut, i * cut, 0) for i in range(8)], (4 * size, width)
    )
    other = swapped(four, "core")
    if with_halves is not None:
        four, other = with_halves(four, other)
    return put_together(
        [four, other],
        lambda: [(i, 0, 4 * size, i * 4 * size, 0) for i in range(2)],
        (8 * size, width),
    )


def summed(keep, got):
    return keep + got.astype(jnp.float32)


def sent(piece, axis):
    return swapped(piece.astype(jnp.bfloat16), axis)


def scatter8(terms, stop=unstopped):
    mine, others = terms
    size, width = mine.shape[0] // 4, mine.shape[1]
    mine, got = tie(mine, sent(others, "core"))
    four = stop(summed(mine, got)).reshape(2, 2, size, width)
    left, right = four[..., : width // 2], four[..., width // 2 :]
    left = summed(left[0], sent(left[1], "pair"))
    right = summed(right[:, 0], sent(right[:, 1], "row"))
    left = summed(left[0], sent(left[1], "row"))
    right = summed(right[0], sent(right[1], "pair"))
    return jnp.concatenate([left, right], 1)


def scatter8_last(terms, stop):
    mine, others = terms
    size, width = mine.shape[0] // 4, mine.shape[1]
    four = summed(mine, sent(others, "core")).reshape(2, 2, size, width)
    two = stop(summed(four[0], sent(four[1], "pair")))
    return summed(two[0], sent(two[1], "row"))


def blocks(rows, places):
    size = rows.shape[0] // len(places)
    return jnp.concatenate(
        [lax.dynamic_slice_in_dim(rows, place * size, size, 0) for place in places], 0
    )


def to_tokens(rows, pair, row, core):
    places = [
        ((c ^ core) * 4 + (p ^ pair) * 2 + (r ^ row))
        for p in range(2)
        for r in range(2)
        for c in range(2)
    ]
    return blocks(rows, places)


def from_tokens(rows, pair, row, core):
    places = [
        ((p ^ pair) * 4 + (r ^ row) * 2 + (c ^ core))
        for c in range(2)
        for p in range(2)
        for r in range(2)
    ]
    return blocks(rows, places)


def exchanged(vector, axis):
    if isinstance(axis, str):
        return swapped(vector, axis)
    count = lax.axis_size("line")
    return lax.ppermute(vector, "line", [(i, i ^ axis) for i in range(count)])


def across(left, right):
    return lax.dot_general(left, right, (((1,), (1,)), ((), ())), preferred_element_type=jnp.float32)

def attend(queries, keys, values, low, bq=512, bk=1024):
    rows, span = queries.shape[0], keys.shape[0]
    offset = span - rows
    first = jnp.min(low.reshape(rows // bq, bq), axis=1) // bk

    def kernel(first_ref, q_ref, k_ref, v_ref, low_ref, o_ref, lse_ref, sums, totals):
        block = pl.program_id(0)
        high = offset + block * bq + lax.broadcasted_iota(jnp.int32, (bq, 1), 0)
        sums[...] = jnp.zeros_like(sums)
        totals[...] = jnp.zeros_like(totals)

        def chunk(c, carry):
            at = pl.multiple_of(c * bk, bk)
            raw = across(q_ref[...], k_ref[pl.ds(at, bk), :])
            place = at + lax.broadcasted_iota(jnp.int32, (bq, bk), 1)
            seen = (place >= low_ref[...]) & (place <= high)
            expo = jnp.where(seen, jnp.exp(CAP * jnp.tanh(raw * (1.0 / CAP))), 0.0)
            totals[...] += jnp.sum(expo, axis=-1, keepdims=True)
            sums[...] += jnp.dot(expo.astype(jnp.bfloat16), v_ref[pl.ds(at, bk), :], preferred_element_type=jnp.float32)
            return carry

        lax.fori_loop(first_ref[block], (offset + (block + 1) * bq - 1) // bk + 1, chunk, 0)
        o_ref[...] = sums[...] / totals[...]
        lse_ref[...] = jnp.log(totals[...])

    whole = lambda i, *_: (0, 0)
    mine = lambda i, *_: (i, 0)
    return pl.pallas_call(
        kernel,
        out_shape=(jax.ShapeDtypeStruct((rows, HEAD_DIM), jnp.float32), jax.ShapeDtypeStruct((rows, 1), jnp.float32)),
        grid_spec=pltpu.PrefetchScalarGridSpec(
            num_scalar_prefetch=1, grid=(rows // bq,),
            in_specs=[pl.BlockSpec((bq, HEAD_DIM), mine), pl.BlockSpec((span, HEAD_DIM), whole), pl.BlockSpec((span, HEAD_DIM), whole), pl.BlockSpec((bq, 1), mine)],
            out_specs=(pl.BlockSpec((bq, HEAD_DIM), mine), pl.BlockSpec((bq, 1), mine)),
            scratch_shapes=[pltpu.VMEM((bq, HEAD_DIM), jnp.float32), pltpu.VMEM((bq, 1), jnp.float32)]),
        compiler_params=pltpu.CompilerParams(vmem_limit_bytes=40 * 1024 * 1024),
        cost_estimate=pl.CostEstimate(flops=4 * rows * span * HEAD_DIM, bytes_accessed=4 * span * HEAD_DIM, transcendentals=2 * rows * span),
    )(first, queries, keys, values, low)

def attend_back(queries, keys, values, low, lse, delta, upstream, bq=1024, bk=512):
    rows, span = queries.shape[0], keys.shape[0]
    offset = span - rows
    first = jnp.min(low.reshape(rows // bq, bq), axis=1) // bk

    def kernel(first_ref, q_ref, up_ref, k_ref, kt_ref, v_ref, low_ref, lse_ref, delta_ref, dq_ref, dk_ref, dv_ref):
        block = pl.program_id(0)
        high = offset + block * bq + lax.broadcasted_iota(jnp.int32, (1, bq), 1)

        @pl.when(block == 0)
        def clear():
            dk_ref[...] = jnp.zeros_like(dk_ref)
            dv_ref[...] = jnp.zeros_like(dv_ref)

        dq_ref[...] = jnp.zeros_like(dq_ref)

        def chunk(c, carry):
            at = pl.multiple_of(c * bk, bk)
            here = pl.ds(at, bk)
            ratio = jnp.tanh(across(k_ref[here, :], q_ref[...]) * (1.0 / CAP))
            place = at + lax.broadcasted_iota(jnp.int32, (bk, bq), 0)
            seen = (place >= low_ref[...]) & (place <= high)
            probs = jnp.where(seen, jnp.exp(CAP * ratio - lse_ref[...]), 0.0)
            dv_ref[here, :] += jnp.dot(probs.astype(jnp.bfloat16), up_ref[...], preferred_element_type=jnp.float32)
            dprobs = across(v_ref[here, :], up_ref[...])
            draw = (probs * (dprobs - delta_ref[...]) * (1.0 - ratio * ratio)).astype(jnp.bfloat16)
            dk_ref[here, :] += jnp.dot(draw, q_ref[...], preferred_element_type=jnp.float32)
            dq_ref[...] += jnp.dot(kt_ref[:, here], draw, preferred_element_type=jnp.float32)
            return carry

        lax.fori_loop(first_ref[block], (offset + (block + 1) * bq - 1) // bk + 1, chunk, 0)

    whole = lambda i, *_: (0, 0)
    mine = lambda i, *_: (i, 0)
    across_lanes = lambda i, *_: (0, i)
    return pl.pallas_call(
        kernel,
        out_shape=(jax.ShapeDtypeStruct((HEAD_DIM, rows), jnp.float32), jax.ShapeDtypeStruct((span, HEAD_DIM), jnp.float32), jax.ShapeDtypeStruct((span, HEAD_DIM), jnp.float32)),
        grid_spec=pltpu.PrefetchScalarGridSpec(
            num_scalar_prefetch=1, grid=(rows // bq,),
            in_specs=[pl.BlockSpec((bq, HEAD_DIM), mine), pl.BlockSpec((bq, HEAD_DIM), mine), pl.BlockSpec((span, HEAD_DIM), whole), pl.BlockSpec((HEAD_DIM, span), whole), pl.BlockSpec((span, HEAD_DIM), whole),
                      pl.BlockSpec((1, bq), across_lanes), pl.BlockSpec((1, bq), across_lanes), pl.BlockSpec((1, bq), across_lanes)],
            out_specs=(pl.BlockSpec((HEAD_DIM, bq), across_lanes), pl.BlockSpec((span, HEAD_DIM), whole), pl.BlockSpec((span, HEAD_DIM), whole))),
        compiler_params=pltpu.CompilerParams(vmem_limit_bytes=48 * 1024 * 1024),
        cost_estimate=pl.CostEstimate(flops=10 * rows * span * HEAD_DIM, bytes_accessed=12 * span * HEAD_DIM, transcendentals=2 * rows * span),
    )(first, queries, upstream, keys, keys.T, values, low.T, lse.T, delta.T)


def body(
    tokens,
    cotangent,
    query_weight,
    key_weight,
    value_weight,
    output_weight,
    gate_weight,
    up_weight,
    down_weight,
    query_scale,
    key_scale,
    value_scale,
    output_scale,
    gate_scale,
    up_scale,
    down_scale,
    pre_attention,
    post_attention,
    pre_feedforward,
    post_feedforward,
    positions,
):
    lines = lax.axis_size("line")
    line, pair = lax.axis_index("line"), lax.axis_index("pair")
    row, core = lax.axis_index("row"), lax.axis_index("core")
    tp_index = row * 2 + core
    scale = 1.0 / math.sqrt(HEAD_DIM)
    even = pair == 0
    qcols = query_weight.shape[1] // 2
    kcols = key_weight.shape[1]
    ocols = output_weight.shape[0] // 2
    fcols = gate_weight.shape[1] // 2
    rows = 8 * tokens.shape[0]

    wq, wk, wv, wo, wg, wu, wd = (
        nested_slice(query_weight),
        nested_slice(key_weight),
        nested_slice(value_weight),
        nested_slice(output_weight.T),
        nested_slice(gate_weight),
        nested_slice(up_weight),
        nested_slice(down_weight.T),
    )

    def paired(keep, give):
        return in_order(keep, swapped(give, "pair"), pair)

    def over_line(block):
        return lax.all_gather(block, "line", axis=0, tiled=True)

    def shared_out(shard):
        return paired(half_of(shard, pair), half_of(shard, 1 - pair))

    kv_block = paired(jnp.where(even, wk, wv), jnp.where(even, wv, wk))
    stream = Stream(
        qkvo=jnp.concatenate([shared_out(wq), kv_block, shared_out(wo)], 1),
        gu=jnp.concatenate([shared_out(wg), shared_out(wu)], 1),
        d=shared_out(wd),
    )

    q_at = tp_index * 2 * qcols + pair * qcols
    k_at = tp_index * kcols
    f_at = tp_index * 2 * fcols + pair * fcols
    q_scale = lax.dynamic_slice_in_dim(query_scale, q_at, qcols, 0)
    k_scale = lax.dynamic_slice_in_dim(key_scale, k_at, kcols, 0)
    v_scale = lax.dynamic_slice_in_dim(value_scale, k_at, kcols, 0)
    kv_scale = jnp.where(even, k_scale, v_scale)
    g_scale = lax.dynamic_slice_in_dim(gate_scale, f_at, fcols, 0)
    u_scale = lax.dynamic_slice_in_dim(up_scale, f_at, fcols, 0)

    inputs = tokens.astype(jnp.float32)
    inverse_one = inverse_rms(inputs)
    h_local = (inputs * inverse_one * pre_attention).astype(jnp.bfloat16)
    h_local = stream.stop(h_local, start=[("w_qkvo", ["qkvo"], over_line)])
    h_one = gather8(h_local)
    h_one = stream.stop(h_one, ["w_qkvo"], [("w_gu", ["gu"], over_line)])
    w_qkv = stream.blocks["w_qkvo"][:, : qcols + kcols]
    w_o = stream.blocks["w_qkvo"][:, qcols + kcols :]
    places = in_order(positions, swapped(positions, "pair"), pair)
    cosine, sine = phases(places)

    z_qkv = jnp.dot(h_one, w_qkv, preferred_element_type=jnp.float32)
    z_qkv = to_tokens(z_qkv, pair, row, core)
    zq, zkv = z_qkv[:, :qcols], z_qkv[:, qcols:]
    kv_rows = zkv * kv_scale
    kv_rows = jnp.where(even, rotate(kv_rows, cosine, sine), kv_rows).astype(jnp.bfloat16)
    depth = min((WINDOW - 1 + rows - 1) // rows, lines - 1)
    kept, other = [kv_rows], [swapped(kv_rows, "pair")]
    for step in range(depth):
        kept.append(hop(kept[-1], 1, step))
        kept[-1], other = stream.stop((kept[-1], other))
        other.append(swapped(kept[-1], "pair"))
    queries = (rotate(zq * q_scale, cosine, sine).astype(jnp.bfloat16) * scale).astype(jnp.bfloat16)
    kept, other = jnp.concatenate(kept[::-1], 0), jnp.concatenate(other[::-1], 0)
    keys = jnp.where(even, kept, other)
    values = jnp.where(even, other, kept)
    low = depth * rows + jnp.arange(rows, dtype=jnp.int32) - jnp.minimum(places, WINDOW - 1)
    low = low[:, None]
    attended_wide, lse = attend(queries, keys, values, low)
    attended = attended_wide.astype(jnp.bfloat16)
    attended = from_tokens(attended, pair, row, core)
    def by_core(left, right):
        half_rows = left.shape[0] // 2
        mine, others = left[:half_rows], left[half_rows:]
        others = jnp.einsum("tc,dc->td", others, right, preferred_element_type=jnp.float32)
        mine, others = tie(mine, others.astype(jnp.bfloat16))
        mine = jnp.einsum("tc,dc->td", mine, right, preferred_element_type=jnp.float32)
        return mine, others

    zo = scatter8(by_core(attended, w_o))
    zo = stream.stop(zo, ["w_gu"], [("w_d", ["d"], over_line)])
    w_gu, w_d = stream.blocks["w_gu"], stream.blocks["w_d"]
    after_attention = zo * output_scale
    inverse_two = inverse_rms(after_attention)
    middle = inputs + after_attention * inverse_two * post_attention
    inverse_three = inverse_rms(middle)
    h_two = gather8((middle * inverse_three * pre_feedforward).astype(jnp.bfloat16))
    z_gu = jnp.dot(h_two, w_gu, preferred_element_type=jnp.float32)
    zg, zu = z_gu[:, :fcols], z_gu[:, fcols:]
    gate_in = zg * g_scale
    up_in = zu * u_scale
    hidden = (jax.nn.gelu(gate_in, approximate=True) * up_in).astype(jnp.bfloat16)
    zd = scatter8(by_core(hidden, w_d))
    fed = zd * down_scale
    inverse_four = inverse_rms(fed)
    block_out = middle + fed * inverse_four * post_feedforward

    upstream = cotangent.astype(jnp.float32)
    dfed, gain_four_grad = norm_back(fed, inverse_four, post_feedforward, upstream)
    down_scale_sum = jnp.sum(dfed * zd, axis=0)
    def over_line_sum(term):
        return lax.psum_scatter(term, "line", scatter_dimension=0, tiled=True)

    def rows_for(part, place):
        size = part.shape[0] // 2
        return lax.dynamic_slice_in_dim(part, place * size, size, 0).astype(jnp.float32)

    def swap_of(name):
        def route(part):
            return swapped(rows_for(part, 1 - pair).astype(jnp.bfloat16), "pair")

        return (name + "_got", [name + "_sum"], route)

    def shared(name):
        return rows_for(stream.blocks[name + "_sum"], pair), stream.blocks[name + "_got"].astype(
            jnp.float32
        )

    def side_by_side(keep, got, first):
        return jnp.where(
            first, jnp.concatenate([keep, got], 1), jnp.concatenate([got, keep], 1)
        )

    def term_of(left, right):
        return jnp.einsum("td,tf->df", left, right, preferred_element_type=jnp.float32).astype(
            jnp.bfloat16
        )

    def down_term(four, other):
        mine = jnp.einsum("td,tf->df", four, hidden[: rows // 2], preferred_element_type=jnp.float32)
        mine, other = tie(mine, other)
        others = jnp.einsum(
            "td,tf->df", other, hidden[rows // 2 :], preferred_element_type=jnp.float32
        )
        stream.blocks["D"] = (mine + others).astype(jnp.bfloat16)
        return stream.stop((four, other), ["D"], [("D_sum", ["D"], over_line_sum)])

    dzd = gather8((dfed * down_scale).astype(jnp.bfloat16), down_term)
    dhidden = jnp.dot(dzd, w_d, preferred_element_type=jnp.float32)
    unused, pull = jax.vjp(
        lambda left, right: jax.nn.gelu(left, approximate=True) * right, gate_in, up_in
    )
    dgate, dup = pull(dhidden)
    gate_scale_sum = jnp.sum(dgate * zg, axis=0)
    up_scale_sum = jnp.sum(dup * zu, axis=0)
    dzg = (dgate * g_scale).astype(jnp.bfloat16)
    dzu = (dup * u_scale).astype(jnp.bfloat16)
    dh_mid = (
        jnp.einsum("tf,df->td", dzg, w_gu[:, :fcols], preferred_element_type=jnp.float32)
        + jnp.einsum("tf,df->td", dzu, w_gu[:, fcols:], preferred_element_type=jnp.float32)
    )
    stream.blocks["GU"] = jnp.concatenate([term_of(h_two, dzg), term_of(h_two, dzu)], 1)
    dh_mid = scatter8(
        jnp.split(dh_mid, 2),
        lambda work: stream.stop(
            work, ["GU", "D_sum"], [("GU_sum", ["GU"], over_line_sum), swap_of("D")]
        ),
    )
    dmid_norm, gain_three_grad = norm_back(middle, inverse_three, pre_feedforward, dh_mid)
    dmiddle = upstream + dmid_norm
    dafter, gain_two_grad = norm_back(after_attention, inverse_two, post_attention, dmiddle)
    output_scale_sum = jnp.sum(dafter * zo, axis=0)
    early = (
        output_scale_sum,
        spread(gate_scale_sum, gate_scale.shape[0], f_at),
        spread(up_scale_sum, up_scale.shape[0], f_at),
        down_scale_sum,
        gain_two_grad,
        gain_three_grad,
        gain_four_grad,
    )
    dzo = gather8((dafter * output_scale).astype(jnp.bfloat16))
    o_term = term_of(dzo, attended)
    dattended = jnp.dot(dzo, w_o, preferred_element_type=jnp.float32).astype(jnp.bfloat16)
    dattended = to_tokens(dattended, pair, row, core)
    delta = jnp.sum(dattended.astype(jnp.float32) * attended_wide, axis=-1, keepdims=True)
    dqueries, dkeys, dvalues = attend_back(queries, keys, values, low, lse, delta, dattended)
    dqueries = dqueries.T * scale

    keep = jnp.where(even, dkeys, dvalues)
    give = jnp.where(even, dvalues, dkeys).astype(jnp.bfloat16)
    got = [swapped(give[i * rows : (i + 1) * rows], "pair") for i in range(depth + 1)]
    equery = rotate(dqueries, cosine, -sine)
    query_scale_sum = jnp.sum(equery * zq, axis=0)
    dzq = from_tokens((equery * q_scale).astype(jnp.bfloat16), pair, row, core)
    q_term = term_of(h_one, dzq)
    got[0], q_term, o_term = stream.stop((got[0], q_term, o_term))
    dkv = None
    for i in range(depth + 1):
        block = keep[i * rows : (i + 1) * rows] + got[i].astype(jnp.float32)
        if dkv is not None:
            block = block + hop(dkv.astype(jnp.bfloat16), -1, depth + 1 - i).astype(jnp.float32)
        dkv = block
    dkv = stream.stop(dkv, ["GU_sum"], [swap_of("GU")])
    ekv = jnp.where(even, rotate(dkv, cosine, -sine), dkv)
    kv_scale_sum = jnp.sum(ekv * zkv, axis=0)
    dzkv = from_tokens((ekv * kv_scale).astype(jnp.bfloat16), pair, row, core)
    kv_term = term_of(h_one, dzkv)
    stream.blocks["QKVO"] = jnp.concatenate([q_term, kv_term, o_term], 1)
    dzkv = stream.stop(
        dzkv, ["QKVO", "D_got"], [("QKVO_sum", ["QKVO"], over_line_sum)]
    )
    dh_one = jnp.einsum(
        "tc,dc->td",
        jnp.concatenate([dzq, dzkv], 1),
        w_qkv,
        preferred_element_type=jnp.float32,
    )
    gain_one_part = jnp.sum(dh_one * h_one.astype(jnp.float32), axis=0) / pre_attention
    late = (
        spread(query_scale_sum, query_scale.shape[0], q_at),
        spread(jnp.where(even, kv_scale_sum, 0.0), key_scale.shape[0], k_at),
        spread(jnp.where(even, 0.0, kv_scale_sum), value_scale.shape[0], k_at),
        gain_one_part,
    )
    sums = jnp.concatenate(early + late)
    dh_one, sums = stream.stop((dh_one, sums), ["GU_got"])
    for axis in ["core", "row", "pair"] + [1 << i for i in range(lines.bit_length() - 1)]:
        sums = sums + exchanged(sums, axis)
    stream.blocks["sums"] = sums
    dh_local = scatter8_last(
        jnp.split(dh_one, 2),
        lambda work: stream.stop(work, ["QKVO_sum", "sums"], [swap_of("QKVO")]),
    )
    sums = stream.blocks["sums"]
    dinput_norm, unused = norm_back(inputs, inverse_one, pre_attention, dh_local)
    token_grad = dmiddle + dinput_norm
    d_keep, d_got = shared("D")
    down_grad = side_by_side(d_keep, d_got, even).T
    gu_keep, gu_got = shared("GU")
    gate_grad = side_by_side(gu_keep[:, :fcols], gu_got[:, :fcols], even)
    up_grad = side_by_side(gu_keep[:, fcols:], gu_got[:, fcols:], even)
    keep, got = shared("QKVO")
    query_grad = side_by_side(keep[:, :qcols], got[:, :qcols], even)
    kv_keep, kv_got = keep[:, qcols : qcols + kcols], got[:, qcols : qcols + kcols]
    key_grad = jnp.where(even, kv_keep, kv_got)
    value_grad = jnp.where(even, kv_got, kv_keep)
    output_grad = side_by_side(keep[:, qcols + kcols :], got[:, qcols + kcols :], even).T

    cuts, at = [], 0
    for vector in early + late:
        cuts.append(sums[at : at + vector.shape[0]])
        at += vector.shape[0]
    o_sum, g_sum, u_sum, d_sum, two_sum, three_sum, four_sum, q_sum, k_sum, v_sum, one_sum = cuts
    return (
        block_out,
        token_grad,
        query_grad,
        key_grad,
        value_grad,
        output_grad,
        gate_grad,
        up_grad,
        down_grad,
        q_sum,
        k_sum,
        v_sum,
        o_sum,
        g_sum,
        u_sum,
        d_sum,
        one_sum,
        two_sum,
        three_sum,
        four_sum,
    )


def solution(mesh):
    seq_count, tp_count = mesh.shape["seq"], mesh.shape["tp"]
    wide = Mesh(mesh.devices.reshape(seq_count // 2, 2, tp_count // 2, 2), EVERY)
    seq, tp = ("line", "pair"), ("row", "core")
    return jax.shard_map(
        body,
        mesh=wide,
        in_specs=(P(EVERY, None),) * 2
        + (P(seq, tp),) * 3
        + (P(tp, seq),)
        + (P(seq, tp),) * 2
        + (P(tp, seq),)
        + (P(),) * 11
        + (P(seq),),
        out_specs=(P(EVERY, None),) * 2
        + (P(seq, tp),) * 3
        + (P(tp, seq),)
        + (P(seq, tp),) * 2
        + (P(tp, seq),)
        + (P(),) * 11,
        check_vma=False,
    )
```

```python
import math

import jax
import jax.numpy as jnp
from jax import lax
from jax.experimental import pallas as pl
from jax.experimental.pallas import tpu as pltpu
from jax.sharding import Mesh
from jax.sharding import PartitionSpec as P

HEAD_DIM = 256
WINDOW = 4096
CAP = 50
EPSILON = 1e-06

EVERY = ("line", "pair", "row", "core")
SWAP = [(0, 1), (1, 0)]


def swapped(block, axis):
    return lax.ppermute(block, axis, SWAP)


def hop(block, distance, first):
    count = lax.axis_size("line")
    route = [(i, i + distance) for i in range(first, count) if 0 <= i + distance < count]
    return lax.ppermute(block, "line", route)


def put_together(sources, moves, shape):
    count = len(moves())
    if any(size % 16 for _, _, size, _, _ in moves()):
        out = jnp.zeros(shape, sources[0].dtype)
        for source, start, size, row, column in moves():
            piece = lax.dynamic_slice_in_dim(sources[source], start, size, 0)
            out = lax.dynamic_update_slice(out, piece, (row, column))
        return out

    def rows_at(row, size):
        return pl.ds(row if isinstance(row, int) else pl.multiple_of(row, 16), size)

    def kernel(*refs):
        out, sems = refs[len(sources)], refs[len(sources) + 1]
        copies = []
        for i, (source, start, size, row, column) in enumerate(moves()):
            piece = refs[source].at[rows_at(start, size)]
            target = out.at[rows_at(row, size), pl.ds(column, sources[source].shape[1])]
            copies.append(pltpu.make_async_copy(piece, target, sems.at[i]))
        for copy in copies:
            copy.start()
        for copy in copies:
            copy.wait()

    size = 2 * math.prod(shape) * sources[0].dtype.itemsize
    return pl.pallas_call(
        kernel,
        out_shape=jax.ShapeDtypeStruct(shape, sources[0].dtype),
        in_specs=[pl.BlockSpec(memory_space=pl.ANY)] * len(sources),
        out_specs=pl.BlockSpec(memory_space=pltpu.VMEM),
        scratch_shapes=[pltpu.SemaphoreType.DMA((count,))],
        compiler_params=pltpu.CompilerParams(vmem_limit_bytes=size // 2 + 4 * 1024 * 1024),
        cost_estimate=pl.CostEstimate(flops=0, bytes_accessed=size, transcendentals=0),
    )(*sources)


def tie(*values):
    return lax.optimization_barrier(values)


class Stream:
    def __init__(self, **blocks):
        self.blocks = blocks

    def stop(self, work, finish=(), start=()):
        here = [self.blocks[name] for name in finish]
        sources = [[self.blocks[name] for name in names] for _, names, _ in start]
        work, here, sources = tie(work, here, sources)
        self.blocks.update(zip(finish, here))
        for (name, _, route), blocks in zip(start, sources):
            self.blocks[name] = route(*blocks)
        return work


def nested_slice(codes):
    values = codes.astype(jnp.float32)
    return (jnp.clip(jnp.floor((values + 8.0) / 16.0), -8.0, 7.0) * 16.0).astype(jnp.bfloat16)


def inverse_rms(values):
    return lax.rsqrt(jnp.mean(values * values, axis=-1, keepdims=True) + EPSILON)


def norm_back(source, inverse, gain, upstream):
    scaled = upstream * gain
    inner = jnp.mean(scaled * source, axis=-1, keepdims=True)
    back = inverse * scaled - source * (inverse * inverse * inverse) * inner
    return (back, jnp.sum(upstream * source * inverse, axis=0))


def phases(positions):
    freqs = 10000.0 ** (-2.0 * jnp.arange(HEAD_DIM // 2, dtype=jnp.float32) / HEAD_DIM)
    angle = positions.astype(jnp.float32)[:, None] * freqs[None, :]
    return (jnp.cos(angle), jnp.sin(angle))


def rotate(values, cosine, sine):
    half = values.shape[-1] // 2
    first = values[..., :half]
    second = values[..., half:]
    return jnp.concatenate([first * cosine - second * sine, second * cosine + first * sine], -1)


def spread(piece, total, offset):
    return lax.dynamic_update_slice_in_dim(jnp.zeros((total,), jnp.float32), piece, offset, 0)


def in_order(mine, other, place):
    return lax.dynamic_slice_in_dim(
        jnp.concatenate([other, mine, other], 0), (1 - place) * mine.shape[0], 2 * mine.shape[0], 0
    )


def half_of(block, place):
    size = block.shape[1] // 2
    return lax.dynamic_slice_in_dim(block, place * size, size, 1)


def unstopped(work):
    return work


def gather8(block, with_halves=None, direct=False):
    size, width = block.shape
    cut = size // 2
    if direct:
        corner = lax.ppermute(block, ("pair", "row"), [(i, 3 - i) for i in range(4)])
        parts = [block, swapped(block, "row"), swapped(block, "pair"), corner]
        four = put_together(
            parts, lambda: [(i, 0, size, i * size, 0) for i in range(4)], (4 * size, width)
        )
        return put_together(
            [four, swapped(four, "core")],
            lambda: [(i, 0, 4 * size, i * 4 * size, 0) for i in range(2)],
            (8 * size, width),
        )
    left, right = block[:cut], block[cut:]
    left_p, right_r = swapped(left, "pair"), swapped(right, "row")
    left_r, right_p = swapped(left, "row"), swapped(right, "pair")
    left_pr, right_pr = swapped(left_p, "row"), swapped(right_r, "pair")
    halves = [left, right, left_r, right_r, left_p, right_p, left_pr, right_pr]
    four = put_together(
        halves, lambda: [(i, 0, cut, i * cut, 0) for i in range(8)], (4 * size, width)
    )
    other = swapped(four, "core")
    if with_halves is not None:
        four, other = with_halves(four, other)
    return put_together(
        [four, other],
        lambda: [(i, 0, 4 * size, i * 4 * size, 0) for i in range(2)],
        (8 * size, width),
    )


def summed(keep, got):
    return keep + got.astype(jnp.float32)


def sent(piece, axis):
    return swapped(piece.astype(jnp.bfloat16), axis)


def scatter8(terms, stop=unstopped):
    mine, others = terms
    size, width = mine.shape[0] // 4, mine.shape[1]
    mine, got = tie(mine, sent(others, "core"))
    four = stop(summed(mine, got)).reshape(2, 2, size, width)
    left, right = four[..., : width // 2], four[..., width // 2 :]
    left = summed(left[0], sent(left[1], "pair"))
    right = summed(right[:, 0], sent(right[:, 1], "row"))
    left = summed(left[0], sent(left[1], "row"))
    right = summed(right[0], sent(right[1], "pair"))
    return jnp.concatenate([left, right], 1)


def scatter8_last(terms, stop):
    mine, others = terms
    size, width = mine.shape[0] // 4, mine.shape[1]
    four = summed(mine, sent(others, "core")).reshape(2, 2, size, width)
    two = stop(summed(four[0], sent(four[1], "pair")))
    return summed(two[0], sent(two[1], "row"))


def blocks(rows, places):
    size = rows.shape[0] // len(places)
    return jnp.concatenate(
        [lax.dynamic_slice_in_dim(rows, place * size, size, 0) for place in places], 0
    )


def to_tokens(rows, pair, row, core):
    places = [
        ((c ^ core) * 4 + (p ^ pair) * 2 + (r ^ row))
        for p in range(2)
        for r in range(2)
        for c in range(2)
    ]
    return blocks(rows, places)


def from_tokens(rows, pair, row, core):
    places = [
        ((p ^ pair) * 4 + (r ^ row) * 2 + (c ^ core))
        for c in range(2)
        for p in range(2)
        for r in range(2)
    ]
    return blocks(rows, places)


def exchanged(vector, axis):
    if isinstance(axis, str):
        return swapped(vector, axis)
    count = lax.axis_size("line")
    return lax.ppermute(vector, "line", [(i, i ^ axis) for i in range(count)])


def across(left, right):
    return lax.dot_general(left, right, (((1,), (1,)), ((), ())), preferred_element_type=jnp.float32)

def attend(queries, keys, values, low, bq=512, bk=1024):
    rows, span = queries.shape[0], keys.shape[0]
    offset = span - rows
    first = jnp.min(low.reshape(rows // bq, bq), axis=1) // bk

    def kernel(first_ref, q_ref, k_ref, v_ref, low_ref, o_ref, lse_ref, sums, totals):
        block = pl.program_id(0)
        high = offset + block * bq + lax.broadcasted_iota(jnp.int32, (bq, 1), 0)
        sums[...] = jnp.zeros_like(sums)
        totals[...] = jnp.zeros_like(totals)

        def chunk(c, carry):
            at = pl.multiple_of(c * bk, bk)
            raw = across(q_ref[...], k_ref[pl.ds(at, bk), :])
            place = at + lax.broadcasted_iota(jnp.int32, (bq, bk), 1)
            seen = (place >= low_ref[...]) & (place <= high)
            expo = jnp.where(seen, jnp.exp(CAP * jnp.tanh(raw * (1.0 / CAP))), 0.0)
            totals[...] += jnp.sum(expo, axis=-1, keepdims=True)
            sums[...] += jnp.dot(expo.astype(jnp.bfloat16), v_ref[pl.ds(at, bk), :], preferred_element_type=jnp.float32)
            return carry

        lax.fori_loop(first_ref[block], (offset + (block + 1) * bq - 1) // bk + 1, chunk, 0)
        o_ref[...] = sums[...] / totals[...]
        lse_ref[...] = jnp.log(totals[...])

    whole = lambda i, *_: (0, 0)
    mine = lambda i, *_: (i, 0)
    return pl.pallas_call(
        kernel,
        out_shape=(jax.ShapeDtypeStruct((rows, HEAD_DIM), jnp.float32), jax.ShapeDtypeStruct((rows, 1), jnp.float32)),
        grid_spec=pltpu.PrefetchScalarGridSpec(
            num_scalar_prefetch=1, grid=(rows // bq,),
            in_specs=[pl.BlockSpec((bq, HEAD_DIM), mine), pl.BlockSpec((span, HEAD_DIM), whole), pl.BlockSpec((span, HEAD_DIM), whole), pl.BlockSpec((bq, 1), mine)],
            out_specs=(pl.BlockSpec((bq, HEAD_DIM), mine), pl.BlockSpec((bq, 1), mine)),
            scratch_shapes=[pltpu.VMEM((bq, HEAD_DIM), jnp.float32), pltpu.VMEM((bq, 1), jnp.float32)]),
        compiler_params=pltpu.CompilerParams(vmem_limit_bytes=40 * 1024 * 1024),
        cost_estimate=pl.CostEstimate(flops=4 * rows * span * HEAD_DIM, bytes_accessed=4 * span * HEAD_DIM, transcendentals=2 * rows * span),
    )(first, queries, keys, values, low)

def attend_back(queries, keys, values, low, lse, delta, upstream, bq=1024, bk=512):
    rows, span = queries.shape[0], keys.shape[0]
    offset = span - rows
    first = jnp.min(low.reshape(rows // bq, bq), axis=1) // bk

    def kernel(first_ref, q_ref, up_ref, k_ref, kt_ref, v_ref, low_ref, lse_ref, delta_ref, dq_ref, dk_ref, dv_ref):
        block = pl.program_id(0)
        high = offset + block * bq + lax.broadcasted_iota(jnp.int32, (1, bq), 1)

        @pl.when(block == 0)
        def clear():
            dk_ref[...] = jnp.zeros_like(dk_ref)
            dv_ref[...] = jnp.zeros_like(dv_ref)

        dq_ref[...] = jnp.zeros_like(dq_ref)

        def chunk(c, carry):
            at = pl.multiple_of(c * bk, bk)
            here = pl.ds(at, bk)
            ratio = jnp.tanh(across(k_ref[here, :], q_ref[...]) * (1.0 / CAP))
            place = at + lax.broadcasted_iota(jnp.int32, (bk, bq), 0)
            seen = (place >= low_ref[...]) & (place <= high)
            probs = jnp.where(seen, jnp.exp(CAP * ratio - lse_ref[...]), 0.0)
            dv_ref[here, :] += jnp.dot(probs.astype(jnp.bfloat16), up_ref[...], preferred_element_type=jnp.float32)
            dprobs = across(v_ref[here, :], up_ref[...])
            draw = (probs * (dprobs - delta_ref[...]) * (1.0 - ratio * ratio)).astype(jnp.bfloat16)
            dk_ref[here, :] += jnp.dot(draw, q_ref[...], preferred_element_type=jnp.float32)
            dq_ref[...] += jnp.dot(kt_ref[:, here], draw, preferred_element_type=jnp.float32)
            return carry

        lax.fori_loop(first_ref[block], (offset + (block + 1) * bq - 1) // bk + 1, chunk, 0)

    whole = lambda i, *_: (0, 0)
    mine = lambda i, *_: (i, 0)
    across_lanes = lambda i, *_: (0, i)
    return pl.pallas_call(
        kernel,
        out_shape=(jax.ShapeDtypeStruct((HEAD_DIM, rows), jnp.float32), jax.ShapeDtypeStruct((span, HEAD_DIM), jnp.float32), jax.ShapeDtypeStruct((span, HEAD_DIM), jnp.float32)),
        grid_spec=pltpu.PrefetchScalarGridSpec(
            num_scalar_prefetch=1, grid=(rows // bq,),
            in_specs=[pl.BlockSpec((bq, HEAD_DIM), mine), pl.BlockSpec((bq, HEAD_DIM), mine), pl.BlockSpec((span, HEAD_DIM), whole), pl.BlockSpec((HEAD_DIM, span), whole), pl.BlockSpec((span, HEAD_DIM), whole),
                      pl.BlockSpec((1, bq), across_lanes), pl.BlockSpec((1, bq), across_lanes), pl.BlockSpec((1, bq), across_lanes)],
            out_specs=(pl.BlockSpec((HEAD_DIM, bq), across_lanes), pl.BlockSpec((span, HEAD_DIM), whole), pl.BlockSpec((span, HEAD_DIM), whole))),
        compiler_params=pltpu.CompilerParams(vmem_limit_bytes=48 * 1024 * 1024),
        cost_estimate=pl.CostEstimate(flops=10 * rows * span * HEAD_DIM, bytes_accessed=12 * span * HEAD_DIM, transcendentals=2 * rows * span),
    )(first, queries, upstream, keys, keys.T, values, low.T, lse.T, delta.T)


def body(
    tokens,
    cotangent,
    query_weight,
    key_weight,
    value_weight,
    output_weight,
    gate_weight,
    up_weight,
    down_weight,
    query_scale,
    key_scale,
    value_scale,
    output_scale,
    gate_scale,
    up_scale,
    down_scale,
    pre_attention,
    post_attention,
    pre_feedforward,
    post_feedforward,
    positions,
):
    lines = lax.axis_size("line")
    line, pair = lax.axis_index("line"), lax.axis_index("pair")
    row, core = lax.axis_index("row"), lax.axis_index("core")
    tp_index = row * 2 + core
    scale = 1.0 / math.sqrt(HEAD_DIM)
    even = pair == 0
    qcols = query_weight.shape[1] // 2
    kcols = key_weight.shape[1]
    ocols = output_weight.shape[0] // 2
    fcols = gate_weight.shape[1] // 2
    rows = 8 * tokens.shape[0]

    wq, wk, wv, wo, wg, wu, wd = (
        nested_slice(query_weight),
        nested_slice(key_weight),
        nested_slice(value_weight),
        nested_slice(output_weight.T),
        nested_slice(gate_weight),
        nested_slice(up_weight),
        nested_slice(down_weight.T),
    )

    def paired(keep, give):
        return in_order(keep, swapped(give, "pair"), pair)

    def over_line(block):
        return lax.all_gather(block, "line", axis=0, tiled=True)

    def shared_out(shard):
        return paired(half_of(shard, pair), half_of(shard, 1 - pair))

    kv_block = paired(jnp.where(even, wk, wv), jnp.where(even, wv, wk))
    stream = Stream(
        qkvo=jnp.concatenate([shared_out(wq), kv_block, shared_out(wo)], 1),
        gu=jnp.concatenate([shared_out(wg), shared_out(wu)], 1),
        d=shared_out(wd),
    )

    q_at = tp_index * 2 * qcols + pair * qcols
    k_at = tp_index * kcols
    f_at = tp_index * 2 * fcols + pair * fcols
    q_scale = lax.dynamic_slice_in_dim(query_scale, q_at, qcols, 0)
    k_scale = lax.dynamic_slice_in_dim(key_scale, k_at, kcols, 0)
    v_scale = lax.dynamic_slice_in_dim(value_scale, k_at, kcols, 0)
    kv_scale = jnp.where(even, k_scale, v_scale)
    g_scale = lax.dynamic_slice_in_dim(gate_scale, f_at, fcols, 0)
    u_scale = lax.dynamic_slice_in_dim(up_scale, f_at, fcols, 0)

    inputs = tokens.astype(jnp.float32)
    inverse_one = inverse_rms(inputs)
    h_local = (inputs * inverse_one * pre_attention).astype(jnp.bfloat16)
    h_local = stream.stop(h_local, start=[("w_qkvo", ["qkvo"], over_line)])
    h_one = gather8(h_local)
    h_one = stream.stop(h_one, ["w_qkvo"], [("w_gu", ["gu"], over_line)])
    w_qkv = stream.blocks["w_qkvo"][:, : qcols + kcols]
    w_o = stream.blocks["w_qkvo"][:, qcols + kcols :]
    places = in_order(positions, swapped(positions, "pair"), pair)
    cosine, sine = phases(places)

    z_qkv = jnp.dot(h_one, w_qkv, preferred_element_type=jnp.float32)
    z_qkv = to_tokens(z_qkv, pair, row, core)
    zq, zkv = z_qkv[:, :qcols], z_qkv[:, qcols:]
    kv_rows = zkv * kv_scale
    kv_rows = jnp.where(even, rotate(kv_rows, cosine, sine), kv_rows).astype(jnp.bfloat16)
    depth = min((WINDOW - 1 + rows - 1) // rows, lines - 1)
    kept, other = [kv_rows], [swapped(kv_rows, "pair")]
    for step in range(depth):
        kept.append(hop(kept[-1], 1, step))
        kept[-1], other = stream.stop((kept[-1], other))
        other.append(swapped(kept[-1], "pair"))
    queries = (rotate(zq * q_scale, cosine, sine).astype(jnp.bfloat16) * scale).astype(jnp.bfloat16)
    kept, other = jnp.concatenate(kept[::-1], 0), jnp.concatenate(other[::-1], 0)
    keys = jnp.where(even, kept, other)
    values = jnp.where(even, other, kept)
    low = depth * rows + jnp.arange(rows, dtype=jnp.int32) - jnp.minimum(places, WINDOW - 1)
    low = low[:, None]
    attended_wide, lse = attend(queries, keys, values, low)
    attended = attended_wide.astype(jnp.bfloat16)
    attended = from_tokens(attended, pair, row, core)
    def by_core(left, right):
        half_rows = left.shape[0] // 2
        mine, others = left[:half_rows], left[half_rows:]
        others = jnp.einsum("tc,dc->td", others, right, preferred_element_type=jnp.float32)
        mine, others = tie(mine, others.astype(jnp.bfloat16))
        mine = jnp.einsum("tc,dc->td", mine, right, preferred_element_type=jnp.float32)
        return mine, others

    zo = scatter8(by_core(attended, w_o))
    zo = stream.stop(zo, ["w_gu"], [("w_d", ["d"], over_line)])
    w_gu, w_d = stream.blocks["w_gu"], stream.blocks["w_d"]
    after_attention = zo * output_scale
    inverse_two = inverse_rms(after_attention)
    middle = inputs + after_attention * inverse_two * post_attention
    inverse_three = inverse_rms(middle)
    h_two = gather8((middle * inverse_three * pre_feedforward).astype(jnp.bfloat16))
    z_gu = jnp.dot(h_two, w_gu, preferred_element_type=jnp.float32)
    zg, zu = z_gu[:, :fcols], z_gu[:, fcols:]
    gate_in = zg * g_scale
    up_in = zu * u_scale
    hidden = (jax.nn.gelu(gate_in, approximate=True) * up_in).astype(jnp.bfloat16)
    zd = scatter8(by_core(hidden, w_d))
    fed = zd * down_scale
    inverse_four = inverse_rms(fed)
    block_out = middle + fed * inverse_four * post_feedforward

    upstream = cotangent.astype(jnp.float32)
    dfed, gain_four_grad = norm_back(fed, inverse_four, post_feedforward, upstream)
    down_scale_sum = jnp.sum(dfed * zd, axis=0)
    def over_line_sum(term):
        return lax.psum_scatter(term, "line", scatter_dimension=0, tiled=True)

    def rows_for(part, place):
        size = part.shape[0] // 2
        return lax.dynamic_slice_in_dim(part, place * size, size, 0).astype(jnp.float32)

    def swap_of(name):
        def route(part):
            return swapped(rows_for(part, 1 - pair).astype(jnp.bfloat16), "pair")

        return (name + "_got", [name + "_sum"], route)

    def shared(name):
        return rows_for(stream.blocks[name + "_sum"], pair), stream.blocks[name + "_got"].astype(
            jnp.float32
        )

    def side_by_side(keep, got, first):
        return jnp.where(
            first, jnp.concatenate([keep, got], 1), jnp.concatenate([got, keep], 1)
        )

    def term_of(left, right):
        return jnp.einsum("td,tf->df", left, right, preferred_element_type=jnp.float32).astype(
            jnp.bfloat16
        )

    def down_term(four, other):
        mine = jnp.einsum("td,tf->df", four, hidden[: rows // 2], preferred_element_type=jnp.float32)
        mine, other = tie(mine, other)
        others = jnp.einsum(
            "td,tf->df", other, hidden[rows // 2 :], preferred_element_type=jnp.float32
        )
        stream.blocks["D"] = (mine + others).astype(jnp.bfloat16)
        return stream.stop((four, other), ["D"], [("D_sum", ["D"], over_line_sum)])

    dzd = gather8((dfed * down_scale).astype(jnp.bfloat16), down_term)
    dhidden = jnp.dot(dzd, w_d, preferred_element_type=jnp.float32)
    unused, pull = jax.vjp(
        lambda left, right: jax.nn.gelu(left, approximate=True) * right, gate_in, up_in
    )
    dgate, dup = pull(dhidden)
    gate_scale_sum = jnp.sum(dgate * zg, axis=0)
    up_scale_sum = jnp.sum(dup * zu, axis=0)
    dzg = (dgate * g_scale).astype(jnp.bfloat16)
    dzu = (dup * u_scale).astype(jnp.bfloat16)
    dh_mid = (
        jnp.einsum("tf,df->td", dzg, w_gu[:, :fcols], preferred_element_type=jnp.float32)
        + jnp.einsum("tf,df->td", dzu, w_gu[:, fcols:], preferred_element_type=jnp.float32)
    )
    stream.blocks["GU"] = jnp.concatenate([term_of(h_two, dzg), term_of(h_two, dzu)], 1)
    dh_mid = scatter8(
        jnp.split(dh_mid, 2),
        lambda work: stream.stop(
            work, ["GU", "D_sum"], [("GU_sum", ["GU"], over_line_sum), swap_of("D")]
        ),
    )
    dmid_norm, gain_three_grad = norm_back(middle, inverse_three, pre_feedforward, dh_mid)
    dmiddle = upstream + dmid_norm
    dafter, gain_two_grad = norm_back(after_attention, inverse_two, post_attention, dmiddle)
    output_scale_sum = jnp.sum(dafter * zo, axis=0)
    early = (
        output_scale_sum,
        spread(gate_scale_sum, gate_scale.shape[0], f_at),
        spread(up_scale_sum, up_scale.shape[0], f_at),
        down_scale_sum,
        gain_two_grad,
        gain_three_grad,
        gain_four_grad,
    )
    dzo = gather8((dafter * output_scale).astype(jnp.bfloat16), direct=True)
    o_term = term_of(dzo, attended)
    dattended = jnp.dot(dzo, w_o, preferred_element_type=jnp.float32).astype(jnp.bfloat16)
    dattended = to_tokens(dattended, pair, row, core)
    delta = jnp.sum(dattended.astype(jnp.float32) * attended_wide, axis=-1, keepdims=True)
    dqueries, dkeys, dvalues = attend_back(queries, keys, values, low, lse, delta, dattended)
    dqueries = dqueries.T * scale

    keep = jnp.where(even, dkeys, dvalues)
    give = jnp.where(even, dvalues, dkeys).astype(jnp.bfloat16)
    got = [swapped(give[i * rows : (i + 1) * rows], "pair") for i in range(depth + 1)]
    equery = rotate(dqueries, cosine, -sine)
    query_scale_sum = jnp.sum(equery * zq, axis=0)
    dzq = from_tokens((equery * q_scale).astype(jnp.bfloat16), pair, row, core)
    q_term = term_of(h_one, dzq)
    got[0], q_term, o_term = stream.stop((got[0], q_term, o_term))
    dkv = None
    for i in range(depth + 1):
        block = keep[i * rows : (i + 1) * rows] + got[i].astype(jnp.float32)
        if dkv is not None:
            block = block + hop(dkv.astype(jnp.bfloat16), -1, depth + 1 - i).astype(jnp.float32)
        dkv = block
    ekv = jnp.where(even, rotate(dkv, cosine, -sine), dkv)
    kv_scale_sum = jnp.sum(ekv * zkv, axis=0)
    dzkv = from_tokens((ekv * kv_scale).astype(jnp.bfloat16), pair, row, core)
    kv_term = term_of(h_one, dzkv)
    stream.blocks["QKVO"] = jnp.concatenate([q_term, kv_term, o_term], 1)
    dzkv = stream.stop(
        dzkv,
        ["QKVO", "GU_sum", "D_got"],
        [("QKVO_sum", ["QKVO"], over_line_sum), swap_of("GU")],
    )
    dh_one = jnp.einsum(
        "tc,dc->td",
        jnp.concatenate([dzq, dzkv], 1),
        w_qkv,
        preferred_element_type=jnp.float32,
    )
    gain_one_part = jnp.sum(dh_one * h_one.astype(jnp.float32), axis=0) / pre_attention
    late = (
        spread(query_scale_sum, query_scale.shape[0], q_at),
        spread(jnp.where(even, kv_scale_sum, 0.0), key_scale.shape[0], k_at),
        spread(jnp.where(even, 0.0, kv_scale_sum), value_scale.shape[0], k_at),
        gain_one_part,
    )
    sums = jnp.concatenate(early + late)
    dh_one, sums = stream.stop((dh_one, sums), ["GU_got"])
    for axis in ["core", "row", "pair"] + [1 << i for i in range(lines.bit_length() - 1)]:
        sums = sums + exchanged(sums, axis)
    stream.blocks["sums"] = sums
    dh_local = scatter8_last(
        jnp.split(dh_one, 2),
        lambda work: stream.stop(work, ["QKVO_sum", "sums"], [swap_of("QKVO")]),
    )
    sums = stream.blocks["sums"]
    dinput_norm, unused = norm_back(inputs, inverse_one, pre_attention, dh_local)
    token_grad = dmiddle + dinput_norm
    d_keep, d_got = shared("D")
    down_grad = side_by_side(d_keep, d_got, even).T
    gu_keep, gu_got = shared("GU")
    gate_grad = side_by_side(gu_keep[:, :fcols], gu_got[:, :fcols], even)
    up_grad = side_by_side(gu_keep[:, fcols:], gu_got[:, fcols:], even)
    keep, got = shared("QKVO")
    query_grad = side_by_side(keep[:, :qcols], got[:, :qcols], even)
    kv_keep, kv_got = keep[:, qcols : qcols + kcols], got[:, qcols : qcols + kcols]
    key_grad = jnp.where(even, kv_keep, kv_got)
    value_grad = jnp.where(even, kv_got, kv_keep)
    output_grad = side_by_side(keep[:, qcols + kcols :], got[:, qcols + kcols :], even).T

    cuts, at = [], 0
    for vector in early + late:
        cuts.append(sums[at : at + vector.shape[0]])
        at += vector.shape[0]
    o_sum, g_sum, u_sum, d_sum, two_sum, three_sum, four_sum, q_sum, k_sum, v_sum, one_sum = cuts
    return (
        block_out,
        token_grad,
        query_grad,
        key_grad,
        value_grad,
        output_grad,
        gate_grad,
        up_grad,
        down_grad,
        q_sum,
        k_sum,
        v_sum,
        o_sum,
        g_sum,
        u_sum,
        d_sum,
        one_sum,
        two_sum,
        three_sum,
        four_sum,
    )


def solution(mesh):
    seq_count, tp_count = mesh.shape["seq"], mesh.shape["tp"]
    wide = Mesh(mesh.devices.reshape(seq_count // 2, 2, tp_count // 2, 2), EVERY)
    seq, tp = ("line", "pair"), ("row", "core")
    return jax.shard_map(
        body,
        mesh=wide,
        in_specs=(P(EVERY, None),) * 2
        + (P(seq, tp),) * 3
        + (P(tp, seq),)
        + (P(seq, tp),) * 2
        + (P(tp, seq),)
        + (P(),) * 11
        + (P(seq),),
        out_specs=(P(EVERY, None),) * 2
        + (P(seq, tp),) * 3
        + (P(tp, seq),)
        + (P(seq, tp),) * 2
        + (P(tp, seq),)
        + (P(),) * 11,
        check_vma=False,
    )
```

```python
import math

import jax
import jax.numpy as jnp
from jax import lax
from jax.experimental import pallas as pl
from jax.experimental.pallas import tpu as pltpu
from jax.sharding import Mesh
from jax.sharding import PartitionSpec as P

HEAD_DIM = 256
WINDOW = 4096
CAP = 50
EPSILON = 1e-06

EVERY = ("line", "pair", "row", "core")
SWAP = [(0, 1), (1, 0)]


def swapped(block, axis):
    return lax.ppermute(block, axis, SWAP)


def hop(block, distance, first):
    count = lax.axis_size("line")
    route = [(i, i + distance) for i in range(first, count) if 0 <= i + distance < count]
    return lax.ppermute(block, "line", route)


def put_together(sources, moves, shape):
    count = len(moves())
    if any(size % 16 for _, _, size, _, _ in moves()):
        out = jnp.zeros(shape, sources[0].dtype)
        for source, start, size, row, column in moves():
            piece = lax.dynamic_slice_in_dim(sources[source], start, size, 0)
            out = lax.dynamic_update_slice(out, piece, (row, column))
        return out

    def rows_at(row, size):
        return pl.ds(row if isinstance(row, int) else pl.multiple_of(row, 16), size)

    def kernel(*refs):
        out, sems = refs[len(sources)], refs[len(sources) + 1]
        copies = []
        for i, (source, start, size, row, column) in enumerate(moves()):
            piece = refs[source].at[rows_at(start, size)]
            target = out.at[rows_at(row, size), pl.ds(column, sources[source].shape[1])]
            copies.append(pltpu.make_async_copy(piece, target, sems.at[i]))
        for copy in copies:
            copy.start()
        for copy in copies:
            copy.wait()

    size = 2 * math.prod(shape) * sources[0].dtype.itemsize
    return pl.pallas_call(
        kernel,
        out_shape=jax.ShapeDtypeStruct(shape, sources[0].dtype),
        in_specs=[pl.BlockSpec(memory_space=pl.ANY)] * len(sources),
        out_specs=pl.BlockSpec(memory_space=pltpu.VMEM),
        scratch_shapes=[pltpu.SemaphoreType.DMA((count,))],
        compiler_params=pltpu.CompilerParams(vmem_limit_bytes=size // 2 + 4 * 1024 * 1024),
        cost_estimate=pl.CostEstimate(flops=0, bytes_accessed=size, transcendentals=0),
    )(*sources)


def tie(*values):
    return lax.optimization_barrier(values)


class Stream:
    def __init__(self, **blocks):
        self.blocks = blocks

    def stop(self, work, finish=(), start=()):
        here = [self.blocks[name] for name in finish]
        sources = [[self.blocks[name] for name in names] for _, names, _ in start]
        work, here, sources = tie(work, here, sources)
        self.blocks.update(zip(finish, here))
        for (name, _, route), blocks in zip(start, sources):
            self.blocks[name] = route(*blocks)
        return work


def nested_slice(codes):
    values = codes.astype(jnp.float32)
    return (jnp.clip(jnp.floor((values + 8.0) / 16.0), -8.0, 7.0) * 16.0).astype(jnp.bfloat16)


def inverse_rms(values):
    return lax.rsqrt(jnp.mean(values * values, axis=-1, keepdims=True) + EPSILON)


def norm_back(source, inverse, gain, upstream):
    scaled = upstream * gain
    inner = jnp.mean(scaled * source, axis=-1, keepdims=True)
    back = inverse * scaled - source * (inverse * inverse * inverse) * inner
    return (back, jnp.sum(upstream * source * inverse, axis=0))


def phases(positions):
    freqs = 10000.0 ** (-2.0 * jnp.arange(HEAD_DIM // 2, dtype=jnp.float32) / HEAD_DIM)
    angle = positions.astype(jnp.float32)[:, None] * freqs[None, :]
    return (jnp.cos(angle), jnp.sin(angle))


def rotate(values, cosine, sine):
    half = values.shape[-1] // 2
    first = values[..., :half]
    second = values[..., half:]
    return jnp.concatenate([first * cosine - second * sine, second * cosine + first * sine], -1)


def spread(piece, total, offset):
    return lax.dynamic_update_slice_in_dim(jnp.zeros((total,), jnp.float32), piece, offset, 0)


def in_order(mine, other, place):
    return lax.dynamic_slice_in_dim(
        jnp.concatenate([other, mine, other], 0), (1 - place) * mine.shape[0], 2 * mine.shape[0], 0
    )


def half_of(block, place):
    size = block.shape[1] // 2
    return lax.dynamic_slice_in_dim(block, place * size, size, 1)


def unstopped(work):
    return work


def gather8(block, with_halves=None, direct=False):
    size, width = block.shape
    cut = size // 2
    if direct:
        corner = lax.ppermute(block, ("pair", "row"), [(i, 3 - i) for i in range(4)])
        parts = [block, swapped(block, "row"), swapped(block, "pair"), corner]
        four = put_together(
            parts, lambda: [(i, 0, size, i * size, 0) for i in range(4)], (4 * size, width)
        )
        return put_together(
            [four, swapped(four, "core")],
            lambda: [(i, 0, 4 * size, i * 4 * size, 0) for i in range(2)],
            (8 * size, width),
        )
    left, right = block[:cut], block[cut:]
    left_p, right_r = swapped(left, "pair"), swapped(right, "row")
    left_r, right_p = swapped(left, "row"), swapped(right, "pair")
    left_pr, right_pr = swapped(left_p, "row"), swapped(right_r, "pair")
    halves = [left, right, left_r, right_r, left_p, right_p, left_pr, right_pr]
    four = put_together(
        halves, lambda: [(i, 0, cut, i * cut, 0) for i in range(8)], (4 * size, width)
    )
    other = swapped(four, "core")
    if with_halves is not None:
        four, other = with_halves(four, other)
    return put_together(
        [four, other],
        lambda: [(i, 0, 4 * size, i * 4 * size, 0) for i in range(2)],
        (8 * size, width),
    )


def summed(keep, got):
    return keep + got.astype(jnp.float32)


def sent(piece, axis):
    return swapped(piece.astype(jnp.bfloat16), axis)


def scatter8(terms, stop=unstopped):
    mine, others = terms
    size, width = mine.shape[0] // 4, mine.shape[1]
    mine, got = tie(mine, sent(others, "core"))
    four = stop(summed(mine, got)).reshape(2, 2, size, width)
    left, right = four[..., : width // 2], four[..., width // 2 :]
    left = summed(left[0], sent(left[1], "pair"))
    right = summed(right[:, 0], sent(right[:, 1], "row"))
    left = summed(left[0], sent(left[1], "row"))
    right = summed(right[0], sent(right[1], "pair"))
    return jnp.concatenate([left, right], 1)


def scatter8_last(terms, stop_one, stop_two):
    mine, others = terms
    size, width = mine.shape[0] // 4, mine.shape[1]
    four = stop_one(summed(mine, sent(others, "core"))).reshape(2, 2, size, width)
    two = stop_two(summed(four[0], sent(four[1], "pair")))
    return summed(two[0], sent(two[1], "row"))


def blocks(rows, places):
    size = rows.shape[0] // len(places)
    return jnp.concatenate(
        [lax.dynamic_slice_in_dim(rows, place * size, size, 0) for place in places], 0
    )


def to_tokens(rows, pair, row, core):
    places = [
        ((c ^ core) * 4 + (p ^ pair) * 2 + (r ^ row))
        for p in range(2)
        for r in range(2)
        for c in range(2)
    ]
    return blocks(rows, places)


def from_tokens(rows, pair, row, core):
    places = [
        ((p ^ pair) * 4 + (r ^ row) * 2 + (c ^ core))
        for c in range(2)
        for p in range(2)
        for r in range(2)
    ]
    return blocks(rows, places)


def exchanged(vector, axis):
    if isinstance(axis, str):
        return swapped(vector, axis)
    count = lax.axis_size("line")
    return lax.ppermute(vector, "line", [(i, i ^ axis) for i in range(count)])


def across(left, right):
    return lax.dot_general(left, right, (((1,), (1,)), ((), ())), preferred_element_type=jnp.float32)

def attend(queries, keys, values, low, bq=512, bk=1024):
    rows, span = queries.shape[0], keys.shape[0]
    offset = span - rows
    first = jnp.min(low.reshape(rows // bq, bq), axis=1) // bk

    def kernel(first_ref, q_ref, k_ref, v_ref, low_ref, o_ref, lse_ref, sums, totals):
        block = pl.program_id(0)
        high = offset + block * bq + lax.broadcasted_iota(jnp.int32, (bq, 1), 0)
        sums[...] = jnp.zeros_like(sums)
        totals[...] = jnp.zeros_like(totals)

        def chunk(c, carry):
            at = pl.multiple_of(c * bk, bk)
            raw = across(q_ref[...], k_ref[pl.ds(at, bk), :])
            place = at + lax.broadcasted_iota(jnp.int32, (bq, bk), 1)
            seen = (place >= low_ref[...]) & (place <= high)
            expo = jnp.where(seen, jnp.exp(CAP * jnp.tanh(raw * (1.0 / CAP))), 0.0)
            totals[...] += jnp.sum(expo, axis=-1, keepdims=True)
            sums[...] += jnp.dot(expo.astype(jnp.bfloat16), v_ref[pl.ds(at, bk), :], preferred_element_type=jnp.float32)
            return carry

        lax.fori_loop(first_ref[block], (offset + (block + 1) * bq - 1) // bk + 1, chunk, 0)
        o_ref[...] = sums[...] / totals[...]
        lse_ref[...] = jnp.log(totals[...])

    whole = lambda i, *_: (0, 0)
    mine = lambda i, *_: (i, 0)
    return pl.pallas_call(
        kernel,
        out_shape=(jax.ShapeDtypeStruct((rows, HEAD_DIM), jnp.float32), jax.ShapeDtypeStruct((rows, 1), jnp.float32)),
        grid_spec=pltpu.PrefetchScalarGridSpec(
            num_scalar_prefetch=1, grid=(rows // bq,),
            in_specs=[pl.BlockSpec((bq, HEAD_DIM), mine), pl.BlockSpec((span, HEAD_DIM), whole), pl.BlockSpec((span, HEAD_DIM), whole), pl.BlockSpec((bq, 1), mine)],
            out_specs=(pl.BlockSpec((bq, HEAD_DIM), mine), pl.BlockSpec((bq, 1), mine)),
            scratch_shapes=[pltpu.VMEM((bq, HEAD_DIM), jnp.float32), pltpu.VMEM((bq, 1), jnp.float32)]),
        compiler_params=pltpu.CompilerParams(vmem_limit_bytes=40 * 1024 * 1024),
        cost_estimate=pl.CostEstimate(flops=4 * rows * span * HEAD_DIM, bytes_accessed=4 * span * HEAD_DIM, transcendentals=2 * rows * span),
    )(first, queries, keys, values, low)

def attend_back(queries, keys, values, low, lse, delta, upstream, bq=1024, bk=512):
    rows, span = queries.shape[0], keys.shape[0]
    offset = span - rows
    first = jnp.min(low.reshape(rows // bq, bq), axis=1) // bk

    def kernel(first_ref, q_ref, up_ref, k_ref, kt_ref, v_ref, low_ref, lse_ref, delta_ref, dq_ref, dk_ref, dv_ref):
        block = pl.program_id(0)
        high = offset + block * bq + lax.broadcasted_iota(jnp.int32, (1, bq), 1)

        @pl.when(block == 0)
        def clear():
            dk_ref[...] = jnp.zeros_like(dk_ref)
            dv_ref[...] = jnp.zeros_like(dv_ref)

        dq_ref[...] = jnp.zeros_like(dq_ref)

        def chunk(c, carry):
            at = pl.multiple_of(c * bk, bk)
            here = pl.ds(at, bk)
            ratio = jnp.tanh(across(k_ref[here, :], q_ref[...]) * (1.0 / CAP))
            place = at + lax.broadcasted_iota(jnp.int32, (bk, bq), 0)
            seen = (place >= low_ref[...]) & (place <= high)
            probs = jnp.where(seen, jnp.exp(CAP * ratio - lse_ref[...]), 0.0)
            dv_ref[here, :] += jnp.dot(probs.astype(jnp.bfloat16), up_ref[...], preferred_element_type=jnp.float32)
            dprobs = across(v_ref[here, :], up_ref[...])
            draw = (probs * (dprobs - delta_ref[...]) * (1.0 - ratio * ratio)).astype(jnp.bfloat16)
            dk_ref[here, :] += jnp.dot(draw, q_ref[...], preferred_element_type=jnp.float32)
            dq_ref[...] += jnp.dot(kt_ref[:, here], draw, preferred_element_type=jnp.float32)
            return carry

        lax.fori_loop(first_ref[block], (offset + (block + 1) * bq - 1) // bk + 1, chunk, 0)

    whole = lambda i, *_: (0, 0)
    mine = lambda i, *_: (i, 0)
    across_lanes = lambda i, *_: (0, i)
    return pl.pallas_call(
        kernel,
        out_shape=(jax.ShapeDtypeStruct((HEAD_DIM, rows), jnp.float32), jax.ShapeDtypeStruct((span, HEAD_DIM), jnp.float32), jax.ShapeDtypeStruct((span, HEAD_DIM), jnp.float32)),
        grid_spec=pltpu.PrefetchScalarGridSpec(
            num_scalar_prefetch=1, grid=(rows // bq,),
            in_specs=[pl.BlockSpec((bq, HEAD_DIM), mine), pl.BlockSpec((bq, HEAD_DIM), mine), pl.BlockSpec((span, HEAD_DIM), whole), pl.BlockSpec((HEAD_DIM, span), whole), pl.BlockSpec((span, HEAD_DIM), whole),
                      pl.BlockSpec((1, bq), across_lanes), pl.BlockSpec((1, bq), across_lanes), pl.BlockSpec((1, bq), across_lanes)],
            out_specs=(pl.BlockSpec((HEAD_DIM, bq), across_lanes), pl.BlockSpec((span, HEAD_DIM), whole), pl.BlockSpec((span, HEAD_DIM), whole))),
        compiler_params=pltpu.CompilerParams(vmem_limit_bytes=48 * 1024 * 1024),
        cost_estimate=pl.CostEstimate(flops=10 * rows * span * HEAD_DIM, bytes_accessed=12 * span * HEAD_DIM, transcendentals=2 * rows * span),
    )(first, queries, upstream, keys, keys.T, values, low.T, lse.T, delta.T)


def body(
    tokens,
    cotangent,
    query_weight,
    key_weight,
    value_weight,
    output_weight,
    gate_weight,
    up_weight,
    down_weight,
    query_scale,
    key_scale,
    value_scale,
    output_scale,
    gate_scale,
    up_scale,
    down_scale,
    pre_attention,
    post_attention,
    pre_feedforward,
    post_feedforward,
    positions,
):
    lines = lax.axis_size("line")
    line, pair = lax.axis_index("line"), lax.axis_index("pair")
    row, core = lax.axis_index("row"), lax.axis_index("core")
    tp_index = row * 2 + core
    scale = 1.0 / math.sqrt(HEAD_DIM)
    even = pair == 0
    qcols = query_weight.shape[1] // 2
    kcols = key_weight.shape[1]
    ocols = output_weight.shape[0] // 2
    fcols = gate_weight.shape[1] // 2
    rows = 8 * tokens.shape[0]

    wq, wk, wv, wo, wg, wu, wd = (
        nested_slice(query_weight),
        nested_slice(key_weight),
        nested_slice(value_weight),
        nested_slice(output_weight.T),
        nested_slice(gate_weight),
        nested_slice(up_weight),
        nested_slice(down_weight.T),
    )

    def paired(keep, give):
        return in_order(keep, swapped(give, "pair"), pair)

    def over_line(block):
        return lax.all_gather(block, "line", axis=0, tiled=True)

    def shared_out(shard):
        return paired(half_of(shard, pair), half_of(shard, 1 - pair))

    kv_block = paired(jnp.where(even, wk, wv), jnp.where(even, wv, wk))
    stream = Stream(
        qkvo=jnp.concatenate([shared_out(wq), kv_block, shared_out(wo)], 1),
        gu=jnp.concatenate([shared_out(wg), shared_out(wu)], 1),
        d=shared_out(wd),
    )

    q_at = tp_index * 2 * qcols + pair * qcols
    k_at = tp_index * kcols
    f_at = tp_index * 2 * fcols + pair * fcols
    q_scale = lax.dynamic_slice_in_dim(query_scale, q_at, qcols, 0)
    k_scale = lax.dynamic_slice_in_dim(key_scale, k_at, kcols, 0)
    v_scale = lax.dynamic_slice_in_dim(value_scale, k_at, kcols, 0)
    kv_scale = jnp.where(even, k_scale, v_scale)
    g_scale = lax.dynamic_slice_in_dim(gate_scale, f_at, fcols, 0)
    u_scale = lax.dynamic_slice_in_dim(up_scale, f_at, fcols, 0)

    inputs = tokens.astype(jnp.float32)
    inverse_one = inverse_rms(inputs)
    h_local = (inputs * inverse_one * pre_attention).astype(jnp.bfloat16)
    h_local = stream.stop(h_local, start=[("w_qkvo", ["qkvo"], over_line)])
    h_one = gather8(h_local)
    h_one = stream.stop(h_one, ["w_qkvo"], [("w_gu", ["gu"], over_line)])
    w_qkv = stream.blocks["w_qkvo"][:, : qcols + kcols]
    w_o = stream.blocks["w_qkvo"][:, qcols + kcols :]
    places = in_order(positions, swapped(positions, "pair"), pair)
    cosine, sine = phases(places)

    z_qkv = jnp.dot(h_one, w_qkv, preferred_element_type=jnp.float32)
    z_qkv = to_tokens(z_qkv, pair, row, core)
    zq, zkv = z_qkv[:, :qcols], z_qkv[:, qcols:]
    kv_rows = zkv * kv_scale
    kv_rows = jnp.where(even, rotate(kv_rows, cosine, sine), kv_rows).astype(jnp.bfloat16)
    depth = min((WINDOW - 1 + rows - 1) // rows, lines - 1)
    kept, other = [kv_rows], [swapped(kv_rows, "pair")]
    for step in range(depth):
        kept.append(hop(kept[-1], 1, step))
        kept[-1], other = stream.stop((kept[-1], other))
        other.append(swapped(kept[-1], "pair"))
    queries = (rotate(zq * q_scale, cosine, sine).astype(jnp.bfloat16) * scale).astype(jnp.bfloat16)
    kept, other = jnp.concatenate(kept[::-1], 0), jnp.concatenate(other[::-1], 0)
    keys = jnp.where(even, kept, other)
    values = jnp.where(even, other, kept)
    low = depth * rows + jnp.arange(rows, dtype=jnp.int32) - jnp.minimum(places, WINDOW - 1)
    low = low[:, None]
    attended_wide, lse = attend(queries, keys, values, low)
    attended = attended_wide.astype(jnp.bfloat16)
    attended = from_tokens(attended, pair, row, core)
    def by_core(left, right):
        half_rows = left.shape[0] // 2
        mine, others = left[:half_rows], left[half_rows:]
        others = jnp.einsum("tc,dc->td", others, right, preferred_element_type=jnp.float32)
        mine, others = tie(mine, others.astype(jnp.bfloat16))
        mine = jnp.einsum("tc,dc->td", mine, right, preferred_element_type=jnp.float32)
        return mine, others

    zo = scatter8(by_core(attended, w_o))
    zo = stream.stop(zo, ["w_gu"], [("w_d", ["d"], over_line)])
    w_gu, w_d = stream.blocks["w_gu"], stream.blocks["w_d"]
    after_attention = zo * output_scale
    inverse_two = inverse_rms(after_attention)
    middle = inputs + after_attention * inverse_two * post_attention
    inverse_three = inverse_rms(middle)
    h_two = gather8((middle * inverse_three * pre_feedforward).astype(jnp.bfloat16))
    z_gu = jnp.dot(h_two, w_gu, preferred_element_type=jnp.float32)
    zg, zu = z_gu[:, :fcols], z_gu[:, fcols:]
    gate_in = zg * g_scale
    up_in = zu * u_scale
    hidden = (jax.nn.gelu(gate_in, approximate=True) * up_in).astype(jnp.bfloat16)
    zd = scatter8(by_core(hidden, w_d))
    fed = zd * down_scale
    inverse_four = inverse_rms(fed)
    block_out = middle + fed * inverse_four * post_feedforward

    upstream = cotangent.astype(jnp.float32)
    dfed, gain_four_grad = norm_back(fed, inverse_four, post_feedforward, upstream)
    down_scale_sum = jnp.sum(dfed * zd, axis=0)
    def over_line_sum(term):
        return lax.psum_scatter(term, "line", scatter_dimension=0, tiled=True)

    def rows_for(part, place):
        size = part.shape[0] // 2
        return lax.dynamic_slice_in_dim(part, place * size, size, 0).astype(jnp.float32)

    def swap_of(name):
        def route(part):
            return swapped(rows_for(part, 1 - pair).astype(jnp.bfloat16), "pair")

        return (name + "_got", [name + "_sum"], route)

    def shared(name):
        return rows_for(stream.blocks[name + "_sum"], pair), stream.blocks[name + "_got"].astype(
            jnp.float32
        )

    def side_by_side(keep, got, first):
        return jnp.where(
            first, jnp.concatenate([keep, got], 1), jnp.concatenate([got, keep], 1)
        )

    def term_of(left, right):
        return jnp.einsum("td,tf->df", left, right, preferred_element_type=jnp.float32).astype(
            jnp.bfloat16
        )

    def down_term(four, other):
        mine = jnp.einsum("td,tf->df", four, hidden[: rows // 2], preferred_element_type=jnp.float32)
        mine, other = tie(mine.astype(jnp.bfloat16), other)
        others = jnp.einsum(
            "td,tf->df", other, hidden[rows // 2 :], preferred_element_type=jnp.float32
        )
        stream.blocks["D"] = (mine.astype(jnp.float32) + others).astype(jnp.bfloat16)
        return stream.stop((four, other), ["D"], [("D_sum", ["D"], over_line_sum)])

    dzd = gather8((dfed * down_scale).astype(jnp.bfloat16), down_term)
    dhidden = jnp.dot(dzd, w_d, preferred_element_type=jnp.float32)
    unused, pull = jax.vjp(
        lambda left, right: jax.nn.gelu(left, approximate=True) * right, gate_in, up_in
    )
    dgate, dup = pull(dhidden)
    gate_scale_sum = jnp.sum(dgate * zg, axis=0)
    up_scale_sum = jnp.sum(dup * zu, axis=0)
    dzg = (dgate * g_scale).astype(jnp.bfloat16)
    dzu = (dup * u_scale).astype(jnp.bfloat16)
    dh_mid = (
        jnp.einsum("tf,df->td", dzg, w_gu[:, :fcols], preferred_element_type=jnp.float32)
        + jnp.einsum("tf,df->td", dzu, w_gu[:, fcols:], preferred_element_type=jnp.float32)
    )
    stream.blocks["GU"] = jnp.concatenate([term_of(h_two, dzg), term_of(h_two, dzu)], 1)
    dh_mid = scatter8(
        jnp.split(dh_mid, 2),
        lambda work: stream.stop(
            work, ["GU", "D_sum"], [("GU_sum", ["GU"], over_line_sum), swap_of("D")]
        ),
    )
    dmid_norm, gain_three_grad = norm_back(middle, inverse_three, pre_feedforward, dh_mid)
    dmiddle = upstream + dmid_norm
    dafter, gain_two_grad = norm_back(after_attention, inverse_two, post_attention, dmiddle)
    output_scale_sum = jnp.sum(dafter * zo, axis=0)
    early = (
        output_scale_sum,
        spread(gate_scale_sum, gate_scale.shape[0], f_at),
        spread(up_scale_sum, up_scale.shape[0], f_at),
        down_scale_sum,
        gain_two_grad,
        gain_three_grad,
        gain_four_grad,
    )
    dzo = gather8((dafter * output_scale).astype(jnp.bfloat16), direct=True)
    o_term = term_of(dzo, attended)
    dattended = jnp.dot(dzo, w_o, preferred_element_type=jnp.float32).astype(jnp.bfloat16)
    dattended = to_tokens(dattended, pair, row, core)
    delta = jnp.sum(dattended.astype(jnp.float32) * attended_wide, axis=-1, keepdims=True)
    dqueries, dkeys, dvalues = attend_back(queries, keys, values, low, lse, delta, dattended)
    dqueries = dqueries.T * scale

    keep = jnp.where(even, dkeys, dvalues)
    give = jnp.where(even, dvalues, dkeys).astype(jnp.bfloat16)
    got = [swapped(give[i * rows : (i + 1) * rows], "pair") for i in range(depth + 1)]
    equery = rotate(dqueries, cosine, -sine)
    query_scale_sum = jnp.sum(equery * zq, axis=0)
    dzq = from_tokens((equery * q_scale).astype(jnp.bfloat16), pair, row, core)
    q_term = term_of(h_one, dzq)
    got[0], q_term, o_term = stream.stop((got[0], q_term, o_term))
    dkv = None
    for i in range(depth + 1):
        block = keep[i * rows : (i + 1) * rows] + got[i].astype(jnp.float32)
        if dkv is not None:
            block = block + hop(dkv.astype(jnp.bfloat16), -1, depth + 1 - i).astype(jnp.float32)
        dkv = block
    ekv = jnp.where(even, rotate(dkv, cosine, -sine), dkv)
    kv_scale_sum = jnp.sum(ekv * zkv, axis=0)
    dzkv = from_tokens((ekv * kv_scale).astype(jnp.bfloat16), pair, row, core)
    kv_term = term_of(h_one, dzkv)
    stream.blocks["QKVO"] = jnp.concatenate([q_term, kv_term, o_term], 1)
    dzkv = stream.stop(
        dzkv,
        ["QKVO", "GU_sum", "D_got"],
        [("QKVO_sum", ["QKVO"], over_line_sum), swap_of("GU")],
    )
    dh_one = jnp.einsum(
        "tc,dc->td",
        jnp.concatenate([dzq, dzkv], 1),
        w_qkv,
        preferred_element_type=jnp.float32,
    )
    gain_one_part = jnp.sum(dh_one * h_one.astype(jnp.float32), axis=0) / pre_attention
    late = (
        spread(query_scale_sum, query_scale.shape[0], q_at),
        spread(jnp.where(even, kv_scale_sum, 0.0), key_scale.shape[0], k_at),
        spread(jnp.where(even, 0.0, kv_scale_sum), value_scale.shape[0], k_at),
        gain_one_part,
    )
    sums = jnp.concatenate(early + late)
    stream.blocks["sums"] = sums + exchanged(sums, "pair")
    dh_one = stream.stop(dh_one, ["GU_got", "sums"])
    sum_axes = ["core", "row"] + [1 << i for i in range(lines.bit_length() - 1)]
    d_keep, d_got = shared("D")
    down_grad = side_by_side(d_keep, d_got, even).T
    gu_keep, gu_got = shared("GU")
    gate_grad = side_by_side(gu_keep[:, :fcols], gu_got[:, :fcols], even)
    up_grad = side_by_side(gu_keep[:, fcols:], gu_got[:, fcols:], even)
    stream.blocks.update(gate=gate_grad, up=up_grad, down=down_grad)

    def sums_after(four):
        four = stream.stop(four, ["sums"])
        for axis in sum_axes[:3]:
            stream.blocks["sums"] += exchanged(stream.blocks["sums"], axis)
        return four

    dh_local = scatter8_last(
        jnp.split(dh_one, 2),
        sums_after,
        lambda work: stream.stop(
            work, ["QKVO_sum", "sums", "gate", "up", "down"], [swap_of("QKVO")]
        ),
    )
    sums = stream.blocks["sums"]
    for axis in sum_axes[3:]:
        sums = sums + exchanged(sums, axis)
    dinput_norm, unused = norm_back(inputs, inverse_one, pre_attention, dh_local)
    token_grad = dmiddle + dinput_norm
    gate_grad, up_grad, down_grad = (stream.blocks[name] for name in ("gate", "up", "down"))
    keep, got = shared("QKVO")
    query_grad = side_by_side(keep[:, :qcols], got[:, :qcols], even)
    kv_keep, kv_got = keep[:, qcols : qcols + kcols], got[:, qcols : qcols + kcols]
    key_grad = jnp.where(even, kv_keep, kv_got)
    value_grad = jnp.where(even, kv_got, kv_keep)
    output_grad = side_by_side(keep[:, qcols + kcols :], got[:, qcols + kcols :], even).T

    cuts, at = [], 0
    for vector in early + late:
        cuts.append(sums[at : at + vector.shape[0]])
        at += vector.shape[0]
    o_sum, g_sum, u_sum, d_sum, two_sum, three_sum, four_sum, q_sum, k_sum, v_sum, one_sum = cuts
    return (
        block_out,
        token_grad,
        query_grad,
        key_grad,
        value_grad,
        output_grad,
        gate_grad,
        up_grad,
        down_grad,
        q_sum,
        k_sum,
        v_sum,
        o_sum,
        g_sum,
        u_sum,
        d_sum,
        one_sum,
        two_sum,
        three_sum,
        four_sum,
    )


def solution(mesh):
    seq_count, tp_count = mesh.shape["seq"], mesh.shape["tp"]
    wide = Mesh(mesh.devices.reshape(seq_count // 2, 2, tp_count // 2, 2), EVERY)
    seq, tp = ("line", "pair"), ("row", "core")
    return jax.shard_map(
        body,
        mesh=wide,
        in_specs=(P(EVERY, None),) * 2
        + (P(seq, tp),) * 3
        + (P(tp, seq),)
        + (P(seq, tp),) * 2
        + (P(tp, seq),)
        + (P(),) * 11
        + (P(seq),),
        out_specs=(P(EVERY, None),) * 2
        + (P(seq, tp),) * 3
        + (P(tp, seq),)
        + (P(seq, tp),) * 2
        + (P(tp, seq),)
        + (P(),) * 11,
        check_vma=False,
    )
```
